32 devices in a mesh: seq: 4 (over z), wide: 8 (over y, x, core).
Axes of the slice: x: 2, y: 2, z: 4, core: 2. Of those that a mesh axis runs over, the one named last changes fastest.
Arguments:
- tokens: bfloat16 [4, 1024, 2048], P('seq', 'wide'), may hold values from -6 to 6
- cotangent: bfloat16 [4, 1024, 2048], P('seq', 'wide'), may hold values from -6 to 6
- norm_gains: bfloat16 [2, 2048], P(None, 'wide'), may hold values from 0.5 to 1.5
- in_weight: bfloat16 [2048, 2, 2560], P('wide'), may hold values from -0.125 to 0.125
- conv_weight: bfloat16 [4, 2560], P(None, 'wide'), may hold values from -3 to 3
- conv_bias: bfloat16 [2560], P('wide'), may hold values from -3 to 3
- gate_weights: bfloat16 [2, 10, 256, 256], P(None, None, None, 'wide'), may hold values from -0.375 to 0.375
- gate_biases: bfloat16 [2, 2560], P(None, 'wide'), may hold values from -4 to 4
- decay_param: bfloat16 [2560], P('wide'), as said below
- out_weight: bfloat16 [2560, 2048], P('wide'), may hold values from -0.125 to 0.125
- mlp_in_weight: bfloat16 [2048, 2, 6144], P(None, None, 'wide'), may hold values from -0.125 to 0.125
- mlp_out_weight: bfloat16 [6144, 2048], P('wide'), may hold values from -0.078125 to 0.078125
Outputs:
- output: bfloat16 [4, 1024, 2048], P('seq', 'wide')
- input_grad: float32 [4, 1024, 2048], P('seq', 'wide')
- norm_gains_grad: float32 [2, 2048], P(None, 'wide')
- in_weight_grad: float32 [2048, 2, 2560], P('wide')
- conv_weight_grad: float32 [4, 2560], P(None, 'wide')
- conv_bias_grad: float32 [2560], P('wide')
- gate_weights_grad: float32 [2, 10, 256, 256], P(None, None, None, 'wide')
- gate_biases_grad: float32 [2, 2560], P(None, 'wide')
- decay_param_grad: float32 [2560], P('wide')
- out_weight_grad: float32 [2560, 2048], P('wide')
- mlp_in_weight_grad: float32 [2048, 2, 6144], P(None, None, 'wide')
- mlp_out_weight_grad: float32 [6144, 2048], P('wide')
The draws below stay inside these ranges and needn't reach their ends.
Inputs may be any that keep to these rules, and one draw needn't show every extreme that they name: softplus(-decay_param) lies between 0.05 / 1024 and 0.03 in every channel.
All inputs are finite; a program needn't handle non-finite values.
Results may differ from the reference program's by a relative error of at most 0.011.
Values may be sent and summed in bfloat16 or wider, within the bound.
No kernel may reach another device: no remote copies, remote signals or barrier semaphores. Data moves between devices by JAX's collectives and lax.ppermute only.
A program may use at most 320 MiB of HBM per device.

```python
import math
import jax
import jax.numpy as jnp
from jax import lax

D = 2048
LRU = 2560
HEADS = 10
BW = 256
FF = 6144
CONV = 4
TOK_DEV = 128
SEQ_LEN = 1024
SEQS = 4
N_WIDE = 8


def draw_decay_param(key, part):
    key = jax.random.fold_in(key, 11)
    keys = jax.random.split(key, 3)
    slow_share = 0.5
    slow_rates = jnp.exp(jax.random.uniform(keys[0], (LRU,), jnp.float32, math.log(0.05 / SEQ_LEN), math.log(0.5 / SEQ_LEN)))
    fast_rates = jnp.exp(jax.random.uniform(keys[1], (LRU,), jnp.float32, math.log(0.005), math.log(0.03)))
    picked = jax.random.uniform(keys[2], (LRU,), jnp.float32) < slow_share
    rates = jnp.where(picked, slow_rates, fast_rates)
    return (-jnp.log(jnp.expm1(rates))).astype(jnp.bfloat16)


def steps_of(own_key, extent, cuts, low, top_value):
    level = 1.0
    for position, parts in cuts:
        steps = jax.random.uniform(jax.random.fold_in(jax.random.fold_in(own_key, 6), position), (parts,), jnp.float32, low / len(cuts), top_value / len(cuts))
        level = level * jnp.repeat(jnp.exp(steps), extent[position] // parts).reshape((-1,) + (1,) * (len(extent) - 1 - position))
    return level


def noise(own_key, extent, scale, limit, shards=(), dtype=jnp.bfloat16):
    drawn = scale * jax.random.normal(own_key, extent, jnp.float32)
    if shards:
        drawn = drawn * steps_of(own_key, extent, shards, -0.22, 0.18)
    return jnp.clip(drawn, -limit, limit).astype(dtype)


def setup_inputs(seed: int = 0) -> dict:
    arg_keys = jax.random.split(jax.random.key(seed), 13)
    return {
        "tokens": noise(arg_keys[0], (SEQS, SEQ_LEN, D), 1.0, 6.0, ((0, 4), (1, 8))),
        "cotangent": noise(arg_keys[1], (SEQS, SEQ_LEN, D), 1.0, 6.0, ((0, 4), (1, 8))),
        "norm_gains": jnp.clip(1.0 + 0.1 * jax.random.normal(arg_keys[2], (2, D), jnp.float32), 0.5, 1.5).astype(jnp.bfloat16),
        "in_weight": noise(arg_keys[3], (D, 2, LRU), D ** -0.5, 0.125, ((0, 8),)),
        "conv_weight": noise(arg_keys[4], (CONV, LRU), CONV ** -0.5, 3.0, ((1, 8),)),
        "conv_bias": noise(arg_keys[5], (LRU,), 0.5, 3.0, ((0, 8),)),
        "gate_weights": noise(arg_keys[6], (2, HEADS, BW, BW), BW ** -0.5, 0.375, ((3, 8),)),
        "gate_biases": noise(arg_keys[7], (2, LRU), 1.0, 4.0, ((1, 8),)),
        "decay_param": draw_decay_param(jax.random.fold_in(arg_keys[12], 71), 0),
        "out_weight": noise(arg_keys[9], (LRU, D), LRU ** -0.5, 0.125, ((0, 8),)),
        "mlp_in_weight": noise(arg_keys[10], (D, 2, FF), D ** -0.5, 0.125, ((2, 8),)),
        "mlp_out_weight": noise(arg_keys[11], (FF, D), FF ** -0.5, 0.078125, ((0, 8),)),
    }


@jax.custom_vjp
def low(v):
    return lax.optimization_barrier(v.astype(jnp.bfloat16)).astype(jnp.float32)

@jax.custom_vjp
def low_back(v):
    return v

def low_keep(v):
    return (low(v), None)

def low_pass(kept, grad):
    return (grad,)

def back_keep(v):
    return (v, None)

def back_low(kept, grad):
    return (low(grad),)
low.defvjp(low_keep, low_pass)
low_back.defvjp(back_keep, back_low)

def matmul(left, right):
    return jnp.dot(left, right, precision=lax.Precision.HIGHEST, preferred_element_type=jnp.float32)

def rms_scale(values, gain):
    return values * lax.rsqrt(lax.optimization_barrier(jnp.mean(values * values, axis=-1, keepdims=True)) + 1e-06) * gain

def linear_recurrence(decay, inflow):

    def one_step(state, pair):
        state = pair[0] * state + pair[1]
        return (state, state)

    def one_block(state, pair):
        return lax.scan(one_step, state, pair)
    blocked = (decay.reshape(N_WIDE, TOK_DEV, LRU), inflow.reshape(N_WIDE, TOK_DEV, LRU))
    _, states = lax.scan(jax.checkpoint(one_block), jnp.zeros((LRU,), jnp.float32), blocked)
    return states.reshape(SEQ_LEN, LRU)

def forward(tokens, norm_gains, in_weight, conv_weight, conv_bias, gate_weights, gate_biases, decay_param, out_weight, mlp_in_weight, mlp_out_weight):
    normed = low(rms_scale(tokens, norm_gains[0]))
    projected = low_back(matmul(normed, in_weight.reshape(D, 2 * LRU)))
    branch = low(projected[:, :LRU])
    gate_branch = projected[:, LRU:]
    padded = jnp.concatenate([jnp.zeros((CONV - 1, LRU), jnp.float32), branch], axis=0)
    conv_out = conv_bias
    for offset in range(CONV):
        conv_out = conv_out + conv_weight[offset] * padded[CONV - 1 - offset:CONV - 1 - offset + SEQ_LEN]
    conv_low = low(conv_out)
    blocks = jnp.einsum('thc,ghcd->gthd', conv_low.reshape(SEQ_LEN, HEADS, LRU // HEADS), gate_weights, precision=lax.Precision.HIGHEST)
    gate_pre = low_back(blocks.reshape(2, SEQ_LEN, LRU) + gate_biases[:, None, :])
    recur_gate = jax.nn.sigmoid(gate_pre[0])
    input_gate = jax.nn.sigmoid(gate_pre[1])
    log_decay = -8.0 * recur_gate * jax.nn.softplus(-decay_param)
    inflow = jnp.sqrt(-jnp.expm1(2.0 * log_decay)) * input_gate * conv_low
    states = linear_recurrence(jnp.exp(log_decay), inflow)
    mixed = low(jax.nn.gelu(gate_branch) * states)
    middle = tokens + low_back(matmul(mixed, out_weight))
    normed_two = low(rms_scale(middle, norm_gains[1]))
    gate_up = low_back(matmul(normed_two, mlp_in_weight.reshape(D, 2 * FF)))
    hidden = low(jax.nn.gelu(gate_up[:, :FF]) * gate_up[:, FF:])
    return middle + low_back(matmul(hidden, mlp_out_weight))

def reference(tokens, cotangent, norm_gains, in_weight, conv_weight, conv_bias, gate_weights, gate_biases, decay_param, out_weight, mlp_in_weight, mlp_out_weight):
    params = tuple((weight.astype(jnp.float32) for weight in (norm_gains, in_weight, conv_weight, conv_bias, gate_weights, gate_biases, decay_param, out_weight, mlp_in_weight, mlp_out_weight)))

    def one_sequence(totals, pair):
        result, pull = jax.vjp(forward, pair[0].astype(jnp.float32), *params)
        grads = pull(pair[1].astype(jnp.float32))
        totals = tuple((total + grad for total, grad in zip(totals, grads[1:])))
        return (totals, (result.astype(jnp.bfloat16), grads[0]))
    zeros = tuple((jnp.zeros_like(weight) for weight in params))
    totals, (outputs, input_grads) = lax.scan(one_sequence, zeros, (tokens, cotangent))
    return (outputs, input_grads, totals[0], totals[1], totals[2], totals[3], totals[4], totals[5], totals[6], totals[7], totals[8], totals[9])
```

```python
import functools
import math
import jax
import jax.numpy as jnp
from jax import lax
from jax.experimental import pallas as pl
from jax.experimental.pallas import tpu as pltpu
from jax.sharding import PartitionSpec as P

BF16 = jnp.bfloat16
F32 = jnp.float32
SUB = 8
LANES = 128
GELU_A = math.sqrt(2.0 / math.pi)
GELU_B = 0.044715


def gelu_parts(v):
    square = v * v
    th = jnp.tanh(GELU_A * v * (1.0 + GELU_B * square))
    value = 0.5 * v * (1.0 + th)
    slope = 0.5 * (1.0 + th) + 0.5 * v * (1.0 - th * th) * (
        GELU_A * (1.0 + 3.0 * GELU_B * square)
    )
    return value, slope


def minus_expm1(v):
    series = jnp.full_like(v, 1.0 / 40320.0)
    for factorial in (5040.0, 720.0, 120.0, 24.0, 6.0, 2.0, 1.0):
        series = series * v + 1.0 / factorial
    return jnp.where(v > -0.5, -v * series, 1.0 - jnp.exp(v))


def sub_iota(width):
    return lax.broadcasted_iota(jnp.int32, (SUB, width), 0)


def roll_down(v, first):
    return jnp.where(sub_iota(v.shape[1]) == 0, first, pltpu.roll(v, 1, 0))


def roll_up(v, last):
    return jnp.where(sub_iota(v.shape[1]) == SUB - 1, last, pltpu.roll(v, SUB - 1, 0))


def rows8(step):
    return pl.ds(pl.multiple_of(step * SUB, SUB), SUB)


def strided_load(refs, s, steps):
    return jnp.concatenate([r[pl.ds(s, SUB, stride=steps), :] for r in refs], axis=1)


def strided_store(ref, s, steps, v):
    for n in range(ref.shape[0]):
        ref.at[n][pl.ds(s, SUB, stride=steps), :] = v[:, n * LANES : (n + 1) * LANES]


def forward_kernel(*refs, taps, groups):
    branch_refs, gateb_refs = refs[:groups], refs[groups : 2 * groups]
    forward_body(branch_refs, gateb_refs, *refs[2 * groups :], taps=taps)


def forward_body(
    branch_refs,
    gateb_refs,
    chan_ref,
    gw_ref,
    mixed_ref,
    states_ref,
    decay_ref,
    rgate_ref,
    igate_ref,
    scale_ref,
    low_ref,
    brow_ref,
    gperm_ref,
    enter_ref,
    ext,
    pre0,
    pre1,
    prod,
    mix,
    tail,
    carry,
    *,
    taps,
):
    rows, width = states_ref.shape
    steps = rows // SUB
    halo = taps - 1

    @pl.when(pl.program_id(1) == 0)
    def _():
        tail[...] = jnp.zeros_like(tail)
        carry[...] = jnp.zeros_like(carry)

    def load(s, _):
        v = strided_load(branch_refs, s, steps).astype(BF16).astype(F32)
        ext[rows8(s + halo), :] = v
        gperm_ref[rows8(s), :] = strided_load(gateb_refs, s, steps)
        return 0

    lax.fori_loop(0, steps, load, 0, unroll=4)
    for back in range(1, halo + 1):
        v = ext[rows8(halo + steps - back), :]
        ext[rows8(halo - back), :] = roll_down(v, tail[back - 1 : back, :])
        tail[back - 1 : back, :] = v[SUB - 1 : SUB]
    big = 8
    wide = SUB * big

    def block(i):
        return pl.ds(pl.multiple_of(i * wide, wide), wide)

    def conv(i, _):
        out = chan_ref[taps : taps + 1, :]
        for k in range(taps):
            v = ext[pl.ds(pl.multiple_of((i * big + halo - k) * SUB, SUB), wide), :]
            out = out + chan_ref[k : k + 1, :] * v
            if k == 0:
                brow_ref[block(i), :] = v.astype(BF16)
        low_ref[block(i), :] = out.astype(BF16)
        return 0

    lax.fori_loop(0, steps // big, conv, 0)
    low = low_ref[...]
    pre0[...] = jnp.dot(low, gw_ref[0, 0], preferred_element_type=F32)
    pre1[...] = jnp.dot(low, gw_ref[1, 0], preferred_element_type=F32)

    def gates(i, _):
        r = jax.nn.sigmoid(pre0[block(i), :] + chan_ref[taps + 1 : taps + 2, :])
        g = jax.nn.sigmoid(pre1[block(i), :] + chan_ref[taps + 2 : taps + 3, :])
        log_decay = r * chan_ref[taps + 3 : taps + 4, :]
        scale = jnp.sqrt(minus_expm1(2.0 * log_decay))
        rgate_ref[block(i), :] = r
        igate_ref[block(i), :] = g
        scale_ref[block(i), :] = scale
        decay_ref[block(i), :] = jnp.exp(log_decay)
        pre0[block(i), :] = scale * g * low_ref[block(i), :].astype(F32)
        return 0

    lax.fori_loop(0, steps // big, gates, 0)

    def scan(s, hp):
        h, p = hp
        a = decay_ref[rows8(s), :]
        h = a * h + pre0[rows8(s), :]
        p = a * p
        states_ref[rows8(s), :] = h
        prod[rows8(s), :] = p
        return h, p

    zero = jnp.zeros((SUB, width), F32)
    h, p = lax.fori_loop(0, steps, scan, (zero, zero + 1.0), unroll=8)
    for shift in (1, 2, 4):
        keep = sub_iota(width) >= shift
        h = h + p * jnp.where(keep, pltpu.roll(h, shift, 0), 0.0)
        p = p * jnp.where(keep, pltpu.roll(p, shift, 0), 1.0)
    first = carry[0:1, :]
    ends = h + p * first
    enter = roll_down(ends, first)
    enter_ref[...] = enter
    carry[0:1, :] = ends[SUB - 1 : SUB]

    def finish(s, _):
        state = states_ref[rows8(s), :] + prod[rows8(s), :] * enter
        states_ref[rows8(s), :] = state
        value, _ = gelu_parts(gperm_ref[rows8(s), :])
        strided_store(mix, s, steps, value * state)
        return 0

    lax.fori_loop(0, steps, finish, 0, unroll=8)
    for n in range(width // LANES):
        mixed_ref[:, n * LANES : (n + 1) * LANES] = mix[n].astype(BF16)


def recur_forward(projected, chan, gate_w, taps, chunk):
    total, width = projected.shape[0], projected.shape[1] // 2
    head = gate_w.shape[2]
    heads = width // head
    chunks = total // chunk
    rows = lambda j, c: (c, j)
    blk = pl.BlockSpec((chunk, head), rows)
    f32s = jax.ShapeDtypeStruct((total, width), F32)
    b16s = jax.ShapeDtypeStruct((total, width), BF16)
    work = pltpu.VMEM((chunk, head), F32)
    groups = head // LANES
    lane = [
        pl.BlockSpec((chunk, LANES), lambda j, c, n=n: (c, j * groups + n))
        for n in (*range(groups), *range(width // LANES, width // LANES + groups))
    ]
    return pl.pallas_call(
        functools.partial(forward_kernel, taps=taps, groups=groups),
        grid=(heads, chunks),
        in_specs=[
            *lane,
            pl.BlockSpec((chan.shape[0], head), lambda j, c: (0, j)),
            pl.BlockSpec((2, 1, head, head), lambda j, c: (0, j, 0, 0)),
        ],
        out_specs=[blk] * 9 + [pl.BlockSpec((SUB, head), rows)],
        out_shape=[b16s, f32s, f32s, f32s, f32s, f32s, b16s, b16s, f32s]
        + [jax.ShapeDtypeStruct((chunks * SUB, width), F32)],
        scratch_shapes=[
            pltpu.VMEM((chunk + (taps - 1) * SUB, head), F32),
            work,
            work,
            work,
            pltpu.VMEM((groups, chunk, LANES), F32),
            pltpu.VMEM((SUB, head), F32),
            pltpu.VMEM((SUB, head), F32),
        ],
        compiler_params=pltpu.CompilerParams(
            dimension_semantics=("arbitrary", "arbitrary"), vmem_limit_bytes=60 << 20
        ),
        name="recur_forward",
    )(*[projected] * 2 * groups, chan, gate_w)


def backward_kernel(*refs, taps, groups):
    backward_body(refs[:groups], *refs[groups:], taps=taps)


def backward_body(
    mgrad_refs,
    states_ref,
    decay_ref,
    rgate_ref,
    igate_ref,
    scale_ref,
    low_ref,
    brow_ref,
    gperm_ref,
    enter_ref,
    chan_ref,
    gw_ref,
    pgrad_ref,
    gwg_ref,
    sums_ref,
    car,
    prod,
    cgrad,
    lowf,
    gout,
    pre,
    sums,
    tail,
    carry,
    *,
    taps,
):
    rows, width = states_ref.shape
    steps = rows // SUB
    halo = taps - 1
    big = 8
    wide = SUB * big

    @pl.when(pl.program_id(1) == 0)
    def _():
        tail[...] = jnp.zeros_like(tail)
        carry[...] = jnp.zeros_like(carry)
        sums[...] = jnp.zeros_like(sums)
        gwg_ref[...] = jnp.zeros_like(gwg_ref)

    def block(i):
        return pl.ds(pl.multiple_of(i * wide, wide), wide)

    def scan(n, uq):
        u, q = uq
        s = steps - 1 - n
        value, slope = gelu_parts(gperm_ref[rows8(s), :])
        mg = strided_load(mgrad_refs, s, steps)
        strided_store(gout, s, steps, mg * states_ref[rows8(s), :] * slope)
        c = mg * value + u
        car[rows8(s), :] = c
        prod[rows8(s), :] = q
        a = decay_ref[rows8(s), :]
        return a * c, a * q

    zero = jnp.zeros((SUB, width), F32)
    u, q = lax.fori_loop(0, steps, scan, (zero, zero + 1.0), unroll=8)
    for shift in (1, 2, 4):
        keep = sub_iota(width) < SUB - shift
        u = u + q * jnp.where(keep, pltpu.roll(u, SUB - shift, 0), 0.0)
        q = q * jnp.where(keep, pltpu.roll(q, SUB - shift, 0), 1.0)
    last = carry[0:1, :]
    ends = u + q * last
    enter = roll_up(ends, last)
    carry[0:1, :] = ends[0:1]
    for n in range(width // LANES):
        pgrad_ref[1, :, n * LANES : (n + 1) * LANES] = gout[n].astype(BF16)
    neg = chan_ref[taps + 3 : taps + 4, :]
    state_in = enter_ref[...]

    def gates(s, acc):
        sum_r, sum_i, sum_d = acc
        c = car[rows8(s), :] + prod[rows8(s), :] * enter
        before = jnp.where(
            s == 0, state_in, states_ref[rows8(jnp.maximum(s - 1, 0)), :]
        )
        a = decay_ref[rows8(s), :]
        r = rgate_ref[rows8(s), :]
        g = igate_ref[rows8(s), :]
        scale = scale_ref[rows8(s), :]
        low = lowf[rows8(s), :]
        c_low = c * low
        dgrad = c * a * before - c_low * g * (a * a) / scale
        pr = dgrad * neg * r * (1.0 - r)
        pi = c_low * scale * g * (1.0 - g)
        pre[0, rows8(s), :] = pr
        pre[1, rows8(s), :] = pi
        cgrad[rows8(s), :] = c * scale * g
        pr = pr.astype(BF16).astype(F32)
        pi = pi.astype(BF16).astype(F32)
        return sum_r + pr, sum_i + pi, sum_d + dgrad * r

    lowf[...] = low_ref[...].astype(F32)
    sum_r, sum_i, sum_d = lax.fori_loop(0, steps, gates, (zero, zero, zero), unroll=4)
    low = low_ref[...]
    pr = pre[0].astype(BF16)
    pi = pre[1].astype(BF16)
    back = (((1,), (1,)), ((), ()))
    over = (((0,), (0,)), ((), ()))
    gwg_ref[0, 0] += lax.dot_general(low, pr, over, preferred_element_type=F32)
    gwg_ref[1, 0] += lax.dot_general(low, pi, over, preferred_element_type=F32)
    cgrad[pl.ds(0, rows), :] = (
        cgrad[pl.ds(0, rows), :]
        + lax.dot_general(pr, gw_ref[0, 0], back, preferred_element_type=F32)
        + lax.dot_general(pi, gw_ref[1, 0], back, preferred_element_type=F32)
    )
    for ahead in range(halo):
        v = cgrad[rows8(ahead), :]
        cgrad[rows8(steps + ahead), :] = roll_up(v, tail[ahead : ahead + 1, :])
        tail[ahead : ahead + 1, :] = v[0:1]
    car[...] = brow_ref[...].astype(F32)

    def conv(s, acc):
        branch = car[rows8(s), :]
        out = zero
        new = []
        for k in range(taps):
            v = cgrad[rows8(s + k), :]
            out = out + chan_ref[k : k + 1, :] * v
            new.append(acc[k] + v * branch)
            if k == 0:
                new_bias = acc[taps] + v
        strided_store(gout, s, steps, out)
        return (*new, new_bias)

    acc = lax.fori_loop(0, steps, conv, (zero,) * (taps + 1), unroll=4)
    for n in range(width // LANES):
        pgrad_ref[0, :, n * LANES : (n + 1) * LANES] = gout[n].astype(BF16)
    for n, v in enumerate((*acc, sum_r, sum_i, sum_d)):
        sums[n] += v
        sums_ref[n : n + 1, :] = jnp.sum(sums[n], axis=0, keepdims=True)


def recur_backward(mixed_grad, saved, chan, gate_w, taps, chunk):
    total, width = mixed_grad.shape
    head = gate_w.shape[2]
    heads = width // head
    chunks = total // chunk
    rows = lambda j, c: (chunks - 1 - c, j)
    blk = pl.BlockSpec((chunk, head), rows)
    work = pltpu.VMEM((chunk, head), F32)
    gws = pl.BlockSpec((2, 1, head, head), lambda j, c: (0, j, 0, 0))
    groups = head // LANES
    lane = [
        pl.BlockSpec((chunk, LANES), lambda j, c, n=n: (chunks - 1 - c, j * groups + n))
        for n in range(groups)
    ]
    n_sums = -(-(taps + 4) // SUB) * SUB
    return pl.pallas_call(
        functools.partial(backward_kernel, taps=taps, groups=groups),
        grid=(heads, chunks),
        in_specs=lane
        + [blk] * 8
        + [
            pl.BlockSpec((SUB, head), rows),
            pl.BlockSpec((chan.shape[0], head), lambda j, c: (0, j)),
            gws,
        ],
        out_specs=[
            pl.BlockSpec((2, chunk, head), lambda j, c: (0, chunks - 1 - c, j)),
            gws,
            pl.BlockSpec((n_sums, head), lambda j, c: (0, j)),
        ],
        out_shape=[
            jax.ShapeDtypeStruct((2, total, width), BF16),
            jax.ShapeDtypeStruct((2, heads, head, head), F32),
            jax.ShapeDtypeStruct((n_sums, width), F32),
        ],
        scratch_shapes=[
            work,
            work,
            pltpu.VMEM((chunk + (taps - 1) * SUB, head), F32),
            work,
            pltpu.VMEM((groups, chunk, LANES), F32),
            pltpu.VMEM((2, chunk, head), F32),
            pltpu.VMEM((taps + 4, SUB, head), F32),
            pltpu.VMEM((SUB, head), F32),
            pltpu.VMEM((SUB, head), F32),
        ],
        compiler_params=pltpu.CompilerParams(
            dimension_semantics=("arbitrary", "arbitrary"), vmem_limit_bytes=60 << 20
        ),
        name="recur_backward",
    )(*[mixed_grad] * groups, *saved, chan, gate_w)


def bit_list(n):
    return [1 << i for i in range(n.bit_length() - 1)]


def swap(block, axis, bit):
    return lax.ppermute(block, axis, [(i, i ^ bit) for i in range(lax.axis_size(axis))])


def gather_near(block):
    n = lax.axis_size("wide")
    core, *links = bit_list(n)
    half = block.shape[1] // 2
    sides = []
    for part, order in ((block[:, :half], links), (block[:, half:], links[::-1])):
        held = part
        for m, bit in enumerate(order):
            held = jnp.stack([held, swap(held, "wide", bit)], axis=m)
        place = sorted(range(len(order)), key=lambda i: -order[i])
        sides.append(held.transpose(*place, len(order), len(order) + 1))
    both = jnp.concatenate(sides, axis=-1)
    both = jnp.stack([both, swap(both, "wide", core)], axis=-3)
    return both.reshape(n * block.shape[0], block.shape[1])


def scatter_near(parts):
    n = lax.axis_size("wide")
    core, *links = bit_list(n)
    rows, width = parts.shape[0] // n, parts.shape[1]
    held = parts.reshape((2,) * len(links) + (2, rows, width))
    held = held[..., 0, :, :].astype(F32) + swap(
        held[..., 1, :, :].astype(BF16), "wide", core
    ).astype(F32)
    half = width // 2
    sides = []
    for part, order in ((held[..., :half], links), (held[..., half:], links[::-1])):
        axes = links[::-1]
        for bit in order:
            axis = axes.index(bit)
            keep = lax.index_in_dim(part, 0, axis, keepdims=False)
            send = lax.index_in_dim(part, 1, axis, keepdims=False).astype(BF16)
            part = keep + swap(send, "wide", bit).astype(F32)
            axes = axes[:axis] + axes[axis + 1 :]
        sides.append(part)
    return jnp.concatenate(sides, axis=-1)


def reorder(rows):
    n = lax.axis_size("wide")
    here = lax.axis_index("wide")
    size = rows.shape[0] // n
    return jnp.concatenate(
        [lax.dynamic_slice_in_dim(rows, (here ^ r) * size, size) for r in range(n)]
    )


def norm_rows(rows):
    inv = lax.rsqrt(jnp.mean(rows * rows, axis=-1, keepdims=True) + 1e-06)
    return inv, rows * inv


def norm_back(grad, gain, inv, unit):
    scaled = grad * gain
    return inv * (scaled - unit * jnp.mean(scaled * unit, axis=-1, keepdims=True))


def dot(left, right):
    return jnp.dot(left, right, preferred_element_type=F32)


def dot_over(left, right):
    return lax.dot_general(
        left, right, (((0,), (0,)), ((), ())), preferred_element_type=F32
    )


def dot_back(left, right):
    return lax.dot_general(
        left, right, (((1,), (1,)), ((), ())), preferred_element_type=F32
    )


def feed_forward(normed, cot, weight_in, weight_out):
    hidden_width = weight_out.shape[0]
    gate_up = dot(normed, weight_in)
    gate, up = gate_up[:, :hidden_width], gate_up[:, hidden_width:]
    value, slope = gelu_parts(gate)
    hidden_grad = dot_back(cot, weight_out)
    hidden = (value * up).astype(BF16)
    gate_up_grad = jnp.concatenate(
        [
            (hidden_grad * up * slope).astype(BF16),
            (hidden_grad * value).astype(BF16),
        ],
        axis=1,
    )
    return hidden, gate_up_grad


def shards(
    tokens,
    cotangent,
    norm_gains,
    in_weight,
    conv_weight,
    conv_bias,
    gate_weights,
    gate_biases,
    decay_param,
    out_weight,
    mlp_in_weight,
    mlp_out_weight,
):
    n_wide, n_seq = lax.axis_size("wide"), lax.axis_size("seq")
    here = lax.axis_index("wide")
    tok_low, cot_low = tokens[0], cotangent[0]
    size, width = tok_low.shape
    own = out_weight.shape[0]
    lru = own * n_wide
    heads, head = gate_weights.shape[1:3]
    taps = conv_weight.shape[0]
    gain_own = norm_gains.shape[1]

    span = max(
        ((w + 1) * own - 1) // head - w * own // head + 1 for w in range(n_wide)
    )
    firsts = [min(w * own // head, heads - span) for w in range(n_wide)]
    win = span * head
    start = jnp.minimum(here * own // head, heads - span) * head
    offset = here * own - start

    small = lax.all_gather(
        jnp.concatenate(
            [
                norm_gains.reshape(-1),
                conv_weight.reshape(-1),
                conv_bias,
                gate_biases.reshape(-1),
                decay_param,
            ]
        ),
        "wide",
    )
    gains = (
        small[:, : 2 * gain_own]
        .reshape(n_wide, 2, gain_own)
        .transpose(1, 0, 2)
        .reshape(2, width)
        .astype(F32)
    )
    channels = (
        small[:, 2 * gain_own :]
        .reshape(n_wide, taps + 4, own)
        .transpose(1, 0, 2)
        .reshape(taps + 4, lru)
    )
    channels = lax.dynamic_slice_in_dim(channels, start, win, axis=1).astype(F32)
    chan = jnp.concatenate(
        [channels[: taps + 3], -8.0 * jax.nn.softplus(-channels[taps + 3 :])]
    )

    tok_all = lax.all_gather(tok_low, "wide", axis=0, tiled=True)
    in_win = lax.all_to_all(
        jnp.stack(
            [
                jnp.concatenate(
                    [
                        in_weight[:, h, f * head : f * head + win]
                        for h in range(2)
                    ],
                    axis=1,
                )
                for f in firsts
            ]
        ),
        "wide",
        split_axis=0,
        concat_axis=0,
        tiled=True,
    ).reshape(width, 2 * win)
    gate_w = lax.all_to_all(
        jnp.stack([gate_weights[:, f : f + span] for f in firsts]),
        "wide",
        split_axis=0,
        concat_axis=0,
        tiled=True,
    )
    gate_w = jnp.moveaxis(gate_w, 0, 3).reshape(2, span, head, head)

    below = max(w * own - f * head for w, f in enumerate(firsts))
    above = max(f * head + win - (w + 1) * own for w, f in enumerate(firsts))
    if max(below, above) <= own:
        lower = lax.ppermute(
            out_weight[own - below :], "wide", [(i, i + 1) for i in range(n_wide - 1)]
        )
        upper = lax.ppermute(
            out_weight[:above], "wide", [(i + 1, i) for i in range(n_wide - 1)]
        )
        out_win = lax.dynamic_slice_in_dim(
            jnp.concatenate([lower, out_weight, upper]), below - offset, win
        )
    else:
        out_win = lax.dynamic_slice_in_dim(
            lax.all_gather(out_weight, "wide", axis=0, tiled=True), start, win
        )
    out_own = lax.dynamic_update_slice_in_dim(
        jnp.zeros((win, width), BF16), out_weight, offset, 0
    )
    in_own = jnp.concatenate(
        [
            lax.dynamic_slice_in_dim(in_win, h * win + offset, own, axis=1)
            for h in range(2)
        ],
        axis=1,
    )

    cot_near = gather_near(cot_low)
    total = size * n_wide
    recompute = n_seq * total <= 8192 and n_seq & (n_seq - 1) == 0 and n_seq > 1

    def others(rows):
        sent = jnp.concatenate([swap(rows, "seq", d) for d in range(1, n_seq)])
        return lax.all_gather(sent, "wide", axis=0, tiled=True)

    inv_all, unit_all = norm_rows(tok_all.astype(F32))
    normed_all = (unit_all * gains[0]).astype(BF16)
    projected = dot(normed_all, in_win)
    chunk = min(total, 512)
    mixed, *saved = recur_forward(projected, chan, gate_w, taps, chunk)
    mixed_near = reorder(mixed)
    rows = tok_low.astype(F32)
    middle = rows + scatter_near(dot(mixed_near, out_own).astype(BF16))
    inv_two, unit_two = norm_rows(middle)
    normed_two = (unit_two * gains[1]).astype(BF16)

    mlp_in = mlp_in_weight.reshape(width, -1)
    normed_near = gather_near(normed_two)
    hidden, gate_up_grad = feed_forward(normed_near, cot_near, mlp_in, mlp_out_weight)
    mlp_out_grad = dot_over(hidden, cot_near)
    mlp_in_grad = dot_over(normed_near, gate_up_grad)
    normed_two_grad = scatter_near(dot_back(gate_up_grad, mlp_in).astype(BF16))
    feed = scatter_near(dot(hidden, mlp_out_weight).astype(BF16))
    result = (middle + feed).astype(BF16)
    middle_grad = cot_low.astype(F32) + norm_back(
        normed_two_grad, gains[1], inv_two, unit_two
    )
    gain_two_grad = jnp.sum(normed_two_grad * unit_two, axis=0)

    mix_near = gather_near(middle_grad.astype(BF16))
    mixed_grad = reorder(dot_back(mix_near, out_win))
    projected_grad, gate_grad, sums = recur_backward(
        mixed_grad, saved, chan, gate_w, taps, chunk
    )
    out_grad = lax.dynamic_slice_in_dim(
        dot_over(mixed_near, mix_near).astype(BF16), offset, own
    )
    own_grad = jnp.concatenate(
        [
            lax.dynamic_slice_in_dim(projected_grad[h], offset, own, axis=1)
            for h in range(2)
        ],
        axis=1,
    )
    normed_grad_part = dot_back(reorder(own_grad), in_own).astype(BF16)
    in_grad = lax.all_to_all(
        dot_over(normed_all, own_grad).astype(BF16).reshape(n_wide, -1, 2 * own),
        "wide",
        split_axis=0,
        concat_axis=0,
        tiled=True,
    )
    in_grad = jnp.concatenate(
        [
            jnp.moveaxis(in_grad[:, :, h * own : (h + 1) * own], 0, 1).reshape(-1, 1, lru)
            for h in range(2)
        ],
        axis=1,
    )
    part = head // n_wide
    gate_grad = lax.all_to_all(
        jnp.moveaxis(
            gate_grad.astype(BF16).reshape(2, span, head, n_wide, part), 3, 0
        ),
        "wide",
        split_axis=0,
        concat_axis=0,
        tiled=True,
    )
    holders = [
        next(w for w, f in enumerate(firsts) if f <= j < f + span) for j in range(heads)
    ]
    gate_grad = jnp.stack(
        [gate_grad[w, :, j - firsts[w]] for j, w in enumerate(holders)], axis=1
    )
    normed_grad = scatter_near(normed_grad_part)
    inv_one, unit_one = norm_rows(rows)
    input_grad = middle_grad + norm_back(normed_grad, gains[0], inv_one, unit_one)
    gain_one_grad = jnp.sum(normed_grad * unit_one, axis=0)

    gains_grad = lax.psum(jnp.stack([gain_one_grad, gain_two_grad]), ("seq", "wide"))
    gains_grad = lax.dynamic_slice_in_dim(gains_grad, here * gain_own, gain_own, axis=1)
    sums = lax.psum(
        lax.dynamic_slice_in_dim(sums[: taps + 4], offset, own, axis=1), "seq"
    )
    decay_grad = sums[taps + 3] * 8.0 * jax.nn.sigmoid(-decay_param.astype(F32))
    in_grad, out_grad, gate_grad = (
        lax.psum(g, "seq").astype(F32) for g in (in_grad, out_grad, gate_grad)
    )
    if recompute:
        normed_far, cot_far = others(normed_two), others(cot_low)
        hidden_far, gate_up_far = feed_forward(
            normed_far, cot_far, mlp_in, mlp_out_weight
        )
        mlp_out_grad = mlp_out_grad + dot_over(hidden_far, cot_far)
        mlp_in_grad = mlp_in_grad + dot_over(normed_far, gate_up_far)
    else:
        mlp_out_grad, mlp_in_grad = (
            lax.psum(g.astype(BF16), "seq").astype(F32)
            for g in (mlp_out_grad, mlp_in_grad)
        )
    return (
        result[None],
        input_grad[None],
        gains_grad,
        in_grad,
        sums[:taps],
        sums[taps],
        gate_grad,
        sums[taps + 1 : taps + 3],
        decay_grad,
        out_grad,
        mlp_in_grad.reshape(mlp_in_weight.shape),
        mlp_out_grad,
    )


def solution(mesh):
    placed = (
        P("seq", "wide", None),
        P("seq", "wide", None),
        P(None, "wide"),
        P("wide", None, None),
        P(None, "wide"),
        P("wide"),
        P(None, None, None, "wide"),
        P(None, "wide"),
        P("wide"),
        P("wide", None),
        P(None, None, "wide"),
        P("wide", None),
    )
    return jax.shard_map(
        shards,
        mesh=mesh,
        in_specs=placed,
        out_specs=(
            P("seq", "wide", None),
            P("seq", "wide", None),
            P(None, "wide"),
            P("wide", None, None),
            P(None, "wide"),
            P("wide"),
            P(None, None, None, "wide"),
            P(None, "wide"),
            P("wide"),
            P("wide", None),
            P(None, None, "wide"),
            P("wide", None),
        ),
        check_vma=False,
    )
```

```python
import functools
import math
import jax
import jax.numpy as jnp
from jax import lax
from jax.experimental import pallas as pl
from jax.experimental.pallas import tpu as pltpu
from jax.sharding import PartitionSpec as P

BF16 = jnp.bfloat16
F32 = jnp.float32
SUB = 8
LANES = 128
GELU_A = math.sqrt(2.0 / math.pi)
GELU_B = 0.044715


def dot(left, right):
    return jnp.dot(left, right, preferred_element_type=F32)


def dot_over(left, right):
    return lax.dot_general(
        left, right, (((0,), (0,)), ((), ())), preferred_element_type=F32
    )


def dot_back(left, right):
    return lax.dot_general(
        left, right, (((1,), (1,)), ((), ())), preferred_element_type=F32
    )


def gelu_parts(v):
    square = v * v
    th = jnp.tanh(GELU_A * v * (1.0 + GELU_B * square))
    value = 0.5 * v * (1.0 + th)
    slope = 0.5 * (1.0 + th) + 0.5 * v * (1.0 - th * th) * (
        GELU_A * (1.0 + 3.0 * GELU_B * square)
    )
    return value, slope


def minus_expm1(v):
    series = jnp.full_like(v, 1.0 / 40320.0)
    for factorial in (5040.0, 720.0, 120.0, 24.0, 6.0, 2.0, 1.0):
        series = series * v + 1.0 / factorial
    return jnp.where(v > -0.5, -v * series, 1.0 - jnp.exp(v))


def sub_iota(width):
    return lax.broadcasted_iota(jnp.int32, (SUB, width), 0)


def roll_down(v, first):
    return jnp.where(sub_iota(v.shape[1]) == 0, first, pltpu.roll(v, 1, 0))


def roll_up(v, last):
    return jnp.where(sub_iota(v.shape[1]) == SUB - 1, last, pltpu.roll(v, SUB - 1, 0))


def rows8(step):
    return pl.ds(pl.multiple_of(step * SUB, SUB), SUB)


def strided_load(refs, s, steps):
    return jnp.concatenate([r[pl.ds(s, SUB, stride=steps), :] for r in refs], axis=1)


def strided_store(ref, s, steps, v):
    for n in range(ref.shape[0]):
        ref.at[n][pl.ds(s, SUB, stride=steps), :] = v[:, n * LANES : (n + 1) * LANES]


def forward_kernel(*refs, taps, groups):
    forward_body(refs[:groups], *refs[groups:], taps=taps)


def forward_body(
    branch_refs,
    chan_ref,
    gw_ref,
    states_ref,
    decay_ref,
    rgate_ref,
    igate_ref,
    scale_ref,
    low_ref,
    brow_ref,
    enter_ref,
    ext,
    pre0,
    pre1,
    prod,
    tail,
    carry,
    *,
    taps,
):
    rows, width = states_ref.shape
    steps = rows // SUB
    halo = taps - 1

    @pl.when(pl.program_id(1) == 0)
    def _():
        tail[...] = jnp.zeros_like(tail)
        carry[...] = jnp.zeros_like(carry)

    def load(s, _):
        v = strided_load(branch_refs, s, steps).astype(BF16).astype(F32)
        ext[rows8(s + halo), :] = v
        return 0

    lax.fori_loop(0, steps, load, 0, unroll=4)
    for back in range(1, halo + 1):
        v = ext[rows8(halo + steps - back), :]
        ext[rows8(halo - back), :] = roll_down(v, tail[back - 1 : back, :])
        tail[back - 1 : back, :] = v[SUB - 1 : SUB]
    big = 8
    wide = SUB * big

    def block(i):
        return pl.ds(pl.multiple_of(i * wide, wide), wide)

    def conv(i, _):
        out = chan_ref[taps : taps + 1, :]
        for k in range(taps):
            v = ext[pl.ds(pl.multiple_of((i * big + halo - k) * SUB, SUB), wide), :]
            out = out + chan_ref[k : k + 1, :] * v
            if k == 0:
                brow_ref[block(i), :] = v.astype(BF16)
        low_ref[block(i), :] = out.astype(BF16)
        return 0

    lax.fori_loop(0, steps // big, conv, 0)
    low = low_ref[...]
    pre0[...] = dot_back(low, gw_ref[0, 0])
    pre1[...] = dot_back(low, gw_ref[1, 0])

    def gates(i, _):
        r = jax.nn.sigmoid(pre0[block(i), :] + chan_ref[taps + 1 : taps + 2, :])
        g = jax.nn.sigmoid(pre1[block(i), :] + chan_ref[taps + 2 : taps + 3, :])
        log_decay = r * chan_ref[taps + 3 : taps + 4, :]
        scale = jnp.sqrt(minus_expm1(2.0 * log_decay))
        rgate_ref[block(i), :] = r
        igate_ref[block(i), :] = g
        scale_ref[block(i), :] = scale
        decay_ref[block(i), :] = jnp.exp(log_decay)
        pre0[block(i), :] = scale * g * low_ref[block(i), :].astype(F32)
        return 0

    lax.fori_loop(0, steps // big, gates, 0)

    def scan(s, hp):
        h, p = hp
        a = decay_ref[rows8(s), :]
        h = a * h + pre0[rows8(s), :]
        p = a * p
        states_ref[rows8(s), :] = h
        prod[rows8(s), :] = p
        return h, p

    zero = jnp.zeros((SUB, width), F32)
    h, p = lax.fori_loop(0, steps, scan, (zero, zero + 1.0), unroll=8)
    for shift in (1, 2, 4):
        keep = sub_iota(width) >= shift
        h = h + p * jnp.where(keep, pltpu.roll(h, shift, 0), 0.0)
        p = p * jnp.where(keep, pltpu.roll(p, shift, 0), 1.0)
    first = carry[0:1, :]
    ends = h + p * first
    enter = roll_down(ends, first)
    enter_ref[...] = enter
    carry[0:1, :] = ends[SUB - 1 : SUB]

    def finish(s, _):
        states_ref[rows8(s), :] = states_ref[rows8(s), :] + prod[rows8(s), :] * enter
        return 0

    lax.fori_loop(0, steps, finish, 0, unroll=8)


def mix_kernel(*refs, groups):
    states_ref, mixed_ref, gperm_ref, out = refs[groups:]
    rows, width = states_ref.shape
    steps = rows // SUB

    def body(s, _):
        v = strided_load(refs[:groups], s, steps)
        gperm_ref[rows8(s), :] = v
        strided_store(out, s, steps, gelu_parts(v)[0] * states_ref[rows8(s), :])
        return 0

    lax.fori_loop(0, steps, body, 0, unroll=8)
    for n in range(width // LANES):
        mixed_ref[:, n * LANES : (n + 1) * LANES] = out[n].astype(BF16)


def mix_forward(gate_branch, states, head, chunk):
    total, width = states.shape
    groups = head // LANES
    blk = pl.BlockSpec((chunk, head), lambda j, c: (c, j))
    lane = [
        pl.BlockSpec((chunk, LANES), lambda j, c, n=n: (c, j * groups + n))
        for n in range(groups)
    ]
    return pl.pallas_call(
        functools.partial(mix_kernel, groups=groups),
        grid=(width // head, total // chunk),
        in_specs=lane + [blk],
        out_specs=[blk, blk],
        out_shape=[
            jax.ShapeDtypeStruct((total, width), BF16),
            jax.ShapeDtypeStruct((total, width), F32),
        ],
        scratch_shapes=[pltpu.VMEM((groups, chunk, LANES), F32)],
        compiler_params=pltpu.CompilerParams(
            dimension_semantics=("arbitrary", "arbitrary"), vmem_limit_bytes=60 << 20
        ),
        name="mix_forward",
    )(*[gate_branch] * groups, states)


def recur_forward(projected, chan, gate_w, taps, chunk):
    total, width = projected.shape
    head = gate_w.shape[2]
    heads = width // head
    chunks = total // chunk
    rows = lambda j, c: (c, j)
    blk = pl.BlockSpec((chunk, head), rows)
    f32s = jax.ShapeDtypeStruct((total, width), F32)
    b16s = jax.ShapeDtypeStruct((total, width), BF16)
    work = pltpu.VMEM((chunk, head), F32)
    groups = head // LANES
    lane = [
        pl.BlockSpec((chunk, LANES), lambda j, c, n=n: (c, j * groups + n))
        for n in range(groups)
    ]
    return pl.pallas_call(
        functools.partial(forward_kernel, taps=taps, groups=groups),
        grid=(heads, chunks),
        in_specs=[
            *lane,
            pl.BlockSpec((chan.shape[0], head), lambda j, c: (0, j)),
            pl.BlockSpec((2, 1, head, head), lambda j, c: (0, j, 0, 0)),
        ],
        out_specs=[blk] * 7 + [pl.BlockSpec((SUB, head), rows)],
        out_shape=[f32s, f32s, f32s, f32s, f32s, b16s, b16s]
        + [jax.ShapeDtypeStruct((chunks * SUB, width), F32)],
        scratch_shapes=[
            pltpu.VMEM((chunk + (taps - 1) * SUB, head), F32),
            work,
            work,
            work,
            pltpu.VMEM((SUB, head), F32),
            pltpu.VMEM((SUB, head), F32),
        ],
        compiler_params=pltpu.CompilerParams(
            dimension_semantics=("arbitrary", "arbitrary"), vmem_limit_bytes=60 << 20
        ),
        name="recur_forward",
    )(*[projected] * groups, chan, gate_w)


def gate_back_kernel(*refs, groups):
    mgrad_refs = refs[:groups]
    states_ref, gperm_ref, ggrad_ref, sgrad_ref, out = refs[groups:]
    rows, width = states_ref.shape
    steps = rows // SUB

    def body(s, _):
        value, slope = gelu_parts(gperm_ref[rows8(s), :])
        mg = strided_load(mgrad_refs, s, steps)
        strided_store(out, s, steps, mg * states_ref[rows8(s), :] * slope)
        sgrad_ref[rows8(s), :] = mg * value
        return 0

    lax.fori_loop(0, steps, body, 0, unroll=8)
    for n in range(width // LANES):
        ggrad_ref[:, n * LANES : (n + 1) * LANES] = out[n].astype(BF16)


def gate_backward(mixed_grad, states, gate_rows, head, chunk):
    total, width = mixed_grad.shape
    groups = head // LANES
    blk = pl.BlockSpec((chunk, head), lambda j, c: (c, j))
    lane = [
        pl.BlockSpec((chunk, LANES), lambda j, c, n=n: (c, j * groups + n))
        for n in range(groups)
    ]
    return pl.pallas_call(
        functools.partial(gate_back_kernel, groups=groups),
        grid=(width // head, total // chunk),
        in_specs=lane + [blk, blk],
        out_specs=[blk, blk],
        out_shape=[
            jax.ShapeDtypeStruct((total, width), BF16),
            jax.ShapeDtypeStruct((total, width), F32),
        ],
        scratch_shapes=[pltpu.VMEM((groups, chunk, LANES), F32)],
        compiler_params=pltpu.CompilerParams(
            dimension_semantics=("arbitrary", "arbitrary"), vmem_limit_bytes=60 << 20
        ),
        name="gate_backward",
    )(*[mixed_grad] * groups, states, gate_rows)


def backward_kernel(
    sgrad_ref,
    states_ref,
    decay_ref,
    rgate_ref,
    igate_ref,
    scale_ref,
    low_ref,
    brow_ref,
    enter_ref,
    chan_ref,
    gw_ref,
    pgrad_ref,
    gwg_ref,
    sums_ref,
    car,
    prod,
    cgrad,
    lowf,
    gout,
    pre,
    sums,
    tail,
    carry,
    *,
    taps,
):
    rows, width = states_ref.shape
    steps = rows // SUB
    halo = taps - 1

    @pl.when(pl.program_id(1) == 0)
    def _():
        tail[...] = jnp.zeros_like(tail)
        carry[...] = jnp.zeros_like(carry)
        sums[...] = jnp.zeros_like(sums)
        gwg_ref[...] = jnp.zeros_like(gwg_ref)

    def scan(n, uq):
        u, q = uq
        s = steps - 1 - n
        c = sgrad_ref[rows8(s), :] + u
        car[rows8(s), :] = c
        prod[rows8(s), :] = q
        a = decay_ref[rows8(s), :]
        return a * c, a * q

    zero = jnp.zeros((SUB, width), F32)
    u, q = lax.fori_loop(0, steps, scan, (zero, zero + 1.0), unroll=8)
    for shift in (1, 2, 4):
        keep = sub_iota(width) < SUB - shift
        u = u + q * jnp.where(keep, pltpu.roll(u, SUB - shift, 0), 0.0)
        q = q * jnp.where(keep, pltpu.roll(q, SUB - shift, 0), 1.0)
    last = carry[0:1, :]
    ends = u + q * last
    enter = roll_up(ends, last)
    carry[0:1, :] = ends[0:1]
    neg = chan_ref[taps + 3 : taps + 4, :]
    state_in = enter_ref[...]

    def gates(s, acc):
        sum_r, sum_i, sum_d = acc
        c = car[rows8(s), :] + prod[rows8(s), :] * enter
        before = jnp.where(
            s == 0, state_in, states_ref[rows8(jnp.maximum(s - 1, 0)), :]
        )
        a = decay_ref[rows8(s), :]
        r = rgate_ref[rows8(s), :]
        g = igate_ref[rows8(s), :]
        scale = scale_ref[rows8(s), :]
        low = lowf[rows8(s), :]
        c_low = c * low
        dgrad = c * a * before - c_low * g * (a * a) / scale
        pr = dgrad * neg * r * (1.0 - r)
        pi = c_low * scale * g * (1.0 - g)
        pre[0, rows8(s), :] = pr
        pre[1, rows8(s), :] = pi
        cgrad[rows8(s), :] = c * scale * g
        pr = pr.astype(BF16).astype(F32)
        pi = pi.astype(BF16).astype(F32)
        return sum_r + pr, sum_i + pi, sum_d + dgrad * r

    lowf[...] = low_ref[...].astype(F32)
    sum_r, sum_i, sum_d = lax.fori_loop(0, steps, gates, (zero, zero, zero), unroll=4)
    low = low_ref[...]
    pr = pre[0].astype(BF16)
    pi = pre[1].astype(BF16)
    gwg_ref[0, 0] += dot_over(pr, low)
    gwg_ref[1, 0] += dot_over(pi, low)
    cgrad[pl.ds(0, rows), :] = (
        cgrad[pl.ds(0, rows), :] + dot(pr, gw_ref[0, 0]) + dot(pi, gw_ref[1, 0])
    )
    for ahead in range(halo):
        v = cgrad[rows8(ahead), :]
        cgrad[rows8(steps + ahead), :] = roll_up(v, tail[ahead : ahead + 1, :])
        tail[ahead : ahead + 1, :] = v[0:1]
    car[...] = brow_ref[...].astype(F32)

    def conv(s, acc):
        branch = car[rows8(s), :]
        out = zero
        new = []
        for k in range(taps):
            v = cgrad[rows8(s + k), :]
            out = out + chan_ref[k : k + 1, :] * v
            new.append(acc[k] + v * branch)
            if k == 0:
                new_bias = acc[taps] + v
        strided_store(gout, s, steps, out)
        return (*new, new_bias)

    acc = lax.fori_loop(0, steps, conv, (zero,) * (taps + 1), unroll=4)
    for n in range(width // LANES):
        pgrad_ref[:, n * LANES : (n + 1) * LANES] = gout[n].astype(BF16)
    for n, v in enumerate((*acc, sum_r, sum_i, sum_d)):
        sums[n] += v
        sums_ref[n : n + 1, :] = jnp.sum(sums[n], axis=0, keepdims=True)


def recur_backward(state_grad, saved, chan, gate_w, taps, chunk):
    total, width = state_grad.shape
    head = gate_w.shape[2]
    heads = width // head
    chunks = total // chunk
    rows = lambda j, c: (chunks - 1 - c, j)
    blk = pl.BlockSpec((chunk, head), rows)
    work = pltpu.VMEM((chunk, head), F32)
    gws = pl.BlockSpec((2, 1, head, head), lambda j, c: (0, j, 0, 0))
    groups = head // LANES
    n_sums = -(-(taps + 4) // SUB) * SUB
    return pl.pallas_call(
        functools.partial(backward_kernel, taps=taps),
        grid=(heads, chunks),
        in_specs=[blk] * 8
        + [
            pl.BlockSpec((SUB, head), rows),
            pl.BlockSpec((chan.shape[0], head), lambda j, c: (0, j)),
            gws,
        ],
        out_specs=[
            blk,
            gws,
            pl.BlockSpec((n_sums, head), lambda j, c: (0, j)),
        ],
        out_shape=[
            jax.ShapeDtypeStruct((total, width), BF16),
            jax.ShapeDtypeStruct((2, heads, head, head), F32),
            jax.ShapeDtypeStruct((n_sums, width), F32),
        ],
        scratch_shapes=[
            work,
            work,
            pltpu.VMEM((chunk + (taps - 1) * SUB, head), F32),
            work,
            pltpu.VMEM((groups, chunk, LANES), F32),
            pltpu.VMEM((2, chunk, head), F32),
            pltpu.VMEM((taps + 4, SUB, head), F32),
            pltpu.VMEM((SUB, head), F32),
            pltpu.VMEM((SUB, head), F32),
        ],
        compiler_params=pltpu.CompilerParams(
            dimension_semantics=("arbitrary", "arbitrary"), vmem_limit_bytes=60 << 20
        ),
        name="recur_backward",
    )(state_grad, *saved, chan, gate_w)


def split_kernel(table_ref, src, dst, *, half):
    _, rows, width = dst.shape
    n = pl.num_programs(0)
    first = pl.multiple_of(table_ref[pl.program_id(0)], LANES)
    start = pl.multiple_of(table_ref[n], rows)
    dst[0] = src[pl.ds(start, rows), half, pl.ds(first, width)]


def split_columns(weight, half, firsts, head, span, start, rows):
    total, _, lru = weight.shape
    n = len(firsts)
    table = jnp.stack([jnp.int32(f * head) for f in firsts] + [start])
    return pl.pallas_call(
        functools.partial(split_kernel, half=half),
        grid_spec=pltpu.PrefetchScalarGridSpec(
            num_scalar_prefetch=1,
            grid=(n,),
            in_specs=[pl.BlockSpec((total, 2, lru), lambda w, table: (0, 0, 0))],
            out_specs=pl.BlockSpec((1, rows, span * head), lambda w, table: (w, 0, 0)),
        ),
        out_shape=jax.ShapeDtypeStruct((n, rows, span * head), weight.dtype),
        name="split_columns",
    )(table, weight)


def far_kernel(
    normed_ref,
    cot_ref,
    gate_ref,
    up_ref,
    wout_ref,
    own_gate_ref,
    own_up_ref,
    own_out_ref,
    ggate_ref,
    gup_ref,
    gout_ref,
):
    @pl.when(pl.program_id(0) == 0)
    def _():
        ggate_ref[...] = own_gate_ref[...]
        gup_ref[...] = own_up_ref[...]
        gout_ref[...] = own_out_ref[...]

    normed = normed_ref[...]
    cot = cot_ref[...]
    value, slope = gelu_parts(dot(normed, gate_ref[...]))
    up = dot(normed, up_ref[...])
    grad = dot_back(cot, wout_ref[...])
    gout_ref[...] += dot_over((value * up).astype(BF16), cot)
    ggate_ref[...] += dot_over(normed, (grad * up * slope).astype(BF16))
    gup_ref[...] += dot_over(normed, (grad * value).astype(BF16))


def far_grads(normed, cot, weight_in, weight_out, sums, part, parts):
    total, width = normed.shape
    hidden = weight_out.shape[0] // parts
    rows = min(512, total)
    once = pl.Buffered(1)
    data = pl.BlockSpec((rows, width), lambda i: (i, 0))
    cols = lambda i: (0, part)
    lines = lambda i: (part, 0)
    held = pl.BlockSpec((width, hidden), cols, pipeline_mode=once)
    up = pl.BlockSpec((width, hidden), lambda i: (0, parts + part), pipeline_mode=once)
    held_out = pl.BlockSpec((hidden, width), lines, pipeline_mode=once)
    return pl.pallas_call(
        far_kernel,
        grid=(total // rows,),
        in_specs=[data, data, held, up, held_out, held, held, held_out],
        out_specs=[
            pl.BlockSpec((width, hidden), cols),
            pl.BlockSpec((width, hidden), cols),
            pl.BlockSpec((hidden, width), lines),
        ],
        out_shape=[jax.ShapeDtypeStruct(v.shape, F32) for v in sums],
        input_output_aliases={5: 0, 6: 1, 7: 2},
        cost_estimate=pl.CostEstimate(
            flops=12 * total * width * hidden,
            bytes_accessed=4 * total * width + 30 * width * hidden,
            transcendentals=total * hidden,
        ),
        compiler_params=pltpu.CompilerParams(
            dimension_semantics=("arbitrary",), vmem_limit_bytes=60 << 20
        ),
        name="far_grads",
    )(normed, cot, weight_in, weight_in, weight_out, *sums)


def norm_kernel(src, gain, dst):
    rows = src[0].astype(F32)
    inv = lax.rsqrt(jnp.mean(rows * rows, axis=-1, keepdims=True) + 1e-06)
    dst[...] = (rows * inv * gain[...]).astype(BF16)


def norm_packed(packed, gain, size):
    n, _, width = packed.shape
    return pl.pallas_call(
        norm_kernel,
        grid=(n,),
        in_specs=[
            pl.BlockSpec((1, size, width), lambda w: (w, 0, 0)),
            pl.BlockSpec((1, width), lambda w: (0, 0)),
        ],
        out_specs=pl.BlockSpec((size, width), lambda w: (w, 0)),
        out_shape=jax.ShapeDtypeStruct((n * size, width), BF16),
        name="norm_packed",
    )(packed, gain)


def join_kernel(first, second, joined):
    joined[:, 0, :] = first[...].astype(F32)
    joined[:, 1, :] = second[...].astype(F32)


def join_halves(first, second):
    total, width = first.shape
    rows = math.gcd(total, 512)
    block = pl.BlockSpec((rows, width), lambda i: (i, 0))
    return pl.pallas_call(
        join_kernel,
        grid=(total // rows,),
        in_specs=[block, block],
        out_specs=pl.BlockSpec((rows, 2, width), lambda i: (i, 0, 0)),
        out_shape=jax.ShapeDtypeStruct((total, 2, width), F32),
        compiler_params=pltpu.CompilerParams(vmem_limit_bytes=60 << 20),
        name="join_halves",
    )(first, second)


def bit_list(n):
    return [1 << i for i in range(n.bit_length() - 1)]


def swap(block, axis, bit):
    return lax.ppermute(block, axis, [(i, i ^ bit) for i in range(lax.axis_size(axis))])


def gather_steps(block):
    n = lax.axis_size("wide")
    links = bit_list(n)[1:]
    half = block.shape[1] // 2
    sides = [block[:, :half], block[:, half:]]
    orders = [links, links[::-1]]
    for m, bits in enumerate(zip(*orders)):
        got = yield [swap(side, "wide", bit) for side, bit in zip(sides, bits)]
        sides = [jnp.stack([s, g], axis=m) for s, g in zip(sides, got)]
    for i, order in enumerate(orders):
        place = sorted(range(len(order)), key=lambda k: -order[k])
        sides[i] = sides[i].transpose(*place, len(order), len(order) + 1)
    return jnp.concatenate(sides, axis=-1).reshape(-1, block.shape[1])


def other_core(rows):
    return swap(rows, "wide", 1)


def scatter_steps(keep, send):
    n = lax.axis_size("wide")
    links = bit_list(n)[1:]
    rows, width = keep.shape[0] // (n // 2), keep.shape[1]
    half = width // 2
    got = yield [other_core(send)]
    held = keep + got[0].astype(F32)
    held = held.reshape((2,) * len(links) + (rows, width))
    sides = [held[..., :half], held[..., half:]]
    axes = [links[::-1], links[::-1]]
    for bits in zip(links, links[::-1]):
        kept, sent = [], []
        for i, bit in enumerate(bits):
            axis = axes[i].index(bit)
            kept.append(lax.index_in_dim(sides[i], 0, axis, keepdims=False))
            part = lax.index_in_dim(sides[i], 1, axis, keepdims=False)
            sent.append(swap(part.astype(BF16), "wide", bit))
            axes[i] = axes[i][:axis] + axes[i][axis + 1 :]
        got = yield sent
        sides = [k + g.astype(F32) for k, g in zip(kept, got)]
    return jnp.concatenate(sides, axis=-1)


def run_steps(steps, arrived=None):
    try:
        while True:
            arrived = steps.send(arrived)
    except StopIteration as end:
        return end.value


def tie(value, *before):
    return lax.optimization_barrier((value, *before))[0]


def line_step(part, stage):
    n = lax.axis_size("seq")
    if n < 2 or n % 2:
        return lax.psum(part, "seq") if stage == 1 else part
    here = lax.axis_index("seq")

    def step(pairs):
        got = lax.ppermute(part, "seq", pairs)
        return got, (part.astype(F32) + got.astype(F32)).astype(BF16)

    middle = n // 2
    if stage == 0:
        for k in range(middle - 1):
            part = step([(k, k + 1), (n - 1 - k, n - 2 - k)])[1]
    elif stage == 1:
        part = step([(middle - 1, middle), (middle, middle - 1)])[1]
    else:
        for k in range(middle - 2, -1, -1):
            got = step([(k + 1, k), (n - 2 - k, n - 1 - k)])[0]
            part = jnp.where((here == k) | (here == n - 1 - k), got, part)
    return part


def sum_small(values, axis):
    n = lax.axis_size(axis)
    if n & (n - 1):
        return lax.psum(values, axis)
    length = values.shape[0]
    padded = jnp.pad(values, (0, -length % (SUB * LANES))).reshape(-1, LANES)
    for bit in bit_list(n):
        padded = padded + swap(padded, axis, bit)
    return padded.reshape(-1)[:length]


def exchange(blocks):
    return lax.all_to_all(blocks, "wide", split_axis=0, concat_axis=0, tiled=True)


def near_place(r, n):
    return 2 * (r % (n // 2)) + r // (n // 2)


def move_kernel(table_ref, src, dst):
    dst[...] = src[...]


def move_rows(rows, near):
    n = lax.axis_size("wide")
    here = lax.axis_index("wide")
    size = rows.shape[0] // n
    table = jnp.stack([here ^ near_place(r, n) for r in range(n)]).astype(jnp.int32)
    device = lambda r, table: (table[r], 0)
    place = lambda r, table: (r, 0)
    block = (size, rows.shape[1])
    return pl.pallas_call(
        move_kernel,
        grid_spec=pltpu.PrefetchScalarGridSpec(
            num_scalar_prefetch=1,
            grid=(n,),
            in_specs=[pl.BlockSpec(block, device if near else place)],
            out_specs=pl.BlockSpec(block, place if near else device),
        ),
        out_shape=jax.ShapeDtypeStruct(rows.shape, rows.dtype),
        name="move_rows",
    )(table, rows)


def to_near(rows):
    return move_rows(rows, True)


def from_near(rows):
    return move_rows(rows, False)


def gather_small(block):
    n = lax.axis_size("wide")
    here = lax.axis_index("wide")
    held = block[None]
    for bit in bit_list(n):
        held = jnp.concatenate([held, swap(held, "wide", bit)])
    return jnp.concatenate(
        [lax.dynamic_slice_in_dim(held, here ^ w, 1) for w in range(n)]
    )


def norm_rows(rows):
    inv = lax.rsqrt(jnp.mean(rows * rows, axis=-1, keepdims=True) + 1e-06)
    return inv, rows * inv


def norm_back(grad, gain, inv, unit):
    scaled = grad * gain
    return inv * (scaled - unit * jnp.mean(scaled * unit, axis=-1, keepdims=True))


def feed_forward_back(gate_up, cot, weight_out):
    hidden_width = weight_out.shape[0]
    gate, up = gate_up[:, :hidden_width], gate_up[:, hidden_width:]
    value, slope = gelu_parts(gate)
    hidden_grad = dot_back(cot, weight_out)
    hidden = (value * up).astype(BF16)
    gate_up_grad = jnp.concatenate(
        [
            (hidden_grad * up * slope).astype(BF16),
            (hidden_grad * value).astype(BF16),
        ],
        axis=1,
    )
    return hidden, gate_up_grad


def feed_forward(normed, cot, weight_in, weight_out):
    return feed_forward_back(dot(normed, weight_in), cot, weight_out)


def shards(
    tokens,
    cotangent,
    norm_gains,
    in_weight,
    conv_weight,
    conv_bias,
    gate_weights,
    gate_biases,
    decay_param,
    out_weight,
    mlp_in_weight,
    mlp_out_weight,
):
    n_wide, n_seq = lax.axis_size("wide"), lax.axis_size("seq")
    here = lax.axis_index("wide")
    tok_low, cot_low = tokens[0], cotangent[0]
    size, width = tok_low.shape
    own = out_weight.shape[0]
    lru = own * n_wide
    heads, head = gate_weights.shape[1:3]
    taps = conv_weight.shape[0]
    gain_own = norm_gains.shape[1]
    hidden_units = mlp_out_weight.shape[0]
    part = head // n_wide

    span = max(
        ((w + 1) * own - 1) // head - w * own // head + 1 for w in range(n_wide)
    )
    firsts = [min(w * own // head, heads - span) for w in range(n_wide)]
    win = span * head
    start = jnp.minimum(here * own // head, heads - span) * head
    offset = here * own - start

    total = size * n_wide
    half = total // 2
    recompute = n_seq * total <= 8192 and n_seq & (n_seq - 1) == 0 and n_seq > 1

    def far_rows(rows):
        return [swap(rows, "seq", d) for d in range(1, n_seq)] if recompute else []

    def far_gather(rows):
        return lax.all_gather(jnp.concatenate(rows), "wide", axis=0, tiled=True)

    small = jnp.concatenate(
        [
            norm_gains.reshape(-1),
            conv_weight.reshape(-1),
            conv_bias,
            gate_biases.reshape(-1),
            decay_param,
        ]
    )
    n_small = small.shape[0]
    small = jnp.pad(small, (0, -n_small % (16 * width))).reshape(-1, width)
    gate_rows = heads * part * head // width
    packed = jnp.concatenate(
        [
            tok_low,
            small,
            gate_weights.transpose(0, 1, 3, 2).reshape(2 * gate_rows, width),
        ]
    )
    got = lax.all_gather(packed, "wide")
    gates_all = got[:, -2 * gate_rows :].reshape(n_wide, 2, gate_rows, width)
    gate_rows = gate_rows // heads
    small = got[:, size : -2 * heads * gate_rows].reshape(n_wide, -1)[:, :n_small]

    own_rows = in_weight.shape[0]
    shared = n_seq % 2 == 0 and own_rows % 32 == 0
    row_part = own_rows // 2 if shared else own_rows
    odd = lax.axis_index("seq") % 2

    def fetch(half):
        begin = (odd * row_part if shared else odd * 0).astype(jnp.int32)
        return split_columns(in_weight, half, firsts, head, span, begin, row_part)

    def share(rows):
        return swap(rows, "seq", 1) if shared else ()

    def whole(rows, other):
        if shared:
            even = jnp.where(odd == 0, rows, other)
            rows = jnp.stack([even, jnp.where(odd == 0, other, rows)], axis=1)
        return rows.reshape(width, win)

    branch_mine = exchange(fetch(0))
    gate_mine = exchange(fetch(1))
    branch_other, gate_other = share(branch_mine), share(gate_mine)
    in_branch = whole(branch_mine, branch_other)
    gains = (
        small[:, : 2 * gain_own]
        .reshape(n_wide, 2, gain_own)
        .transpose(1, 0, 2)
        .reshape(2, width)
        .astype(F32)
    )
    channels = (
        small[:, 2 * gain_own :]
        .reshape(n_wide, taps + 4, own)
        .transpose(1, 0, 2)
        .reshape(taps + 4, lru)
    )
    channels = lax.dynamic_slice_in_dim(channels, start, win, axis=1).astype(F32)
    chan = jnp.concatenate(
        [channels[: taps + 3], -8.0 * jax.nn.softplus(-channels[taps + 3 :])]
    )
    normed_all = norm_packed(got, gains[:1], size)
    out_own = lax.dynamic_update_slice_in_dim(
        jnp.zeros((win, width), BF16), out_weight, offset, 0
    )
    mlp_in = mlp_in_weight.reshape(width, -1)

    in_branch, normed_all, chan, gains, out_own, mlp_in, gate_mine, gate_other = (
        lax.optimization_barrier(
            (in_branch, normed_all, chan, gains, out_own, mlp_in, gate_mine, gate_other)
        )
    )

    in_gate = whole(gate_mine, gate_other)

    below = max(w * own - f * head for w, f in enumerate(firsts))
    above = max(f * head + win - (w + 1) * own for w, f in enumerate(firsts))
    if max(below, above) <= own:
        around = [
            lax.ppermute(
                out_weight[own - below :],
                "wide",
                [(i, i + 1) for i in range(n_wide - 1)],
            ),
            out_weight,
            lax.ppermute(
                out_weight[:above], "wide", [(i + 1, i) for i in range(n_wide - 1)]
            ),
        ]
        first_row = below - offset
    else:
        around = [lax.all_gather(out_weight, "wide", axis=0, tiled=True)]
        first_row = start
    cot_sent = far_rows(cot_low)
    cot_all = lax.all_gather(tie(cot_low, in_branch), "wide", axis=0, tiled=True)
    gate_w = (
        lax.dynamic_slice_in_dim(
            gates_all, start // head * gate_rows, span * gate_rows, axis=2
        )
        .reshape(n_wide, 2, span, part, head)
        .transpose(1, 2, 0, 3, 4)
        .reshape(2, span, head, head)
    )
    chunk = min(total, 512)
    states, *saved, enter = recur_forward(
        dot(normed_all, in_branch), chan, gate_w, taps, chunk
    )
    in_gate, states, around = lax.optimization_barrier((in_gate, states, around))
    mixed, gate_rows = mix_forward(dot(normed_all, in_gate), states, head, chunk)
    mixed_near = to_near(mixed)
    out_send = dot(mixed_near[half:], out_own).astype(BF16)
    out_send, mixed_near, cot_all = lax.optimization_barrier(
        (out_send, mixed_near, cot_all)
    )
    rows = tok_low.astype(F32)
    steps = scatter_steps(dot(mixed_near[:half], out_own), out_send)
    way = lax.optimization_barrier(steps.send(None))
    way = steps.send(way)
    in_own = jnp.concatenate(
        [
            lax.dynamic_slice_in_dim(weight, offset, own, axis=1)
            for weight in (in_branch, in_gate)
        ],
        axis=1,
    )
    out_win = lax.dynamic_slice_in_dim(jnp.concatenate(around), first_row, win)
    way, in_own, out_win = lax.optimization_barrier((way, in_own, out_win))
    middle = rows + run_steps(steps, way)
    inv_two, unit_two = norm_rows(middle)
    normed_two = (unit_two * gains[1]).astype(BF16)
    middle, normed_two, inv_two, unit_two, cot_all = lax.optimization_barrier(
        (middle, normed_two, inv_two, unit_two, cot_all)
    )

    steps = gather_steps(normed_two)
    way = steps.send(None)
    sent = far_rows(normed_two)
    cot_near = to_near(cot_all)
    way, cot_near, cot_sent = lax.optimization_barrier((way, cot_near, cot_sent))
    normed_even = run_steps(steps, way)
    normed_even, cot_sent = lax.optimization_barrier((normed_even, cot_sent))
    cot_far = far_gather(cot_sent) if recompute else ()
    normed_near = jnp.concatenate([normed_even, other_core(normed_even)])
    hidden, gate_up_grad = feed_forward(normed_near, cot_near, mlp_in, mlp_out_weight)
    up_send = dot_back(gate_up_grad[half:], mlp_in).astype(BF16)
    (
        up_send,
        hidden,
        gate_up_grad,
        normed_near,
        sent[:1],
    ) = lax.optimization_barrier(
        (
            up_send,
            hidden,
            gate_up_grad,
            normed_near,
            sent[:1],
        )
    )
    steps = scatter_steps(dot_back(gate_up_grad[:half], mlp_in), up_send)
    way = steps.send(None)
    way, gate_up_grad, hidden = lax.optimization_barrier((way, gate_up_grad, hidden))
    way = steps.send(way)
    gate_sum = dot_over(normed_near, gate_up_grad[:, :hidden_units])
    up_sum = dot_over(normed_near, gate_up_grad[:, hidden_units:])
    way, gate_sum, up_sum, hidden = lax.optimization_barrier(
        (way, gate_sum, up_sum, hidden)
    )
    out_sum = dot_over(hidden, cot_near)
    normed_two_grad = run_steps(steps, way)
    middle_grad = cot_low.astype(F32) + norm_back(
        normed_two_grad, gains[1], inv_two, unit_two
    )
    mix_low = middle_grad.astype(BF16)
    gain_two_grad = jnp.sum(normed_two_grad * unit_two, axis=0)
    middle_grad, mix_low, gain_two_grad, out_sum, hidden, cot_far, sent = (
        lax.optimization_barrier(
            (middle_grad, mix_low, gain_two_grad, out_sum, hidden, cot_far, sent)
        )
    )

    normed_far = far_gather(sent) if recompute else ()
    steps = gather_steps(mix_low)
    way = lax.optimization_barrier(steps.send(None))
    way = steps.send(way)
    feed_send = dot(hidden[half:], mlp_out_weight).astype(BF16)
    feed_keep = dot(hidden[:half], mlp_out_weight)
    way, feed_send, feed_keep = lax.optimization_barrier((way, feed_send, feed_keep))
    mix_even = run_steps(steps, way)
    mix_near = jnp.concatenate([mix_even, other_core(mix_even)])
    mix_near = lax.optimization_barrier(mix_near)
    mixed_grad = from_near(dot_back(mix_near, out_win))
    gate_half, state_grad = gate_backward(mixed_grad, states, gate_rows, head, chunk)
    out_grad = lax.dynamic_slice_in_dim(
        dot_over(mixed_near, mix_near).astype(BF16), offset, own
    )

    def in_part(grad):
        return dot_over(normed_all, grad).astype(BF16).reshape(n_wide, -1, own)

    def in_rows(part):
        return jnp.moveaxis(exchange(part), 0, 1).reshape(-1, lru)

    gate_half = lax.dynamic_slice_in_dim(gate_half, offset, own, axis=1)
    gate_part = in_part(gate_half)
    state_grad, gate_part, out_grad = lax.optimization_barrier(
        (state_grad, gate_part, out_grad)
    )
    gate_rows_grad = in_rows(gate_part)
    out_grad = line_step(out_grad, 0)
    branch_half, gate_grad, sums = recur_backward(
        state_grad, (states, *saved, enter), chan, gate_w, taps, chunk
    )
    branch_half = lax.dynamic_slice_in_dim(branch_half, offset, own, axis=1)
    branch_part = in_part(branch_half)
    branch_half, branch_part, gate_grad, sums, gate_rows_grad, normed_far, out_grad = (
        lax.optimization_barrier(
            (branch_half, branch_part, gate_grad, sums, gate_rows_grad, normed_far, out_grad)
        )
    )
    branch_rows_grad = in_rows(branch_part)
    out_grad = line_step(out_grad, 1)
    gate_rows_grad = line_step(gate_rows_grad, 0)
    own_near = to_near(jnp.concatenate([branch_half, gate_half], axis=1))
    normed_send = dot_back(own_near[half:], in_own).astype(BF16)
    normed_keep = dot_back(own_near[:half], in_own)
    normed_send, normed_keep, branch_rows_grad, normed_far = lax.optimization_barrier(
        (normed_send, normed_keep, branch_rows_grad, normed_far)
    )

    parts = hidden_units // 256 if hidden_units % 256 == 0 else 1
    held = (gate_sum, up_sum, out_sum)
    normed_steps = scatter_steps(normed_keep, normed_send)
    feed_steps = scatter_steps(feed_keep, feed_send)

    def far_part(held, done):
        for p in range(done, parts if done == 2 else min(done + 1, parts)):
            if recompute:
                held = far_grads(
                    normed_far, cot_far, mlp_in, mlp_out_weight, held, p, parts
                )
        return held

    way = normed_steps.send(None)
    gate_grad = exchange(
        gate_grad.astype(BF16)
        .reshape(2, span, n_wide, part, head)
        .transpose(2, 0, 1, 3, 4)
    )
    held = far_part(held, 0)
    way, held, out_grad, gate_rows_grad, gate_grad = lax.optimization_barrier(
        (way, held, out_grad, gate_rows_grad, gate_grad)
    )
    way = normed_steps.send(way)
    out_grad = line_step(out_grad, 2)
    gate_rows_grad = line_step(gate_rows_grad, 1)
    branch_rows_grad = line_step(branch_rows_grad, 0)
    holders = [
        next(w for w, f in enumerate(firsts) if f <= j < f + span) for j in range(heads)
    ]
    gate_grad = jnp.stack(
        [gate_grad[w, :, j - firsts[w]] for j, w in enumerate(holders)], axis=1
    )
    held = far_part(held, 1)
    way, held, out_grad, gate_rows_grad, branch_rows_grad, gate_grad, feed_keep = (
        lax.optimization_barrier(
            (way, held, out_grad, gate_rows_grad, branch_rows_grad, gate_grad, feed_keep)
        )
    )
    normed_grad = run_steps(normed_steps, way)
    inv_one, unit_one = norm_rows(rows)
    input_grad = middle_grad + norm_back(normed_grad, gains[0], inv_one, unit_one)
    gain_one_grad = jnp.sum(normed_grad * unit_one, axis=0)
    feed_way = feed_steps.send(None)
    gate_rows_grad = line_step(gate_rows_grad, 2)
    branch_rows_grad = line_step(branch_rows_grad, 1)
    gate_grad = line_step(gate_grad, 0)
    held = far_part(held, 2)
    feed_way, held, gate_rows_grad, branch_rows_grad, gate_grad, gain_one_grad = (
        lax.optimization_barrier(
            (feed_way, held, gate_rows_grad, branch_rows_grad, gate_grad, gain_one_grad)
        )
    )
    feed = run_steps(feed_steps, feed_way)
    result = (middle + feed).astype(BF16)
    branch_rows_grad = line_step(branch_rows_grad, 2)
    gate_grad = line_step(line_step(gate_grad, 1), 2)
    if recompute:
        mlp_in_grad = join_halves(held[0], held[1])
    else:
        mlp_in_grad = jnp.stack(held[:2], axis=1)
    mlp_out_grad = held[2]
    in_grad = join_halves(branch_rows_grad, gate_rows_grad)
    sums = lax.dynamic_slice_in_dim(sums[: taps + 4], offset, own, axis=1)
    gate_grad = gate_grad.astype(F32).transpose(0, 1, 3, 2)
    out_grad = out_grad.astype(F32)

    gains_grad = sum_small(jnp.concatenate([gain_one_grad, gain_two_grad]), "wide")
    gains_grad = lax.dynamic_slice_in_dim(
        gains_grad.reshape(2, width), here * gain_own, gain_own, axis=1
    )
    small = sum_small(
        jnp.concatenate([gains_grad.reshape(-1), sums.reshape(-1)]), "seq"
    )
    gains_grad = small[: 2 * gain_own].reshape(2, gain_own)
    sums = small[2 * gain_own :].reshape(taps + 4, own)
    decay_grad = sums[taps + 3] * 8.0 * jax.nn.sigmoid(-decay_param.astype(F32))
    if not recompute:
        mlp_out_grad, mlp_in_grad = (
            lax.psum(g.astype(BF16), "seq").astype(F32)
            for g in (mlp_out_grad, mlp_in_grad)
        )
    return (
        result[None],
        input_grad[None],
        gains_grad,
        in_grad,
        sums[:taps],
        sums[taps],
        gate_grad,
        sums[taps + 1 : taps + 3],
        decay_grad,
        out_grad,
        mlp_in_grad,
        mlp_out_grad,
    )


def solution(mesh):
    placed = (
        P("seq", "wide", None),
        P("seq", "wide", None),
        P(None, "wide"),
        P("wide", None, None),
        P(None, "wide"),
        P("wide"),
        P(None, None, None, "wide"),
        P(None, "wide"),
        P("wide"),
        P("wide", None),
        P(None, None, "wide"),
        P("wide", None),
    )
    return jax.shard_map(
        shards,
        mesh=mesh,
        in_specs=placed,
        out_specs=(
            P("seq", "wide", None),
            P("seq", "wide", None),
            P(None, "wide"),
            P("wide", None, None),
            P(None, "wide"),
            P("wide"),
            P(None, None, None, "wide"),
            P(None, "wide"),
            P("wide"),
            P("wide", None),
            P(None, None, "wide"),
            P("wide", None),
        ),
        check_vma=False,
    )
```

```python
import functools
import math
import jax
import jax.numpy as jnp
from jax import lax
from jax.experimental import pallas as pl
from jax.experimental.pallas import tpu as pltpu
from jax.sharding import PartitionSpec as P

BF16 = jnp.bfloat16
F32 = jnp.float32
SUB = 8
LANES = 128
GELU_A = math.sqrt(2.0 / math.pi)
GELU_B = 0.044715


def dot(left, right):
    return jnp.dot(left, right, preferred_element_type=F32)


def dot_over(left, right):
    return lax.dot_general(
        left, right, (((0,), (0,)), ((), ())), preferred_element_type=F32
    )


def dot_back(left, right):
    return lax.dot_general(
        left, right, (((1,), (1,)), ((), ())), preferred_element_type=F32
    )


def gelu_parts(v):
    square = v * v
    th = jnp.tanh(GELU_A * v * (1.0 + GELU_B * square))
    value = 0.5 * v * (1.0 + th)
    slope = 0.5 * (1.0 + th) + 0.5 * v * (1.0 - th * th) * (
        GELU_A * (1.0 + 3.0 * GELU_B * square)
    )
    return value, slope


def minus_expm1(v):
    series = jnp.full_like(v, 1.0 / 40320.0)
    for factorial in (5040.0, 720.0, 120.0, 24.0, 6.0, 2.0, 1.0):
        series = series * v + 1.0 / factorial
    return jnp.where(v > -0.5, -v * series, 1.0 - jnp.exp(v))


def sub_iota(width):
    return lax.broadcasted_iota(jnp.int32, (SUB, width), 0)


def roll_down(v, first):
    return jnp.where(sub_iota(v.shape[1]) == 0, first, pltpu.roll(v, 1, 0))


def roll_up(v, last):
    return jnp.where(sub_iota(v.shape[1]) == SUB - 1, last, pltpu.roll(v, SUB - 1, 0))


def rows8(step):
    return pl.ds(pl.multiple_of(step * SUB, SUB), SUB)


def strided_load(refs, s, steps):
    return jnp.concatenate([r[pl.ds(s, SUB, stride=steps), :] for r in refs], axis=1)


def strided_store(ref, s, steps, v):
    for n in range(ref.shape[0]):
        ref.at[n][pl.ds(s, SUB, stride=steps), :] = v[:, n * LANES : (n + 1) * LANES]


def forward_kernel(*refs, taps, groups):
    forward_body(refs[:groups], *refs[groups:], taps=taps)


def forward_body(
    branch_refs,
    chan_ref,
    gw_ref,
    states_ref,
    decay_ref,
    rgate_ref,
    igate_ref,
    scale_ref,
    low_ref,
    brow_ref,
    enter_ref,
    ext,
    pre0,
    pre1,
    prod,
    tail,
    carry,
    *,
    taps,
):
    rows, width = states_ref.shape
    steps = rows // SUB
    halo = taps - 1

    @pl.when(pl.program_id(1) == 0)
    def _():
        tail[...] = jnp.zeros_like(tail)
        carry[...] = jnp.zeros_like(carry)

    def load(s, _):
        v = strided_load(branch_refs, s, steps).astype(BF16).astype(F32)
        ext[rows8(s + halo), :] = v
        return 0

    lax.fori_loop(0, steps, load, 0, unroll=4)
    for back in range(1, halo + 1):
        v = ext[rows8(halo + steps - back), :]
        ext[rows8(halo - back), :] = roll_down(v, tail[back - 1 : back, :])
        tail[back - 1 : back, :] = v[SUB - 1 : SUB]
    big = 8
    wide = SUB * big

    def block(i):
        return pl.ds(pl.multiple_of(i * wide, wide), wide)

    def conv(i, _):
        out = chan_ref[taps : taps + 1, :]
        for k in range(taps):
            v = ext[pl.ds(pl.multiple_of((i * big + halo - k) * SUB, SUB), wide), :]
            out = out + chan_ref[k : k + 1, :] * v
            if k == 0:
                brow_ref[block(i), :] = v.astype(BF16)
        low_ref[block(i), :] = out.astype(BF16)
        return 0

    lax.fori_loop(0, steps // big, conv, 0)
    low = low_ref[...]
    pre0[...] = dot_back(low, gw_ref[0, 0])
    pre1[...] = dot_back(low, gw_ref[1, 0])

    def gates(i, _):
        r = jax.nn.sigmoid(pre0[block(i), :] + chan_ref[taps + 1 : taps + 2, :])
        g = jax.nn.sigmoid(pre1[block(i), :] + chan_ref[taps + 2 : taps + 3, :])
        log_decay = r * chan_ref[taps + 3 : taps + 4, :]
        scale = jnp.sqrt(minus_expm1(2.0 * log_decay))
        rgate_ref[block(i), :] = r
        igate_ref[block(i), :] = g
        scale_ref[block(i), :] = scale
        decay_ref[block(i), :] = jnp.exp(log_decay)
        pre0[block(i), :] = scale * g * low_ref[block(i), :].astype(F32)
        return 0

    lax.fori_loop(0, steps // big, gates, 0)

    def scan(s, hp):
        h, p = hp
        a = decay_ref[rows8(s), :]
        h = a * h + pre0[rows8(s), :]
        p = a * p
        states_ref[rows8(s), :] = h
        prod[rows8(s), :] = p
        return h, p

    zero = jnp.zeros((SUB, width), F32)
    h, p = lax.fori_loop(0, steps, scan, (zero, zero + 1.0), unroll=8)
    for shift in (1, 2, 4):
        keep = sub_iota(width) >= shift
        h = h + p * jnp.where(keep, pltpu.roll(h, shift, 0), 0.0)
        p = p * jnp.where(keep, pltpu.roll(p, shift, 0), 1.0)
    first = carry[0:1, :]
    ends = h + p * first
    enter = roll_down(ends, first)
    enter_ref[...] = enter
    carry[0:1, :] = ends[SUB - 1 : SUB]

    def finish(s, _):
        states_ref[rows8(s), :] = states_ref[rows8(s), :] + prod[rows8(s), :] * enter
        return 0

    lax.fori_loop(0, steps, finish, 0, unroll=8)


def mix_kernel(*refs, groups):
    states_ref, mixed_ref, gperm_ref, out = refs[groups:]
    rows, width = states_ref.shape
    steps = rows // SUB

    def body(s, _):
        v = strided_load(refs[:groups], s, steps)
        gperm_ref[rows8(s), :] = v
        strided_store(out, s, steps, gelu_parts(v)[0] * states_ref[rows8(s), :])
        return 0

    lax.fori_loop(0, steps, body, 0, unroll=8)
    for n in range(width // LANES):
        mixed_ref[:, n * LANES : (n + 1) * LANES] = out[n].astype(BF16)


def mix_forward(gate_branch, states, head, chunk):
    total, width = states.shape
    groups = head // LANES
    blk = pl.BlockSpec((chunk, head), lambda j, c: (c, j))
    lane = [
        pl.BlockSpec((chunk, LANES), lambda j, c, n=n: (c, j * groups + n))
        for n in range(groups)
    ]
    return pl.pallas_call(
        functools.partial(mix_kernel, groups=groups),
        grid=(width // head, total // chunk),
        in_specs=lane + [blk],
        out_specs=[blk, blk],
        out_shape=[
            jax.ShapeDtypeStruct((total, width), BF16),
            jax.ShapeDtypeStruct((total, width), F32),
        ],
        scratch_shapes=[pltpu.VMEM((groups, chunk, LANES), F32)],
        compiler_params=pltpu.CompilerParams(
            dimension_semantics=("arbitrary", "arbitrary"), vmem_limit_bytes=60 << 20
        ),
        name="mix_forward",
    )(*[gate_branch] * groups, states)


def recur_forward(projected, chan, gate_w, taps, chunk):
    total, width = projected.shape
    head = gate_w.shape[2]
    heads = width // head
    chunks = total // chunk
    rows = lambda j, c: (c, j)
    blk = pl.BlockSpec((chunk, head), rows)
    f32s = jax.ShapeDtypeStruct((total, width), F32)
    b16s = jax.ShapeDtypeStruct((total, width), BF16)
    work = pltpu.VMEM((chunk, head), F32)
    groups = head // LANES
    lane = [
        pl.BlockSpec((chunk, LANES), lambda j, c, n=n: (c, j * groups + n))
        for n in range(groups)
    ]
    return pl.pallas_call(
        functools.partial(forward_kernel, taps=taps, groups=groups),
        grid=(heads, chunks),
        in_specs=[
            *lane,
            pl.BlockSpec((chan.shape[0], head), lambda j, c: (0, j)),
            pl.BlockSpec((2, 1, head, head), lambda j, c: (0, j, 0, 0)),
        ],
        out_specs=[blk] * 7 + [pl.BlockSpec((SUB, head), rows)],
        out_shape=[f32s, f32s, f32s, f32s, f32s, b16s, b16s]
        + [jax.ShapeDtypeStruct((chunks * SUB, width), F32)],
        scratch_shapes=[
            pltpu.VMEM((chunk + (taps - 1) * SUB, head), F32),
            work,
            work,
            work,
            pltpu.VMEM((SUB, head), F32),
            pltpu.VMEM((SUB, head), F32),
        ],
        compiler_params=pltpu.CompilerParams(
            dimension_semantics=("arbitrary", "arbitrary"), vmem_limit_bytes=60 << 20
        ),
        name="recur_forward",
    )(*[projected] * groups, chan, gate_w)


def gate_back_kernel(*refs, groups):
    mgrad_refs = refs[:groups]
    states_ref, gperm_ref, ggrad_ref, sgrad_ref, out = refs[groups:]
    rows, width = states_ref.shape
    steps = rows // SUB

    def body(s, _):
        value, slope = gelu_parts(gperm_ref[rows8(s), :])
        mg = strided_load(mgrad_refs, s, steps)
        strided_store(out, s, steps, mg * states_ref[rows8(s), :] * slope)
        sgrad_ref[rows8(s), :] = mg * value
        return 0

    lax.fori_loop(0, steps, body, 0, unroll=8)
    for n in range(width // LANES):
        ggrad_ref[:, n * LANES : (n + 1) * LANES] = out[n].astype(BF16)


def gate_backward(mixed_grad, states, gate_rows, head, chunk):
    total, width = mixed_grad.shape
    groups = head // LANES
    blk = pl.BlockSpec((chunk, head), lambda j, c: (c, j))
    lane = [
        pl.BlockSpec((chunk, LANES), lambda j, c, n=n: (c, j * groups + n))
        for n in range(groups)
    ]
    return pl.pallas_call(
        functools.partial(gate_back_kernel, groups=groups),
        grid=(width // head, total // chunk),
        in_specs=lane + [blk, blk],
        out_specs=[blk, blk],
        out_shape=[
            jax.ShapeDtypeStruct((total, width), BF16),
            jax.ShapeDtypeStruct((total, width), F32),
        ],
        scratch_shapes=[pltpu.VMEM((groups, chunk, LANES), F32)],
        compiler_params=pltpu.CompilerParams(
            dimension_semantics=("arbitrary", "arbitrary"), vmem_limit_bytes=60 << 20
        ),
        name="gate_backward",
    )(*[mixed_grad] * groups, states, gate_rows)


def backward_kernel(
    sgrad_ref,
    states_ref,
    decay_ref,
    rgate_ref,
    igate_ref,
    scale_ref,
    low_ref,
    brow_ref,
    enter_ref,
    chan_ref,
    gw_ref,
    pgrad_ref,
    gwg_ref,
    sums_ref,
    car,
    prod,
    cgrad,
    lowf,
    gout,
    pre,
    sums,
    tail,
    carry,
    *,
    taps,
):
    rows, width = states_ref.shape
    steps = rows // SUB
    halo = taps - 1

    @pl.when(pl.program_id(1) == 0)
    def _():
        tail[...] = jnp.zeros_like(tail)
        carry[...] = jnp.zeros_like(carry)
        sums[...] = jnp.zeros_like(sums)
        gwg_ref[...] = jnp.zeros_like(gwg_ref)

    def scan(n, uq):
        u, q = uq
        s = steps - 1 - n
        c = sgrad_ref[rows8(s), :] + u
        car[rows8(s), :] = c
        prod[rows8(s), :] = q
        a = decay_ref[rows8(s), :]
        return a * c, a * q

    zero = jnp.zeros((SUB, width), F32)
    u, q = lax.fori_loop(0, steps, scan, (zero, zero + 1.0), unroll=8)
    for shift in (1, 2, 4):
        keep = sub_iota(width) < SUB - shift
        u = u + q * jnp.where(keep, pltpu.roll(u, SUB - shift, 0), 0.0)
        q = q * jnp.where(keep, pltpu.roll(q, SUB - shift, 0), 1.0)
    last = carry[0:1, :]
    ends = u + q * last
    enter = roll_up(ends, last)
    carry[0:1, :] = ends[0:1]
    neg = chan_ref[taps + 3 : taps + 4, :]
    state_in = enter_ref[...]

    def gates(s, acc):
        sum_r, sum_i, sum_d = acc
        c = car[rows8(s), :] + prod[rows8(s), :] * enter
        before = jnp.where(
            s == 0, state_in, states_ref[rows8(jnp.maximum(s - 1, 0)), :]
        )
        a = decay_ref[rows8(s), :]
        r = rgate_ref[rows8(s), :]
        g = igate_ref[rows8(s), :]
        scale = scale_ref[rows8(s), :]
        low = lowf[rows8(s), :]
        c_low = c * low
        dgrad = c * a * before - c_low * g * (a * a) / scale
        pr = dgrad * neg * r * (1.0 - r)
        pi = c_low * scale * g * (1.0 - g)
        pre[0, rows8(s), :] = pr
        pre[1, rows8(s), :] = pi
        cgrad[rows8(s), :] = c * scale * g
        pr = pr.astype(BF16).astype(F32)
        pi = pi.astype(BF16).astype(F32)
        return sum_r + pr, sum_i + pi, sum_d + dgrad * r

    lowf[...] = low_ref[...].astype(F32)
    sum_r, sum_i, sum_d = lax.fori_loop(0, steps, gates, (zero, zero, zero), unroll=4)
    low = low_ref[...]
    pr = pre[0].astype(BF16)
    pi = pre[1].astype(BF16)
    gwg_ref[0, 0] += dot_over(pr, low)
    gwg_ref[1, 0] += dot_over(pi, low)
    cgrad[pl.ds(0, rows), :] = (
        cgrad[pl.ds(0, rows), :] + dot(pr, gw_ref[0, 0]) + dot(pi, gw_ref[1, 0])
    )
    for ahead in range(halo):
        v = cgrad[rows8(ahead), :]
        cgrad[rows8(steps + ahead), :] = roll_up(v, tail[ahead : ahead + 1, :])
        tail[ahead : ahead + 1, :] = v[0:1]
    car[...] = brow_ref[...].astype(F32)

    def conv(s, acc):
        branch = car[rows8(s), :]
        out = zero
        new = []
        for k in range(taps):
            v = cgrad[rows8(s + k), :]
            out = out + chan_ref[k : k + 1, :] * v
            new.append(acc[k] + v * branch)
            if k == 0:
                new_bias = acc[taps] + v
        strided_store(gout, s, steps, out)
        return (*new, new_bias)

    acc = lax.fori_loop(0, steps, conv, (zero,) * (taps + 1), unroll=4)
    for n in range(width // LANES):
        pgrad_ref[:, n * LANES : (n + 1) * LANES] = gout[n].astype(BF16)
    for n, v in enumerate((*acc, sum_r, sum_i, sum_d)):
        sums[n] += v
        sums_ref[n : n + 1, :] = jnp.sum(sums[n], axis=0, keepdims=True)


def recur_backward(state_grad, saved, chan, gate_w, taps, chunk):
    total, width = state_grad.shape
    head = gate_w.shape[2]
    heads = width // head
    chunks = total // chunk
    rows = lambda j, c: (chunks - 1 - c, j)
    blk = pl.BlockSpec((chunk, head), rows)
    work = pltpu.VMEM((chunk, head), F32)
    gws = pl.BlockSpec((2, 1, head, head), lambda j, c: (0, j, 0, 0))
    groups = head // LANES
    n_sums = -(-(taps + 4) // SUB) * SUB
    return pl.pallas_call(
        functools.partial(backward_kernel, taps=taps),
        grid=(heads, chunks),
        in_specs=[blk] * 8
        + [
            pl.BlockSpec((SUB, head), rows),
            pl.BlockSpec((chan.shape[0], head), lambda j, c: (0, j)),
            gws,
        ],
        out_specs=[
            blk,
            gws,
            pl.BlockSpec((n_sums, head), lambda j, c: (0, j)),
        ],
        out_shape=[
            jax.ShapeDtypeStruct((total, width), BF16),
            jax.ShapeDtypeStruct((2, heads, head, head), F32),
            jax.ShapeDtypeStruct((n_sums, width), F32),
        ],
        scratch_shapes=[
            work,
            work,
            pltpu.VMEM((chunk + (taps - 1) * SUB, head), F32),
            work,
            pltpu.VMEM((groups, chunk, LANES), F32),
            pltpu.VMEM((2, chunk, head), F32),
            pltpu.VMEM((taps + 4, SUB, head), F32),
            pltpu.VMEM((SUB, head), F32),
            pltpu.VMEM((SUB, head), F32),
        ],
        compiler_params=pltpu.CompilerParams(
            dimension_semantics=("arbitrary", "arbitrary"), vmem_limit_bytes=60 << 20
        ),
        name="recur_backward",
    )(state_grad, *saved, chan, gate_w)


def split_kernel(table_ref, src, dst, *, half):
    _, rows, width = dst.shape
    n = pl.num_programs(0)
    first = pl.multiple_of(table_ref[pl.program_id(0)], LANES)
    start = pl.multiple_of(table_ref[n], rows)
    dst[0] = src[pl.ds(start, rows), half, pl.ds(first, width)]


def split_columns(weight, half, firsts, head, span, start, rows):
    total, _, lru = weight.shape
    n = len(firsts)
    table = jnp.stack([jnp.int32(f * head) for f in firsts] + [start])
    return pl.pallas_call(
        functools.partial(split_kernel, half=half),
        grid_spec=pltpu.PrefetchScalarGridSpec(
            num_scalar_prefetch=1,
            grid=(n,),
            in_specs=[pl.BlockSpec((total, 2, lru), lambda w, table: (0, 0, 0))],
            out_specs=pl.BlockSpec((1, rows, span * head), lambda w, table: (w, 0, 0)),
        ),
        out_shape=jax.ShapeDtypeStruct((n, rows, span * head), weight.dtype),
        name="split_columns",
    )(table, weight)


def far_kernel(
    normed_ref,
    cot_ref,
    gate_ref,
    up_ref,
    wout_ref,
    own_gate_ref,
    own_up_ref,
    own_out_ref,
    ggate_ref,
    gup_ref,
    gout_ref,
):
    @pl.when(pl.program_id(0) == 0)
    def _():
        ggate_ref[...] = own_gate_ref[...]
        gup_ref[...] = own_up_ref[...]
        gout_ref[...] = own_out_ref[...]

    normed = normed_ref[...]
    cot = cot_ref[...]
    value, slope = gelu_parts(dot(normed, gate_ref[...]))
    up = dot(normed, up_ref[...])
    grad = dot_back(cot, wout_ref[...])
    gout_ref[...] += dot_over((value * up).astype(BF16), cot)
    ggate_ref[...] += dot_over(normed, (grad * up * slope).astype(BF16))
    gup_ref[...] += dot_over(normed, (grad * value).astype(BF16))


def far_grads(normed, cot, weight_in, weight_out, sums, part, parts):
    total, width = normed.shape
    hidden = weight_out.shape[0] // parts
    rows = min(512, total)
    once = pl.Buffered(1)
    data = pl.BlockSpec((rows, width), lambda i: (i, 0))
    cols = lambda i: (0, part)
    lines = lambda i: (part, 0)
    held = pl.BlockSpec((width, hidden), cols, pipeline_mode=once)
    up = pl.BlockSpec((width, hidden), lambda i: (0, parts + part), pipeline_mode=once)
    held_out = pl.BlockSpec((hidden, width), lines, pipeline_mode=once)
    return pl.pallas_call(
        far_kernel,
        grid=(total // rows,),
        in_specs=[data, data, held, up, held_out, held, held, held_out],
        out_specs=[
            pl.BlockSpec((width, hidden), cols),
            pl.BlockSpec((width, hidden), cols),
            pl.BlockSpec((hidden, width), lines),
        ],
        out_shape=[jax.ShapeDtypeStruct(v.shape, F32) for v in sums],
        input_output_aliases={5: 0, 6: 1, 7: 2},
        cost_estimate=pl.CostEstimate(
            flops=1024, bytes_accessed=1024, transcendentals=0
        ),
        compiler_params=pltpu.CompilerParams(
            dimension_semantics=("arbitrary",), vmem_limit_bytes=60 << 20
        ),
        name="far_grads",
    )(normed, cot, weight_in, weight_in, weight_out, *sums)


def norm_kernel(src, gain, dst):
    rows = src[0].astype(F32)
    inv = lax.rsqrt(jnp.mean(rows * rows, axis=-1, keepdims=True) + 1e-06)
    dst[...] = (rows * inv * gain[...]).astype(BF16)


def norm_packed(packed, gain, size):
    n, _, width = packed.shape
    return pl.pallas_call(
        norm_kernel,
        grid=(n,),
        in_specs=[
            pl.BlockSpec((1, size, width), lambda w: (w, 0, 0)),
            pl.BlockSpec((1, width), lambda w: (0, 0)),
        ],
        out_specs=pl.BlockSpec((size, width), lambda w: (w, 0)),
        out_shape=jax.ShapeDtypeStruct((n * size, width), BF16),
        name="norm_packed",
    )(packed, gain)


def join_kernel(first, second, joined):
    joined[:, 0, :] = first[...].astype(F32)
    joined[:, 1, :] = second[...].astype(F32)


def join_halves(first, second):
    total, width = first.shape
    rows = math.gcd(total, 512)
    block = pl.BlockSpec((rows, width), lambda i: (i, 0))
    return pl.pallas_call(
        join_kernel,
        grid=(total // rows,),
        in_specs=[block, block],
        out_specs=pl.BlockSpec((rows, 2, width), lambda i: (i, 0, 0)),
        out_shape=jax.ShapeDtypeStruct((total, 2, width), F32),
        compiler_params=pltpu.CompilerParams(vmem_limit_bytes=60 << 20),
        name="join_halves",
    )(first, second)


def bit_list(n):
    return [1 << i for i in range(n.bit_length() - 1)]


def swap(block, axis, bit):
    return lax.ppermute(block, axis, [(i, i ^ bit) for i in range(lax.axis_size(axis))])


def gather_steps(block):
    n = lax.axis_size("wide")
    links = bit_list(n)[1:]
    half = block.shape[1] // 2
    sides = [block[:, :half], block[:, half:]]
    orders = [links, links[::-1]]
    for m, bits in enumerate(zip(*orders)):
        got = yield [swap(side, "wide", bit) for side, bit in zip(sides, bits)]
        sides = [jnp.stack([s, g], axis=m) for s, g in zip(sides, got)]
    for i, order in enumerate(orders):
        place = sorted(range(len(order)), key=lambda k: -order[k])
        sides[i] = sides[i].transpose(*place, len(order), len(order) + 1)
    return jnp.concatenate(sides, axis=-1).reshape(-1, block.shape[1])


def other_core(rows):
    return swap(rows, "wide", 1)


def scatter_steps(keep, send):
    n = lax.axis_size("wide")
    links = bit_list(n)[1:]
    rows, width = keep.shape[0] // (n // 2), keep.shape[1]
    half = width // 2
    got = yield [other_core(send)]
    held = keep + got[0].astype(F32)
    held = held.reshape((2,) * len(links) + (rows, width))
    sides = [held[..., :half], held[..., half:]]
    axes = [links[::-1], links[::-1]]
    for bits in zip(links, links[::-1]):
        kept, sent = [], []
        for i, bit in enumerate(bits):
            axis = axes[i].index(bit)
            kept.append(lax.index_in_dim(sides[i], 0, axis, keepdims=False))
            part = lax.index_in_dim(sides[i], 1, axis, keepdims=False)
            sent.append(swap(part.astype(BF16), "wide", bit))
            axes[i] = axes[i][:axis] + axes[i][axis + 1 :]
        got = yield sent
        sides = [k + g.astype(F32) for k, g in zip(kept, got)]
    return jnp.concatenate(sides, axis=-1)


def run_steps(steps, arrived=None):
    try:
        while True:
            arrived = steps.send(arrived)
    except StopIteration as end:
        return end.value


def tie(value, *before):
    return lax.optimization_barrier((value, *before))[0]


def line_step(part, stage):
    n = lax.axis_size("seq")
    if n < 2 or n % 2:
        return lax.psum(part, "seq") if stage == 1 else part
    here = lax.axis_index("seq")

    def step(pairs):
        got = lax.ppermute(part, "seq", pairs)
        return got, (part.astype(F32) + got.astype(F32)).astype(BF16)

    middle = n // 2
    if stage == 0:
        for k in range(middle - 1):
            part = step([(k, k + 1), (n - 1 - k, n - 2 - k)])[1]
    elif stage == 1:
        part = step([(middle - 1, middle), (middle, middle - 1)])[1]
    else:
        for k in range(middle - 2, -1, -1):
            got = step([(k + 1, k), (n - 2 - k, n - 1 - k)])[0]
            part = jnp.where((here == k) | (here == n - 1 - k), got, part)
    return part


def sum_small(values, axis):
    n = lax.axis_size(axis)
    if n & (n - 1):
        return lax.psum(values, axis)
    length = values.shape[0]
    padded = jnp.pad(values, (0, -length % (SUB * LANES))).reshape(-1, LANES)
    for bit in bit_list(n):
        padded = padded + swap(padded, axis, bit)
    return padded.reshape(-1)[:length]


def exchange(blocks):
    return lax.all_to_all(blocks, "wide", split_axis=0, concat_axis=0, tiled=True)


def near_place(r, n):
    return 2 * (r % (n // 2)) + r // (n // 2)


def move_kernel(table_ref, src, dst):
    dst[...] = src[...]


def move_rows(rows, near):
    n = lax.axis_size("wide")
    here = lax.axis_index("wide")
    size = rows.shape[0] // n
    table = jnp.stack([here ^ near_place(r, n) for r in range(n)]).astype(jnp.int32)
    device = lambda r, table: (table[r], 0)
    place = lambda r, table: (r, 0)
    block = (size, rows.shape[1])
    return pl.pallas_call(
        move_kernel,
        grid_spec=pltpu.PrefetchScalarGridSpec(
            num_scalar_prefetch=1,
            grid=(n,),
            in_specs=[pl.BlockSpec(block, device if near else place)],
            out_specs=pl.BlockSpec(block, place if near else device),
        ),
        out_shape=jax.ShapeDtypeStruct(rows.shape, rows.dtype),
        name="move_rows",
    )(table, rows)


def to_near(rows):
    return move_rows(rows, True)


def from_near(rows):
    return move_rows(rows, False)


def gather_small(block):
    n = lax.axis_size("wide")
    here = lax.axis_index("wide")
    held = block[None]
    for bit in bit_list(n):
        held = jnp.concatenate([held, swap(held, "wide", bit)])
    return jnp.concatenate(
        [lax.dynamic_slice_in_dim(held, here ^ w, 1) for w in range(n)]
    )


def norm_rows(rows):
    inv = lax.rsqrt(jnp.mean(rows * rows, axis=-1, keepdims=True) + 1e-06)
    return inv, rows * inv


def norm_back(grad, gain, inv, unit):
    scaled = grad * gain
    return inv * (scaled - unit * jnp.mean(scaled * unit, axis=-1, keepdims=True))


def feed_forward_back(gate_up, cot, weight_out):
    hidden_width = weight_out.shape[0]
    gate, up = gate_up[:, :hidden_width], gate_up[:, hidden_width:]
    value, slope = gelu_parts(gate)
    hidden_grad = dot_back(cot, weight_out)
    hidden = (value * up).astype(BF16)
    gate_up_grad = jnp.concatenate(
        [
            (hidden_grad * up * slope).astype(BF16),
            (hidden_grad * value).astype(BF16),
        ],
        axis=1,
    )
    return hidden, gate_up_grad


def feed_forward(normed, cot, weight_in, weight_out):
    return feed_forward_back(dot(normed, weight_in), cot, weight_out)


def shards(
    tokens,
    cotangent,
    norm_gains,
    in_weight,
    conv_weight,
    conv_bias,
    gate_weights,
    gate_biases,
    decay_param,
    out_weight,
    mlp_in_weight,
    mlp_out_weight,
):
    n_wide, n_seq = lax.axis_size("wide"), lax.axis_size("seq")
    here = lax.axis_index("wide")
    tok_low, cot_low = tokens[0], cotangent[0]
    size, width = tok_low.shape
    own = out_weight.shape[0]
    lru = own * n_wide
    heads, head = gate_weights.shape[1:3]
    taps = conv_weight.shape[0]
    gain_own = norm_gains.shape[1]
    hidden_units = mlp_out_weight.shape[0]
    part = head // n_wide

    span = max(
        ((w + 1) * own - 1) // head - w * own // head + 1 for w in range(n_wide)
    )
    firsts = [min(w * own // head, heads - span) for w in range(n_wide)]
    win = span * head
    start = jnp.minimum(here * own // head, heads - span) * head
    offset = here * own - start

    total = size * n_wide
    half = total // 2
    recompute = n_seq * total <= 8192 and n_seq & (n_seq - 1) == 0 and n_seq > 1

    def far_rows(rows):
        return [swap(rows, "seq", d) for d in range(1, n_seq)] if recompute else []

    def far_gather(rows):
        return lax.all_gather(rows, "wide", axis=0, tiled=True)

    small = jnp.concatenate(
        [
            norm_gains.reshape(-1),
            conv_weight.reshape(-1),
            conv_bias,
            gate_biases.reshape(-1),
            decay_param,
        ]
    )
    n_small = small.shape[0]
    small = jnp.pad(small, (0, -n_small % (16 * width))).reshape(-1, width)
    gate_rows = heads * part * head // width
    packed = jnp.concatenate(
        [
            tok_low,
            small,
            gate_weights.transpose(0, 1, 3, 2).reshape(2 * gate_rows, width),
        ]
    )
    got = lax.all_gather(packed, "wide")
    gates_all = got[:, -2 * gate_rows :].reshape(n_wide, 2, gate_rows, width)
    gate_rows = gate_rows // heads
    small = got[:, size : -2 * heads * gate_rows].reshape(n_wide, -1)[:, :n_small]

    own_rows = in_weight.shape[0]
    shared = n_seq % 2 == 0 and own_rows % 32 == 0
    row_part = own_rows // 2 if shared else own_rows
    odd = lax.axis_index("seq") % 2

    def fetch(half):
        begin = (odd * row_part if shared else odd * 0).astype(jnp.int32)
        return split_columns(in_weight, half, firsts, head, span, begin, row_part)

    def share(rows):
        return swap(rows, "seq", 1) if shared else ()

    def whole(rows, other):
        if shared:
            even = jnp.where(odd == 0, rows, other)
            rows = jnp.stack([even, jnp.where(odd == 0, other, rows)], axis=1)
        return rows.reshape(width, win)

    send_branch, send_gate = lax.optimization_barrier((fetch(0), fetch(1)))
    branch_mine = exchange(send_branch)
    gate_mine = exchange(send_gate)
    branch_other, gate_other = share(branch_mine), share(gate_mine)
    in_branch = whole(branch_mine, branch_other)
    gains = (
        small[:, : 2 * gain_own]
        .reshape(n_wide, 2, gain_own)
        .transpose(1, 0, 2)
        .reshape(2, width)
        .astype(F32)
    )
    channels = (
        small[:, 2 * gain_own :]
        .reshape(n_wide, taps + 4, own)
        .transpose(1, 0, 2)
        .reshape(taps + 4, lru)
    )
    channels = lax.dynamic_slice_in_dim(channels, start, win, axis=1).astype(F32)
    chan = jnp.concatenate(
        [channels[: taps + 3], -8.0 * jax.nn.softplus(-channels[taps + 3 :])]
    )
    normed_all = norm_packed(got, gains[:1], size)
    out_own = lax.dynamic_update_slice_in_dim(
        jnp.zeros((win, width), BF16), out_weight, offset, 0
    )
    mlp_in = mlp_in_weight.reshape(width, -1)

    in_branch, normed_all, chan, gains, out_own, mlp_in, gate_mine = (
        lax.optimization_barrier(
            (in_branch, normed_all, chan, gains, out_own, mlp_in, gate_mine)
        )
    )


    below = max(w * own - f * head for w, f in enumerate(firsts))
    above = max(f * head + win - (w + 1) * own for w, f in enumerate(firsts))
    if max(below, above) <= own:
        around = [
            lax.ppermute(
                out_weight[own - below :],
                "wide",
                [(i, i + 1) for i in range(n_wide - 1)],
            ),
            out_weight,
            lax.ppermute(
                out_weight[:above], "wide", [(i + 1, i) for i in range(n_wide - 1)]
            ),
        ]
        first_row = below - offset
    else:
        around = [lax.all_gather(out_weight, "wide", axis=0, tiled=True)]
        first_row = start
    cot_sent = far_rows(cot_low)
    cot_all = lax.all_gather(tie(cot_low, in_branch), "wide", axis=0, tiled=True)
    gate_w = (
        lax.dynamic_slice_in_dim(
            gates_all, start // head * gate_rows, span * gate_rows, axis=2
        )
        .reshape(n_wide, 2, span, part, head)
        .transpose(1, 2, 0, 3, 4)
        .reshape(2, span, head, head)
    )
    chunk = min(total, 512)
    states, *saved, enter = recur_forward(
        dot(normed_all, in_branch), chan, gate_w, taps, chunk
    )
    gate_mine, gate_other, states, around = lax.optimization_barrier(
        (gate_mine, gate_other, states, around)
    )
    in_gate = whole(gate_mine, gate_other)
    mixed, gate_rows = mix_forward(dot(normed_all, in_gate), states, head, chunk)
    mixed_near = to_near(mixed)
    out_send = dot(mixed_near[half:], out_own).astype(BF16)
    out_send, mixed_near, cot_all = lax.optimization_barrier(
        (out_send, mixed_near, cot_all)
    )
    rows = tok_low.astype(F32)
    steps = scatter_steps(dot(mixed_near[:half], out_own), out_send)
    way, in_branch, in_gate, around = lax.optimization_barrier(
        (steps.send(None), in_branch, in_gate, around)
    )
    way = steps.send(way)
    in_own = jnp.concatenate(
        [
            lax.dynamic_slice_in_dim(weight, offset, own, axis=1)
            for weight in (in_branch, in_gate)
        ],
        axis=1,
    )
    out_win = lax.dynamic_slice_in_dim(jnp.concatenate(around), first_row, win)
    way, in_own, out_win = lax.optimization_barrier((way, in_own, out_win))
    middle = rows + run_steps(steps, way)
    inv_two, unit_two = norm_rows(middle)
    normed_two = (unit_two * gains[1]).astype(BF16)
    middle, normed_two, inv_two, unit_two, cot_all = lax.optimization_barrier(
        (middle, normed_two, inv_two, unit_two, cot_all)
    )

    steps = gather_steps(normed_two)
    way = steps.send(None)
    sent = far_rows(normed_two)
    cot_near = to_near(cot_all)
    way, cot_near, cot_sent = lax.optimization_barrier((way, cot_near, cot_sent))
    cot_sent = jnp.concatenate(cot_sent) if recompute else ()
    way, cot_sent = lax.optimization_barrier((steps.send(way), cot_sent))
    normed_even = run_steps(steps, way)
    normed_even, cot_sent = lax.optimization_barrier((normed_even, cot_sent))
    cot_far = far_gather(cot_sent) if recompute else ()
    normed_near = jnp.concatenate([normed_even, other_core(normed_even)])
    hidden, gate_up_grad = feed_forward(normed_near, cot_near, mlp_in, mlp_out_weight)
    up_send = dot_back(gate_up_grad[half:], mlp_in).astype(BF16)
    (
        up_send,
        hidden,
        gate_up_grad,
        normed_near,
        sent[:1],
    ) = lax.optimization_barrier(
        (
            up_send,
            hidden,
            gate_up_grad,
            normed_near,
            sent[:1],
        )
    )
    steps = scatter_steps(dot_back(gate_up_grad[:half], mlp_in), up_send)
    way = steps.send(None)
    way, gate_up_grad, hidden = lax.optimization_barrier((way, gate_up_grad, hidden))
    way = steps.send(way)
    gate_sum = dot_over(normed_near, gate_up_grad[:, :hidden_units])
    up_sum = dot_over(normed_near, gate_up_grad[:, hidden_units:])
    way, gate_sum, up_sum, hidden = lax.optimization_barrier(
        (way, gate_sum, up_sum, hidden)
    )
    out_sum = dot_over(hidden, cot_near)
    normed_two_grad = run_steps(steps, way)
    middle_grad = cot_low.astype(F32) + norm_back(
        normed_two_grad, gains[1], inv_two, unit_two
    )
    mix_low = middle_grad.astype(BF16)
    gain_two_grad = jnp.sum(normed_two_grad * unit_two, axis=0)
    middle_grad, mix_low, gain_two_grad, out_sum, hidden, sent = (
        lax.optimization_barrier(
            (middle_grad, mix_low, gain_two_grad, out_sum, hidden, sent)
        )
    )

    steps = gather_steps(mix_low)
    way, sent = lax.optimization_barrier((steps.send(None), sent))
    way = steps.send(way)
    normed_far = far_gather(jnp.concatenate(sent)) if recompute else ()
    feed_send = dot(hidden[half:], mlp_out_weight).astype(BF16)
    feed_keep = dot(hidden[:half], mlp_out_weight)
    way, feed_send, feed_keep = lax.optimization_barrier((way, feed_send, feed_keep))
    mix_even = run_steps(steps, way)
    mix_near = jnp.concatenate([mix_even, other_core(mix_even)])
    mix_near, cot_far = lax.optimization_barrier((mix_near, cot_far))
    mixed_grad = from_near(dot_back(mix_near, out_win))
    out_grad = lax.dynamic_slice_in_dim(
        dot_over(mixed_near, mix_near).astype(BF16), offset, own
    )
    gate_half, state_grad = gate_backward(mixed_grad, states, gate_rows, head, chunk)
    state_grad, out_grad = lax.optimization_barrier((state_grad, out_grad))
    out_grad = line_step(out_grad, 0)

    def in_part(grad):
        return dot_over(normed_all, grad).astype(BF16).reshape(n_wide, -1, own)

    def in_rows(part):
        return jnp.moveaxis(exchange(part), 0, 1).reshape(-1, lru)

    branch_half, gate_grad, sums = recur_backward(
        state_grad, (states, *saved, enter), chan, gate_w, taps, chunk
    )
    branch_half = lax.dynamic_slice_in_dim(branch_half, offset, own, axis=1)
    branch_part = in_part(branch_half)
    branch_half, branch_part, gate_half, gate_grad, sums = lax.optimization_barrier(
        (branch_half, branch_part, gate_half, gate_grad, sums)
    )
    branch_rows_grad = in_rows(branch_part)
    gate_half = lax.dynamic_slice_in_dim(gate_half, offset, own, axis=1)
    gate_part = in_part(gate_half)
    own_near = to_near(jnp.concatenate([branch_half, gate_half], axis=1))
    normed_send = dot_back(own_near[half:], in_own).astype(BF16)
    (
        branch_rows_grad,
        gate_part,
        own_near,
        normed_send,
        out_grad,
        normed_far,
        gate_grad,
        feed_keep,
    ) = lax.optimization_barrier(
        (
            branch_rows_grad,
            gate_part,
            own_near,
            normed_send,
            out_grad,
            normed_far,
            gate_grad,
            feed_keep,
        )
    )
    branch_rows_grad = lax.psum(branch_rows_grad, "seq")
    gate_rows_grad = in_rows(gate_part)
    out_grad = line_step(out_grad, 1)
    normed_steps = scatter_steps(dot_back(own_near[:half], in_own), normed_send)
    way = normed_steps.send(None)

    parts = hidden_units // 256 if hidden_units % 256 == 0 else 1
    held = (gate_sum, up_sum, out_sum)
    feed_steps = scatter_steps(feed_keep, feed_send)

    def far_part(held, done):
        for p in range(done, parts if done == 2 else min(done + 1, parts)):
            if recompute:
                held = far_grads(
                    normed_far, cot_far, mlp_in, mlp_out_weight, held, p, parts
                )
        return held

    held = far_part(held, 0)
    way, held, gate_rows_grad, out_grad, normed_far, gate_grad, feed_keep = (
        lax.optimization_barrier(
            (way, held, gate_rows_grad, out_grad, normed_far, gate_grad, feed_keep)
        )
    )
    gate_grad = exchange(
        gate_grad.astype(BF16)
        .reshape(2, span, n_wide, part, head)
        .transpose(2, 0, 1, 3, 4)
    )
    out_grad = line_step(out_grad, 2)
    way = normed_steps.send(way)
    feed_way = feed_steps.send(None)
    held = far_part(held, 1)
    way, feed_way, held, gate_grad, out_grad, normed_far = lax.optimization_barrier(
        (way, feed_way, held, gate_grad, out_grad, normed_far)
    )
    holders = [
        next(w for w, f in enumerate(firsts) if f <= j < f + span) for j in range(heads)
    ]
    gate_grad = jnp.stack(
        [gate_grad[w, :, j - firsts[w]] for j, w in enumerate(holders)], axis=1
    )
    out_grad = out_grad.astype(F32)
    way = normed_steps.send(way)
    feed_way = feed_steps.send(feed_way)
    branch_rows_grad, gate_rows_grad, gate_grad, out_grad, normed_far = (
        lax.optimization_barrier(
            (branch_rows_grad, gate_rows_grad, gate_grad, out_grad, normed_far)
        )
    )
    gate_rows_grad, gate_grad = lax.psum((gate_rows_grad, gate_grad), "seq")
    held = far_part(held, 2)
    way, feed_way, held = lax.optimization_barrier((way, feed_way, held))
    normed_grad = run_steps(normed_steps, way)
    inv_one, unit_one = norm_rows(rows)
    input_grad = middle_grad + norm_back(normed_grad, gains[0], inv_one, unit_one)
    gain_one_grad = jnp.sum(normed_grad * unit_one, axis=0)
    feed = run_steps(feed_steps, feed_way)
    result = (middle + feed).astype(BF16)
    if recompute:
        mlp_in_grad = join_halves(held[0], held[1])
    else:
        mlp_in_grad = jnp.stack(held[:2], axis=1)
    mlp_out_grad = held[2]
    in_grad = join_halves(branch_rows_grad, gate_rows_grad)
    sums = lax.dynamic_slice_in_dim(sums[: taps + 4], offset, own, axis=1)
    gate_grad = gate_grad.astype(F32).transpose(0, 1, 3, 2)

    gains_grad = sum_small(jnp.concatenate([gain_one_grad, gain_two_grad]), "wide")
    gains_grad = lax.dynamic_slice_in_dim(
        gains_grad.reshape(2, width), here * gain_own, gain_own, axis=1
    )
    small = sum_small(
        jnp.concatenate([gains_grad.reshape(-1), sums.reshape(-1)]), "seq"
    )
    gains_grad = small[: 2 * gain_own].reshape(2, gain_own)
    sums = small[2 * gain_own :].reshape(taps + 4, own)
    decay_grad = sums[taps + 3] * 8.0 * jax.nn.sigmoid(-decay_param.astype(F32))
    if not recompute:
        mlp_out_grad, mlp_in_grad = (
            lax.psum(g.astype(BF16), "seq").astype(F32)
            for g in (mlp_out_grad, mlp_in_grad)
        )
    return (
        result[None],
        input_grad[None],
        gains_grad,
        in_grad,
        sums[:taps],
        sums[taps],
        gate_grad,
        sums[taps + 1 : taps + 3],
        decay_grad,
        out_grad,
        mlp_in_grad,
        mlp_out_grad,
    )


def solution(mesh):
    placed = (
        P("seq", "wide", None),
        P("seq", "wide", None),
        P(None, "wide"),
        P("wide", None, None),
        P(None, "wide"),
        P("wide"),
        P(None, None, None, "wide"),
        P(None, "wide"),
        P("wide"),
        P("wide", None),
        P(None, None, "wide"),
        P("wide", None),
    )
    return jax.shard_map(
        shards,
        mesh=mesh,
        in_specs=placed,
        out_specs=(
            P("seq", "wide", None),
            P("seq", "wide", None),
            P(None, "wide"),
            P("wide", None, None),
            P(None, "wide"),
            P("wide"),
            P(None, None, None, "wide"),
            P(None, "wide"),
            P("wide"),
            P("wide", None),
            P(None, None, "wide"),
            P("wide", None),
        ),
        check_vma=False,
    )
```

```python
import functools
import math
import jax
import jax.numpy as jnp
from jax import lax
from jax.experimental import pallas as pl
from jax.experimental.pallas import tpu as pltpu
from jax.sharding import PartitionSpec as P

BF16 = jnp.bfloat16
F32 = jnp.float32
SUB = 8
LANES = 128
GELU_A = math.sqrt(2.0 / math.pi)
GELU_B = 0.044715


def dot(left, right):
    return jnp.dot(left, right, preferred_element_type=F32)


def dot_over(left, right):
    return lax.dot_general(
        left, right, (((0,), (0,)), ((), ())), preferred_element_type=F32
    )


def dot_back(left, right):
    return lax.dot_general(
        left, right, (((1,), (1,)), ((), ())), preferred_element_type=F32
    )


def gelu_parts(v):
    square = v * v
    th = jnp.tanh(GELU_A * v * (1.0 + GELU_B * square))
    value = 0.5 * v * (1.0 + th)
    slope = 0.5 * (1.0 + th) + 0.5 * v * (1.0 - th * th) * (
        GELU_A * (1.0 + 3.0 * GELU_B * square)
    )
    return value, slope


def minus_expm1(v):
    series = jnp.full_like(v, 1.0 / 40320.0)
    for factorial in (5040.0, 720.0, 120.0, 24.0, 6.0, 2.0, 1.0):
        series = series * v + 1.0 / factorial
    return jnp.where(v > -0.5, -v * series, 1.0 - jnp.exp(v))


def sub_iota(width):
    return lax.broadcasted_iota(jnp.int32, (SUB, width), 0)


def roll_down(v, first):
    return jnp.where(sub_iota(v.shape[1]) == 0, first, pltpu.roll(v, 1, 0))


def roll_up(v, last):
    return jnp.where(sub_iota(v.shape[1]) == SUB - 1, last, pltpu.roll(v, SUB - 1, 0))


def rows8(step):
    return pl.ds(pl.multiple_of(step * SUB, SUB), SUB)


def strided_load(refs, s, steps):
    return jnp.concatenate([r[pl.ds(s, SUB, stride=steps), :] for r in refs], axis=1)


def strided_store(ref, s, steps, v):
    for n in range(ref.shape[0]):
        ref.at[n][pl.ds(s, SUB, stride=steps), :] = v[:, n * LANES : (n + 1) * LANES]


def forward_kernel(*refs, taps, groups):
    forward_body(refs[:groups], *refs[groups:], taps=taps)


def forward_body(
    branch_refs,
    chan_ref,
    gw_ref,
    states_ref,
    decay_ref,
    rgate_ref,
    igate_ref,
    scale_ref,
    low_ref,
    brow_ref,
    enter_ref,
    ext,
    pre0,
    pre1,
    prod,
    tail,
    carry,
    *,
    taps,
):
    rows, width = states_ref.shape
    steps = rows // SUB
    halo = taps - 1

    @pl.when(pl.program_id(1) == 0)
    def _():
        tail[...] = jnp.zeros_like(tail)
        carry[...] = jnp.zeros_like(carry)

    def load(s, _):
        v = strided_load(branch_refs, s, steps).astype(BF16).astype(F32)
        ext[rows8(s + halo), :] = v
        return 0

    lax.fori_loop(0, steps, load, 0, unroll=4)
    for back in range(1, halo + 1):
        v = ext[rows8(halo + steps - back), :]
        ext[rows8(halo - back), :] = roll_down(v, tail[back - 1 : back, :])
        tail[back - 1 : back, :] = v[SUB - 1 : SUB]
    big = 8
    wide = SUB * big

    def block(i):
        return pl.ds(pl.multiple_of(i * wide, wide), wide)

    def conv(i, _):
        out = chan_ref[taps : taps + 1, :]
        for k in range(taps):
            v = ext[pl.ds(pl.multiple_of((i * big + halo - k) * SUB, SUB), wide), :]
            out = out + chan_ref[k : k + 1, :] * v
            if k == 0:
                brow_ref[block(i), :] = v.astype(BF16)
        low_ref[block(i), :] = out.astype(BF16)
        return 0

    lax.fori_loop(0, steps // big, conv, 0)
    low = low_ref[...]
    pre0[...] = dot_back(low, gw_ref[0, 0])
    pre1[...] = dot_back(low, gw_ref[1, 0])

    def gates(i, _):
        r = jax.nn.sigmoid(pre0[block(i), :] + chan_ref[taps + 1 : taps + 2, :])
        g = jax.nn.sigmoid(pre1[block(i), :] + chan_ref[taps + 2 : taps + 3, :])
        log_decay = r * chan_ref[taps + 3 : taps + 4, :]
        scale = jnp.sqrt(minus_expm1(2.0 * log_decay))
        rgate_ref[block(i), :] = r
        igate_ref[block(i), :] = g
        scale_ref[block(i), :] = scale
        decay_ref[block(i), :] = jnp.exp(log_decay)
        pre0[block(i), :] = scale * g * low_ref[block(i), :].astype(F32)
        return 0

    lax.fori_loop(0, steps // big, gates, 0)

    def scan(s, hp):
        h, p = hp
        a = decay_ref[rows8(s), :]
        h = a * h + pre0[rows8(s), :]
        p = a * p
        states_ref[rows8(s), :] = h
        prod[rows8(s), :] = p
        return h, p

    zero = jnp.zeros((SUB, width), F32)
    h, p = lax.fori_loop(0, steps, scan, (zero, zero + 1.0), unroll=8)
    for shift in (1, 2, 4):
        keep = sub_iota(width) >= shift
        h = h + p * jnp.where(keep, pltpu.roll(h, shift, 0), 0.0)
        p = p * jnp.where(keep, pltpu.roll(p, shift, 0), 1.0)
    first = carry[0:1, :]
    ends = h + p * first
    enter = roll_down(ends, first)
    enter_ref[...] = enter
    carry[0:1, :] = ends[SUB - 1 : SUB]

    def finish(s, _):
        states_ref[rows8(s), :] = states_ref[rows8(s), :] + prod[rows8(s), :] * enter
        return 0

    lax.fori_loop(0, steps, finish, 0, unroll=8)


def near_index(device, n):
    bits = lax.axis_index("wide") ^ device
    return (bits >> 1) + (bits & 1) * (n // 2)


def mix_kernel(*refs, groups, n, size):
    states_ref, mixed_ref, gperm_ref, out, stage, sems = refs[groups:]
    rows, width = states_ref.shape
    steps = rows // SUB
    head, chunk = pl.program_id(0), pl.program_id(1)
    chunks = pl.num_programs(1)
    step = head * chunks + chunk
    last = pl.num_programs(0) * chunks - 1
    slot = step % 2

    def copies(slot):
        made = []
        for k in range(rows // size):
            place = near_index(chunk * (rows // size) + k, n)
            made.append(
                pltpu.make_async_copy(
                    stage.at[slot, pl.ds(k * size, size)],
                    mixed_ref.at[
                        pl.ds(pl.multiple_of(place * size, size), size),
                        pl.ds(pl.multiple_of(head * width, width), width),
                    ],
                    sems.at[slot, k],
                )
            )
        return made

    def body(s, _):
        v = strided_load(refs[:groups], s, steps)
        gperm_ref[rows8(s), :] = v
        strided_store(out, s, steps, gelu_parts(v)[0] * states_ref[rows8(s), :])
        return 0

    lax.fori_loop(0, steps, body, 0, unroll=8)

    @pl.when(step >= 2)
    def _():
        for copy in copies(slot):
            copy.wait()

    for g in range(width // LANES):
        stage[slot, :, g * LANES : (g + 1) * LANES] = out[g].astype(BF16)
    for copy in copies(slot):
        copy.start()

    @pl.when(step == last)
    def _():
        for copy in copies(slot):
            copy.wait()

    @pl.when((step == last) & (step >= 1))
    def _():
        for copy in copies(1 - slot):
            copy.wait()


def mix_forward(gate_branch, states, head, chunk, size):
    total, width = states.shape
    groups = head // LANES
    blk = pl.BlockSpec((chunk, head), lambda j, c: (c, j))
    lane = [
        pl.BlockSpec((chunk, LANES), lambda j, c, n=n: (c, j * groups + n))
        for n in range(groups)
    ]
    return pl.pallas_call(
        functools.partial(
            mix_kernel, groups=groups, n=lax.axis_size("wide"), size=size
        ),
        grid=(width // head, total // chunk),
        in_specs=lane + [blk],
        out_specs=[pl.BlockSpec(memory_space=pl.ANY), blk],
        out_shape=[
            jax.ShapeDtypeStruct((total, width), BF16),
            jax.ShapeDtypeStruct((total, width), F32),
        ],
        scratch_shapes=[
            pltpu.VMEM((groups, chunk, LANES), F32),
            pltpu.VMEM((2, chunk, head), BF16),
            pltpu.SemaphoreType.DMA((2, chunk // size)),
        ],
        compiler_params=pltpu.CompilerParams(
            dimension_semantics=("arbitrary", "arbitrary"), vmem_limit_bytes=60 << 20
        ),
        name="mix_forward",
    )(*[gate_branch] * groups, states)


def recur_forward(projected, chan, gate_w, taps, chunk):
    total, width = projected.shape
    head = gate_w.shape[2]
    heads = width // head
    chunks = total // chunk
    rows = lambda j, c: (c, j)
    blk = pl.BlockSpec((chunk, head), rows)
    f32s = jax.ShapeDtypeStruct((total, width), F32)
    b16s = jax.ShapeDtypeStruct((total, width), BF16)
    work = pltpu.VMEM((chunk, head), F32)
    groups = head // LANES
    lane = [
        pl.BlockSpec((chunk, LANES), lambda j, c, n=n: (c, j * groups + n))
        for n in range(groups)
    ]
    return pl.pallas_call(
        functools.partial(forward_kernel, taps=taps, groups=groups),
        grid=(heads, chunks),
        in_specs=[
            *lane,
            pl.BlockSpec((chan.shape[0], head), lambda j, c: (0, j)),
            pl.BlockSpec((2, 1, head, head), lambda j, c: (0, j, 0, 0)),
        ],
        out_specs=[blk] * 7 + [pl.BlockSpec((SUB, head), rows)],
        out_shape=[f32s, f32s, f32s, f32s, f32s, b16s, b16s]
        + [jax.ShapeDtypeStruct((chunks * SUB, width), F32)],
        scratch_shapes=[
            pltpu.VMEM((chunk + (taps - 1) * SUB, head), F32),
            work,
            work,
            work,
            pltpu.VMEM((SUB, head), F32),
            pltpu.VMEM((SUB, head), F32),
        ],
        compiler_params=pltpu.CompilerParams(
            dimension_semantics=("arbitrary", "arbitrary"), vmem_limit_bytes=60 << 20
        ),
        name="recur_forward",
    )(*[projected] * groups, chan, gate_w)


def gate_back_kernel(
    mgrad_ref, states_ref, gperm_ref, ggrad_ref, sgrad_ref, out, near, sems, *, n, size
):
    rows, width = states_ref.shape
    steps = rows // SUB
    groups = width // LANES
    chunks = pl.num_programs(1)
    step = pl.program_id(0) * chunks + pl.program_id(1)
    last = pl.num_programs(0) * chunks - 1
    slot = step % 2

    def copies(step, slot):
        made = []
        for k in range(rows // size):
            place = near_index(step % chunks * (rows // size) + k, n)
            for g in range(groups):
                lane = step // chunks * width + g * LANES
                made.append(
                    pltpu.make_async_copy(
                        mgrad_ref.at[
                            pl.ds(pl.multiple_of(place * size, size), size),
                            pl.ds(pl.multiple_of(lane, LANES), LANES),
                        ],
                        near.at[slot, g, pl.ds(k * size, size)],
                        sems.at[slot, k, g],
                    )
                )
        return made

    @pl.when(step == 0)
    def _():
        for copy in copies(step, slot):
            copy.start()

    @pl.when(step < last)
    def _():
        for copy in copies(step + 1, 1 - slot):
            copy.start()

    for copy in copies(step, slot):
        copy.wait()

    def body(s, _):
        value, slope = gelu_parts(gperm_ref[rows8(s), :])
        mg = strided_load([near.at[slot, g] for g in range(groups)], s, steps)
        strided_store(out, s, steps, mg * states_ref[rows8(s), :] * slope)
        sgrad_ref[rows8(s), :] = mg * value
        return 0

    lax.fori_loop(0, steps, body, 0, unroll=8)
    for g in range(groups):
        ggrad_ref[:, g * LANES : (g + 1) * LANES] = out[g].astype(BF16)


def gate_backward(mixed_grad, states, gate_rows, head, chunk, size):
    total, width = mixed_grad.shape
    groups = head // LANES
    blk = pl.BlockSpec((chunk, head), lambda j, c: (c, j))
    return pl.pallas_call(
        functools.partial(gate_back_kernel, n=lax.axis_size("wide"), size=size),
        grid=(width // head, total // chunk),
        in_specs=[pl.BlockSpec(memory_space=pl.ANY), blk, blk],
        out_specs=[blk, blk],
        out_shape=[
            jax.ShapeDtypeStruct((total, width), BF16),
            jax.ShapeDtypeStruct((total, width), F32),
        ],
        scratch_shapes=[
            pltpu.VMEM((groups, chunk, LANES), F32),
            pltpu.VMEM((2, groups, chunk, LANES), F32),
            pltpu.SemaphoreType.DMA((2, chunk // size, groups)),
        ],
        compiler_params=pltpu.CompilerParams(
            dimension_semantics=("arbitrary", "arbitrary"), vmem_limit_bytes=60 << 20
        ),
        name="gate_backward",
    )(mixed_grad, states, gate_rows)


def backward_kernel(
    sgrad_ref,
    states_ref,
    decay_ref,
    rgate_ref,
    igate_ref,
    scale_ref,
    low_ref,
    brow_ref,
    enter_ref,
    chan_ref,
    gw_ref,
    pgrad_ref,
    gwg_ref,
    sums_ref,
    car,
    prod,
    cgrad,
    lowf,
    gout,
    pre,
    sums,
    tail,
    carry,
    *,
    taps,
):
    rows, width = states_ref.shape
    steps = rows // SUB
    halo = taps - 1

    @pl.when(pl.program_id(1) == 0)
    def _():
        tail[...] = jnp.zeros_like(tail)
        carry[...] = jnp.zeros_like(carry)
        sums[...] = jnp.zeros_like(sums)
        gwg_ref[...] = jnp.zeros_like(gwg_ref)

    def scan(n, uq):
        u, q = uq
        s = steps - 1 - n
        c = sgrad_ref[rows8(s), :] + u
        car[rows8(s), :] = c
        prod[rows8(s), :] = q
        a = decay_ref[rows8(s), :]
        return a * c, a * q

    zero = jnp.zeros((SUB, width), F32)
    u, q = lax.fori_loop(0, steps, scan, (zero, zero + 1.0), unroll=8)
    for shift in (1, 2, 4):
        keep = sub_iota(width) < SUB - shift
        u = u + q * jnp.where(keep, pltpu.roll(u, SUB - shift, 0), 0.0)
        q = q * jnp.where(keep, pltpu.roll(q, SUB - shift, 0), 1.0)
    last = carry[0:1, :]
    ends = u + q * last
    enter = roll_up(ends, last)
    carry[0:1, :] = ends[0:1]
    neg = chan_ref[taps + 3 : taps + 4, :]
    state_in = enter_ref[...]

    def gates(s, acc):
        sum_r, sum_i, sum_d = acc
        c = car[rows8(s), :] + prod[rows8(s), :] * enter
        before = jnp.where(
            s == 0, state_in, states_ref[rows8(jnp.maximum(s - 1, 0)), :]
        )
        a = decay_ref[rows8(s), :]
        r = rgate_ref[rows8(s), :]
        g = igate_ref[rows8(s), :]
        scale = scale_ref[rows8(s), :]
        low = lowf[rows8(s), :]
        c_low = c * low
        dgrad = c * a * before - c_low * g * (a * a) / scale
        pr = dgrad * neg * r * (1.0 - r)
        pi = c_low * scale * g * (1.0 - g)
        pre[0, rows8(s), :] = pr
        pre[1, rows8(s), :] = pi
        cgrad[rows8(s), :] = c * scale * g
        pr = pr.astype(BF16).astype(F32)
        pi = pi.astype(BF16).astype(F32)
        return sum_r + pr, sum_i + pi, sum_d + dgrad * r

    lowf[...] = low_ref[...].astype(F32)
    sum_r, sum_i, sum_d = lax.fori_loop(0, steps, gates, (zero, zero, zero), unroll=4)
    low = low_ref[...]
    pr = pre[0].astype(BF16)
    pi = pre[1].astype(BF16)
    gwg_ref[0, 0] += dot_over(pr, low)
    gwg_ref[1, 0] += dot_over(pi, low)
    cgrad[pl.ds(0, rows), :] = (
        cgrad[pl.ds(0, rows), :] + dot(pr, gw_ref[0, 0]) + dot(pi, gw_ref[1, 0])
    )
    for ahead in range(halo):
        v = cgrad[rows8(ahead), :]
        cgrad[rows8(steps + ahead), :] = roll_up(v, tail[ahead : ahead + 1, :])
        tail[ahead : ahead + 1, :] = v[0:1]
    car[...] = brow_ref[...].astype(F32)

    def conv(s, acc):
        branch = car[rows8(s), :]
        out = zero
        new = []
        for k in range(taps):
            v = cgrad[rows8(s + k), :]
            out = out + chan_ref[k : k + 1, :] * v
            new.append(acc[k] + v * branch)
            if k == 0:
                new_bias = acc[taps] + v
        strided_store(gout, s, steps, out)
        return (*new, new_bias)

    acc = lax.fori_loop(0, steps, conv, (zero,) * (taps + 1), unroll=4)
    for n in range(width // LANES):
        pgrad_ref[:, n * LANES : (n + 1) * LANES] = gout[n].astype(BF16)
    for n, v in enumerate((*acc, sum_r, sum_i, sum_d)):
        sums[n] += v
        sums_ref[n : n + 1, :] = jnp.sum(sums[n], axis=0, keepdims=True)


def recur_backward(state_grad, saved, chan, gate_w, taps, chunk):
    total, width = state_grad.shape
    head = gate_w.shape[2]
    heads = width // head
    chunks = total // chunk
    rows = lambda j, c: (chunks - 1 - c, j)
    blk = pl.BlockSpec((chunk, head), rows)
    work = pltpu.VMEM((chunk, head), F32)
    gws = pl.BlockSpec((2, 1, head, head), lambda j, c: (0, j, 0, 0))
    groups = head // LANES
    n_sums = -(-(taps + 4) // SUB) * SUB
    return pl.pallas_call(
        functools.partial(backward_kernel, taps=taps),
        grid=(heads, chunks),
        in_specs=[blk] * 8
        + [
            pl.BlockSpec((SUB, head), rows),
            pl.BlockSpec((chan.shape[0], head), lambda j, c: (0, j)),
            gws,
        ],
        out_specs=[
            blk,
            gws,
            pl.BlockSpec((n_sums, head), lambda j, c: (0, j)),
        ],
        out_shape=[
            jax.ShapeDtypeStruct((total, width), BF16),
            jax.ShapeDtypeStruct((2, heads, head, head), F32),
            jax.ShapeDtypeStruct((n_sums, width), F32),
        ],
        scratch_shapes=[
            work,
            work,
            pltpu.VMEM((chunk + (taps - 1) * SUB, head), F32),
            work,
            pltpu.VMEM((groups, chunk, LANES), F32),
            pltpu.VMEM((2, chunk, head), F32),
            pltpu.VMEM((taps + 4, SUB, head), F32),
            pltpu.VMEM((SUB, head), F32),
            pltpu.VMEM((SUB, head), F32),
        ],
        compiler_params=pltpu.CompilerParams(
            dimension_semantics=("arbitrary", "arbitrary"), vmem_limit_bytes=60 << 20
        ),
        name="recur_backward",
    )(state_grad, *saved, chan, gate_w)


def split_kernel(table_ref, src, dst, *, half):
    _, rows, width = dst.shape
    n = pl.num_programs(0)
    first = pl.multiple_of(table_ref[pl.program_id(0)], LANES)
    start = pl.multiple_of(table_ref[n], rows)
    dst[0] = src[pl.ds(start, rows), half, pl.ds(first, width)]


def split_columns(weight, half, firsts, head, span, start, rows):
    total, _, lru = weight.shape
    n = len(firsts)
    table = jnp.stack([jnp.int32(f * head) for f in firsts] + [start])
    return pl.pallas_call(
        functools.partial(split_kernel, half=half),
        grid_spec=pltpu.PrefetchScalarGridSpec(
            num_scalar_prefetch=1,
            grid=(n,),
            in_specs=[pl.BlockSpec((total, 2, lru), lambda w, table: (0, 0, 0))],
            out_specs=pl.BlockSpec((1, rows, span * head), lambda w, table: (w, 0, 0)),
        ),
        out_shape=jax.ShapeDtypeStruct((n, rows, span * head), weight.dtype),
        name="split_columns",
    )(table, weight)


def far_kernel(
    normed_ref,
    cot_ref,
    gate_ref,
    up_ref,
    wout_ref,
    own_gate_ref,
    own_up_ref,
    own_out_ref,
    ggate_ref,
    gup_ref,
    gout_ref,
):
    @pl.when(pl.program_id(0) == 0)
    def _():
        ggate_ref[...] = own_gate_ref[...]
        gup_ref[...] = own_up_ref[...]
        gout_ref[...] = own_out_ref[...]

    normed = normed_ref[...]
    cot = cot_ref[...]
    value, slope = gelu_parts(dot(normed, gate_ref[...]))
    up = dot(normed, up_ref[...])
    grad = dot_back(cot, wout_ref[...])
    gout_ref[...] += dot_over((value * up).astype(BF16), cot)
    ggate_ref[...] += dot_over(normed, (grad * up * slope).astype(BF16))
    gup_ref[...] += dot_over(normed, (grad * value).astype(BF16))


def far_grads(normed, cot, weight_in, weight_out, sums, part, parts):
    total, width = normed.shape
    hidden = weight_out.shape[0] // parts
    rows = min(512, total)
    once = pl.Buffered(1)
    data = pl.BlockSpec((rows, width), lambda i: (i, 0))
    cols = lambda i: (0, part)
    lines = lambda i: (part, 0)
    held = pl.BlockSpec((width, hidden), cols, pipeline_mode=once)
    up = pl.BlockSpec((width, hidden), lambda i: (0, parts + part), pipeline_mode=once)
    held_out = pl.BlockSpec((hidden, width), lines, pipeline_mode=once)
    return pl.pallas_call(
        far_kernel,
        grid=(total // rows,),
        in_specs=[data, data, held, up, held_out, held, held, held_out],
        out_specs=[
            pl.BlockSpec((width, hidden), cols),
            pl.BlockSpec((width, hidden), cols),
            pl.BlockSpec((hidden, width), lines),
        ],
        out_shape=[jax.ShapeDtypeStruct(v.shape, F32) for v in sums],
        input_output_aliases={5: 0, 6: 1, 7: 2},
        cost_estimate=pl.CostEstimate(
            flops=1024, bytes_accessed=1024, transcendentals=0
        ),
        compiler_params=pltpu.CompilerParams(
            dimension_semantics=("arbitrary",), vmem_limit_bytes=60 << 20
        ),
        name="far_grads",
    )(normed, cot, weight_in, weight_in, weight_out, *sums)


def norm_kernel(src, gain, dst):
    rows = src[0].astype(F32)
    inv = lax.rsqrt(jnp.mean(rows * rows, axis=-1, keepdims=True) + 1e-06)
    dst[...] = (rows * inv * gain[...]).astype(BF16)


def norm_packed(packed, gain, size):
    n, _, width = packed.shape
    return pl.pallas_call(
        norm_kernel,
        grid=(n,),
        in_specs=[
            pl.BlockSpec((1, size, width), lambda w: (w, 0, 0)),
            pl.BlockSpec((1, width), lambda w: (0, 0)),
        ],
        out_specs=pl.BlockSpec((size, width), lambda w: (w, 0)),
        out_shape=jax.ShapeDtypeStruct((n * size, width), BF16),
        name="norm_packed",
    )(packed, gain)


def join_kernel(first, second, joined):
    joined[:, 0, :] = first[...].astype(F32)
    joined[:, 1, :] = second[...].astype(F32)


def join_halves(first, second):
    total, width = first.shape
    rows = math.gcd(total, 512)
    block = pl.BlockSpec((rows, width), lambda i: (i, 0))
    return pl.pallas_call(
        join_kernel,
        grid=(total // rows,),
        in_specs=[block, block],
        out_specs=pl.BlockSpec((rows, 2, width), lambda i: (i, 0, 0)),
        out_shape=jax.ShapeDtypeStruct((total, 2, width), F32),
        compiler_params=pltpu.CompilerParams(vmem_limit_bytes=60 << 20),
        name="join_halves",
    )(first, second)


def bit_list(n):
    return [1 << i for i in range(n.bit_length() - 1)]


def swap(block, axis, bit):
    return lax.ppermute(block, axis, [(i, i ^ bit) for i in range(lax.axis_size(axis))])


def gather_steps(block):
    n = lax.axis_size("wide")
    links = bit_list(n)[1:]
    half = block.shape[1] // 2
    sides = [block[:, :half], block[:, half:]]
    orders = [links, links[::-1]]
    for m, bits in enumerate(zip(*orders)):
        got = yield [swap(side, "wide", bit) for side, bit in zip(sides, bits)]
        sides = [jnp.stack([s, g], axis=m) for s, g in zip(sides, got)]
    for i, order in enumerate(orders):
        place = sorted(range(len(order)), key=lambda k: -order[k])
        sides[i] = sides[i].transpose(*place, len(order), len(order) + 1)
    return jnp.concatenate(sides, axis=-1).reshape(-1, block.shape[1])


def other_core(rows):
    return swap(rows, "wide", 1)


def scatter_steps(keep, send):
    n = lax.axis_size("wide")
    links = bit_list(n)[1:]
    rows, width = keep.shape[0] // (n // 2), keep.shape[1]
    half = width // 2
    got = yield [other_core(send)]
    held = keep + got[0].astype(F32)
    held = held.reshape((2,) * len(links) + (rows, width))
    sides = [held[..., :half], held[..., half:]]
    axes = [links[::-1], links[::-1]]
    for bits in zip(links, links[::-1]):
        kept, sent = [], []
        for i, bit in enumerate(bits):
            axis = axes[i].index(bit)
            kept.append(lax.index_in_dim(sides[i], 0, axis, keepdims=False))
            part = lax.index_in_dim(sides[i], 1, axis, keepdims=False)
            sent.append(swap(part.astype(BF16), "wide", bit))
            axes[i] = axes[i][:axis] + axes[i][axis + 1 :]
        got = yield sent
        sides = [k + g.astype(F32) for k, g in zip(kept, got)]
    return jnp.concatenate(sides, axis=-1)


def run_steps(steps, arrived=None):
    try:
        while True:
            arrived = steps.send(arrived)
    except StopIteration as end:
        return end.value


def tie(value, *before):
    return lax.optimization_barrier((value, *before))[0]


def line_step(part, stage):
    n = lax.axis_size("seq")
    if n < 2 or n % 2:
        return lax.psum(part, "seq") if stage == 1 else part
    here = lax.axis_index("seq")

    def step(pairs):
        got = lax.ppermute(part, "seq", pairs)
        return got, (part.astype(F32) + got.astype(F32)).astype(BF16)

    middle = n // 2
    if stage == 0:
        for k in range(middle - 1):
            part = step([(k, k + 1), (n - 1 - k, n - 2 - k)])[1]
    elif stage == 1:
        part = step([(middle - 1, middle), (middle, middle - 1)])[1]
    else:
        for k in range(middle - 2, -1, -1):
            got = step([(k + 1, k), (n - 2 - k, n - 1 - k)])[0]
            part = jnp.where((here == k) | (here == n - 1 - k), got, part)
    return part


def sum_small(values, axis):
    n = lax.axis_size(axis)
    if n & (n - 1):
        return lax.psum(values, axis)
    length = values.shape[0]
    padded = jnp.pad(values, (0, -length % (SUB * LANES))).reshape(-1, LANES)
    for bit in bit_list(n):
        padded = padded + swap(padded, axis, bit)
    return padded.reshape(-1)[:length]


def exchange(blocks):
    return lax.all_to_all(blocks, "wide", split_axis=0, concat_axis=0, tiled=True)


def near_place(r, n):
    return 2 * (r % (n // 2)) + r // (n // 2)


def move_kernel(table_ref, src, dst):
    dst[...] = src[...]


def move_rows(rows, near):
    n = lax.axis_size("wide")
    here = lax.axis_index("wide")
    size = rows.shape[0] // n
    table = jnp.stack([here ^ near_place(r, n) for r in range(n)]).astype(jnp.int32)
    device = lambda r, table: (table[r], 0)
    place = lambda r, table: (r, 0)
    block = (size, rows.shape[1])
    return pl.pallas_call(
        move_kernel,
        grid_spec=pltpu.PrefetchScalarGridSpec(
            num_scalar_prefetch=1,
            grid=(n,),
            in_specs=[pl.BlockSpec(block, device if near else place)],
            out_specs=pl.BlockSpec(block, place if near else device),
        ),
        out_shape=jax.ShapeDtypeStruct(rows.shape, rows.dtype),
        name="move_rows",
    )(table, rows)


def to_near(rows):
    return move_rows(rows, True)


def norm_rows(rows):
    inv = lax.rsqrt(jnp.mean(rows * rows, axis=-1, keepdims=True) + 1e-06)
    return inv, rows * inv


def norm_back(grad, gain, inv, unit):
    scaled = grad * gain
    return inv * (scaled - unit * jnp.mean(scaled * unit, axis=-1, keepdims=True))


def feed_forward_back(gate_up, cot, weight_out):
    hidden_width = weight_out.shape[0]
    gate, up = gate_up[:, :hidden_width], gate_up[:, hidden_width:]
    value, slope = gelu_parts(gate)
    hidden_grad = dot_back(cot, weight_out)
    hidden = (value * up).astype(BF16)
    gate_up_grad = jnp.concatenate(
        [
            (hidden_grad * up * slope).astype(BF16),
            (hidden_grad * value).astype(BF16),
        ],
        axis=1,
    )
    return hidden, gate_up_grad


def feed_forward(normed, cot, weight_in, weight_out):
    return feed_forward_back(dot(normed, weight_in), cot, weight_out)


def shards(
    tokens,
    cotangent,
    norm_gains,
    in_weight,
    conv_weight,
    conv_bias,
    gate_weights,
    gate_biases,
    decay_param,
    out_weight,
    mlp_in_weight,
    mlp_out_weight,
):
    n_wide, n_seq = lax.axis_size("wide"), lax.axis_size("seq")
    here = lax.axis_index("wide")
    tok_low, cot_low = tokens[0], cotangent[0]
    size, width = tok_low.shape
    own = out_weight.shape[0]
    lru = own * n_wide
    heads, head = gate_weights.shape[1:3]
    taps = conv_weight.shape[0]
    gain_own = norm_gains.shape[1]
    hidden_units = mlp_out_weight.shape[0]
    part = head // n_wide

    span = max(
        ((w + 1) * own - 1) // head - w * own // head + 1 for w in range(n_wide)
    )
    firsts = [min(w * own // head, heads - span) for w in range(n_wide)]
    win = span * head
    start = jnp.minimum(here * own // head, heads - span) * head
    offset = here * own - start

    total = size * n_wide
    half = total // 2
    recompute = n_seq * total <= 8192 and n_seq & (n_seq - 1) == 0 and n_seq > 1

    def far_rows(rows):
        return [swap(rows, "seq", d) for d in range(1, n_seq)] if recompute else []

    def far_gather(rows):
        return lax.all_gather(rows, "wide", axis=0, tiled=True)

    small = jnp.concatenate(
        [
            norm_gains.reshape(-1),
            conv_weight.reshape(-1),
            conv_bias,
            gate_biases.reshape(-1),
            decay_param,
        ]
    )
    n_small = small.shape[0]
    small = jnp.pad(small, (0, -n_small % (16 * width))).reshape(-1, width)
    gate_rows = heads * part * head // width
    packed = jnp.concatenate(
        [
            tok_low,
            small,
            gate_weights.transpose(0, 1, 3, 2).reshape(2 * gate_rows, width),
        ]
    )
    got = lax.all_gather(packed, "wide")
    gates_all = got[:, -2 * gate_rows :].reshape(n_wide, 2, gate_rows, width)
    gate_rows = gate_rows // heads
    small = got[:, size : -2 * heads * gate_rows].reshape(n_wide, -1)[:, :n_small]

    own_rows = in_weight.shape[0]
    shared = n_seq % 2 == 0 and own_rows % 32 == 0
    row_part = own_rows // 2 if shared else own_rows
    odd = lax.axis_index("seq") % 2

    def fetch(half):
        begin = (odd * row_part if shared else odd * 0).astype(jnp.int32)
        return split_columns(in_weight, half, firsts, head, span, begin, row_part)

    def share(rows):
        return swap(rows, "seq", 1) if shared else ()

    def whole(rows, other):
        if shared:
            even = jnp.where(odd == 0, rows, other)
            rows = jnp.stack([even, jnp.where(odd == 0, other, rows)], axis=1)
        return rows.reshape(width, win)

    send_branch, send_gate = lax.optimization_barrier((fetch(0), fetch(1)))
    branch_mine = exchange(send_branch)
    gate_mine = exchange(send_gate)
    branch_other, gate_other = share(branch_mine), share(gate_mine)
    in_branch = whole(branch_mine, branch_other)
    gains = (
        small[:, : 2 * gain_own]
        .reshape(n_wide, 2, gain_own)
        .transpose(1, 0, 2)
        .reshape(2, width)
        .astype(F32)
    )
    channels = (
        small[:, 2 * gain_own :]
        .reshape(n_wide, taps + 4, own)
        .transpose(1, 0, 2)
        .reshape(taps + 4, lru)
    )
    channels = lax.dynamic_slice_in_dim(channels, start, win, axis=1).astype(F32)
    chan = jnp.concatenate(
        [channels[: taps + 3], -8.0 * jax.nn.softplus(-channels[taps + 3 :])]
    )
    normed_all = norm_packed(got, gains[:1], size)
    out_own = lax.dynamic_update_slice_in_dim(
        jnp.zeros((win, width), BF16), out_weight, offset, 0
    )
    mlp_in = mlp_in_weight.reshape(width, -1)

    in_branch, normed_all, chan, gains, out_own, mlp_in, gate_mine = (
        lax.optimization_barrier(
            (in_branch, normed_all, chan, gains, out_own, mlp_in, gate_mine)
        )
    )


    below = max(w * own - f * head for w, f in enumerate(firsts))
    above = max(f * head + win - (w + 1) * own for w, f in enumerate(firsts))
    if max(below, above) <= own:
        around = [
            lax.ppermute(
                out_weight[own - below :],
                "wide",
                [(i, i + 1) for i in range(n_wide - 1)],
            ),
            out_weight,
            lax.ppermute(
                out_weight[:above], "wide", [(i + 1, i) for i in range(n_wide - 1)]
            ),
        ]
        first_row = below - offset
    else:
        around = [lax.all_gather(out_weight, "wide", axis=0, tiled=True)]
        first_row = start
    cot_sent = far_rows(cot_low)
    cot_all = lax.all_gather(tie(cot_low, in_branch), "wide", axis=0, tiled=True)
    gate_w = (
        lax.dynamic_slice_in_dim(
            gates_all, start // head * gate_rows, span * gate_rows, axis=2
        )
        .reshape(n_wide, 2, span, part, head)
        .transpose(1, 2, 0, 3, 4)
        .reshape(2, span, head, head)
    )
    chunk = min(total, 512)
    states, *saved, enter = recur_forward(
        dot(normed_all, in_branch), chan, gate_w, taps, chunk
    )
    gate_mine, gate_other, states, around = lax.optimization_barrier(
        (gate_mine, gate_other, states, around)
    )
    in_gate = whole(gate_mine, gate_other)
    mixed_near, gate_rows = mix_forward(
        dot(normed_all, in_gate), states, head, chunk, size
    )
    out_send = dot(mixed_near[half:], out_own).astype(BF16)
    out_send, mixed_near, cot_all = lax.optimization_barrier(
        (out_send, mixed_near, cot_all)
    )
    rows = tok_low.astype(F32)
    steps = scatter_steps(dot(mixed_near[:half], out_own), out_send)
    way, in_branch, in_gate, around = lax.optimization_barrier(
        (steps.send(None), in_branch, in_gate, around)
    )
    way = steps.send(way)
    in_own = jnp.concatenate(
        [
            lax.dynamic_slice_in_dim(weight, offset, own, axis=1)
            for weight in (in_branch, in_gate)
        ],
        axis=1,
    )
    out_win = lax.dynamic_slice_in_dim(jnp.concatenate(around), first_row, win)
    way, in_own, out_win = lax.optimization_barrier((way, in_own, out_win))
    middle = rows + run_steps(steps, way)
    inv_two, unit_two = norm_rows(middle)
    normed_two = (unit_two * gains[1]).astype(BF16)
    middle, normed_two, inv_two, unit_two, cot_all = lax.optimization_barrier(
        (middle, normed_two, inv_two, unit_two, cot_all)
    )

    steps = gather_steps(normed_two)
    way = steps.send(None)
    sent = far_rows(normed_two)
    cot_near = to_near(cot_all)
    way, cot_near, cot_sent = lax.optimization_barrier((way, cot_near, cot_sent))
    cot_sent = jnp.concatenate(cot_sent) if recompute else ()
    way, cot_sent = lax.optimization_barrier((steps.send(way), cot_sent))
    normed_even = run_steps(steps, way)
    normed_even, cot_sent = lax.optimization_barrier((normed_even, cot_sent))
    cot_far = far_gather(cot_sent) if recompute else ()
    normed_odd = other_core(normed_even)
    hidden_even, grad_even = feed_forward(
        normed_even, cot_near[:half], mlp_in, mlp_out_weight
    )
    hidden_odd, grad_odd = feed_forward(
        normed_odd, cot_near[half:], mlp_in, mlp_out_weight
    )
    up_send = dot_back(grad_odd, mlp_in).astype(BF16)
    up_send, hidden_even, hidden_odd, grad_even, grad_odd, normed_odd, first_sent = (
        lax.optimization_barrier(
            (
                up_send,
                hidden_even,
                hidden_odd,
                grad_even,
                grad_odd,
                normed_odd,
                sent[:1],
            )
        )
    )
    sent = first_sent + sent[1:]
    steps = scatter_steps(dot_back(grad_even, mlp_in), up_send)
    way, grad_even, grad_odd, hidden_even, hidden_odd = lax.optimization_barrier(
        (steps.send(None), grad_even, grad_odd, hidden_even, hidden_odd)
    )
    way = steps.send(way)
    gate_sum = dot_over(normed_even, grad_even[:, :hidden_units]) + dot_over(
        normed_odd, grad_odd[:, :hidden_units]
    )
    up_sum = dot_over(normed_even, grad_even[:, hidden_units:]) + dot_over(
        normed_odd, grad_odd[:, hidden_units:]
    )
    way, gate_sum, up_sum, hidden_even, hidden_odd = lax.optimization_barrier(
        (way, gate_sum, up_sum, hidden_even, hidden_odd)
    )
    out_sum = dot_over(hidden_even, cot_near[:half]) + dot_over(
        hidden_odd, cot_near[half:]
    )
    normed_two_grad = run_steps(steps, way)
    middle_grad = cot_low.astype(F32) + norm_back(
        normed_two_grad, gains[1], inv_two, unit_two
    )
    mix_low = middle_grad.astype(BF16)
    gain_two_grad = jnp.sum(normed_two_grad * unit_two, axis=0)
    (
        middle_grad,
        mix_low,
        gain_two_grad,
        out_sum,
        hidden_even,
        hidden_odd,
        sent,
    ) = lax.optimization_barrier(
        (
            middle_grad,
            mix_low,
            gain_two_grad,
            out_sum,
            hidden_even,
            hidden_odd,
            sent,
        )
    )

    steps = gather_steps(mix_low)
    way, sent = lax.optimization_barrier((steps.send(None), sent))
    way = steps.send(way)
    normed_far = far_gather(jnp.concatenate(sent)) if recompute else ()
    feed_send = dot(hidden_odd, mlp_out_weight).astype(BF16)
    feed_keep = dot(hidden_even, mlp_out_weight)
    way, feed_send, feed_keep = lax.optimization_barrier((way, feed_send, feed_keep))
    mix_even = run_steps(steps, way)
    mix_odd = other_core(mix_even)
    even_grad = dot_back(mix_even, out_win)
    mix_odd, even_grad, cot_far = lax.optimization_barrier(
        (mix_odd, even_grad, cot_far)
    )
    mix_near = jnp.concatenate([mix_even, mix_odd])
    mixed_grad = jnp.concatenate([even_grad, dot_back(mix_odd, out_win)])
    out_grad = lax.dynamic_slice_in_dim(
        dot_over(mixed_near, mix_near).astype(BF16), offset, own
    )
    gate_half, state_grad = gate_backward(
        mixed_grad, states, gate_rows, head, chunk, size
    )
    state_grad, out_grad = lax.optimization_barrier((state_grad, out_grad))
    out_grad = line_step(out_grad, 0)

    def in_part(grad):
        return dot_over(normed_all, grad).astype(BF16).reshape(n_wide, -1, own)

    def in_rows(part):
        return jnp.moveaxis(exchange(part), 0, 1).reshape(-1, lru)

    branch_half, gate_grad, sums = recur_backward(
        state_grad, (states, *saved, enter), chan, gate_w, taps, chunk
    )
    branch_half = lax.dynamic_slice_in_dim(branch_half, offset, own, axis=1)
    branch_part = in_part(branch_half)
    branch_half, branch_part, gate_half, gate_grad, sums = lax.optimization_barrier(
        (branch_half, branch_part, gate_half, gate_grad, sums)
    )
    branch_rows_grad = in_rows(branch_part)
    gate_half = lax.dynamic_slice_in_dim(gate_half, offset, own, axis=1)
    gate_part = in_part(gate_half)
    own_near = to_near(jnp.concatenate([branch_half, gate_half], axis=1))
    normed_send = dot_back(own_near[half:], in_own).astype(BF16)
    (
        branch_rows_grad,
        gate_part,
        own_near,
        normed_send,
        out_grad,
        normed_far,
        gate_grad,
        feed_keep,
    ) = lax.optimization_barrier(
        (
            branch_rows_grad,
            gate_part,
            own_near,
            normed_send,
            out_grad,
            normed_far,
            gate_grad,
            feed_keep,
        )
    )
    branch_rows_grad = lax.psum(branch_rows_grad, "seq")
    gate_rows_grad = in_rows(gate_part)
    out_grad = line_step(out_grad, 1)
    normed_steps = scatter_steps(dot_back(own_near[:half], in_own), normed_send)
    way = normed_steps.send(None)

    parts = hidden_units // 256 if hidden_units % 256 == 0 else 1
    held = (gate_sum, up_sum, out_sum)
    feed_steps = scatter_steps(feed_keep, feed_send)

    def far_part(held, done):
        for p in range(done, parts if done == 2 else min(done + 1, parts)):
            if recompute:
                held = far_grads(
                    normed_far, cot_far, mlp_in, mlp_out_weight, held, p, parts
                )
        return held

    held = far_part(held, 0)
    way, held, gate_rows_grad, out_grad, normed_far, gate_grad, feed_keep = (
        lax.optimization_barrier(
            (way, held, gate_rows_grad, out_grad, normed_far, gate_grad, feed_keep)
        )
    )
    gate_grad = exchange(
        gate_grad.astype(BF16)
        .reshape(2, span, n_wide, part, head)
        .transpose(2, 0, 1, 3, 4)
    )
    out_grad = line_step(out_grad, 2)
    way = normed_steps.send(way)
    feed_way = feed_steps.send(None)
    held = far_part(held, 1)
    way, feed_way, held, gate_grad, out_grad, normed_far = lax.optimization_barrier(
        (way, feed_way, held, gate_grad, out_grad, normed_far)
    )
    holders = [
        next(w for w, f in enumerate(firsts) if f <= j < f + span) for j in range(heads)
    ]
    gate_grad = jnp.stack(
        [gate_grad[w, :, j - firsts[w]] for j, w in enumerate(holders)], axis=1
    )
    out_grad = out_grad.astype(F32)
    way = normed_steps.send(way)
    feed_way = feed_steps.send(feed_way)
    branch_rows_grad, gate_rows_grad, gate_grad, out_grad, normed_far = (
        lax.optimization_barrier(
            (branch_rows_grad, gate_rows_grad, gate_grad, out_grad, normed_far)
        )
    )
    gate_rows_grad, gate_grad = lax.psum((gate_rows_grad, gate_grad), "seq")
    held = far_part(held, 2)
    way, feed_way, held = lax.optimization_barrier((way, feed_way, held))
    normed_grad = run_steps(normed_steps, way)
    inv_one, unit_one = norm_rows(rows)
    input_grad = middle_grad + norm_back(normed_grad, gains[0], inv_one, unit_one)
    gain_one_grad = jnp.sum(normed_grad * unit_one, axis=0)
    feed = run_steps(feed_steps, feed_way)
    result = (middle + feed).astype(BF16)
    if recompute:
        mlp_in_grad = join_halves(held[0], held[1])
    else:
        mlp_in_grad = jnp.stack(held[:2], axis=1)
    mlp_out_grad = held[2]
    in_grad = join_halves(branch_rows_grad, gate_rows_grad)
    sums = lax.dynamic_slice_in_dim(sums[: taps + 4], offset, own, axis=1)
    gate_grad = gate_grad.astype(F32).transpose(0, 1, 3, 2)

    gains_grad = sum_small(jnp.concatenate([gain_one_grad, gain_two_grad]), "wide")
    gains_grad = lax.dynamic_slice_in_dim(
        gains_grad.reshape(2, width), here * gain_own, gain_own, axis=1
    )
    small = sum_small(
        jnp.concatenate([gains_grad.reshape(-1), sums.reshape(-1)]), "seq"
    )
    gains_grad = small[: 2 * gain_own].reshape(2, gain_own)
    sums = small[2 * gain_own :].reshape(taps + 4, own)
    decay_grad = sums[taps + 3] * 8.0 * jax.nn.sigmoid(-decay_param.astype(F32))
    if not recompute:
        mlp_out_grad, mlp_in_grad = (
            lax.psum(g.astype(BF16), "seq").astype(F32)
            for g in (mlp_out_grad, mlp_in_grad)
        )
    return (
        result[None],
        input_grad[None],
        gains_grad,
        in_grad,
        sums[:taps],
        sums[taps],
        gate_grad,
        sums[taps + 1 : taps + 3],
        decay_grad,
        out_grad,
        mlp_in_grad,
        mlp_out_grad,
    )


def solution(mesh):
    placed = (
        P("seq", "wide", None),
        P("seq", "wide", None),
        P(None, "wide"),
        P("wide", None, None),
        P(None, "wide"),
        P("wide"),
        P(None, None, None, "wide"),
        P(None, "wide"),
        P("wide"),
        P("wide", None),
        P(None, None, "wide"),
        P("wide", None),
    )
    return jax.shard_map(
        shards,
        mesh=mesh,
        in_specs=placed,
        out_specs=(
            P("seq", "wide", None),
            P("seq", "wide", None),
            P(None, "wide"),
            P("wide", None, None),
            P(None, "wide"),
            P("wide"),
            P(None, None, None, "wide"),
            P(None, "wide"),
            P("wide"),
            P("wide", None),
            P(None, None, "wide"),
            P("wide", None),
        ),
        check_vma=False,
    )
```

```python
import functools
import math
import jax
import jax.numpy as jnp
from jax import lax
from jax.experimental import pallas as pl
from jax.experimental.pallas import tpu as pltpu
from jax.sharding import PartitionSpec as P

BF16 = jnp.bfloat16
F32 = jnp.float32
SUB = 8
LANES = 128
GELU_A = math.sqrt(2.0 / math.pi)
GELU_B = 0.044715


def dot(left, right):
    return jnp.dot(left, right, preferred_element_type=F32)


def dot_over(left, right):
    return lax.dot_general(
        left, right, (((0,), (0,)), ((), ())), preferred_element_type=F32
    )


def dot_back(left, right):
    return lax.dot_general(
        left, right, (((1,), (1,)), ((), ())), preferred_element_type=F32
    )


def gelu_parts(v):
    square = v * v
    th = jnp.tanh(GELU_A * v * (1.0 + GELU_B * square))
    value = 0.5 * v * (1.0 + th)
    slope = 0.5 * (1.0 + th) + 0.5 * v * (1.0 - th * th) * (
        GELU_A * (1.0 + 3.0 * GELU_B * square)
    )
    return value, slope


def minus_expm1(v):
    series = jnp.full_like(v, 1.0 / 40320.0)
    for factorial in (5040.0, 720.0, 120.0, 24.0, 6.0, 2.0, 1.0):
        series = series * v + 1.0 / factorial
    return jnp.where(v > -0.5, -v * series, 1.0 - jnp.exp(v))


def sub_iota(width):
    return lax.broadcasted_iota(jnp.int32, (SUB, width), 0)


def roll_down(v, first):
    return jnp.where(sub_iota(v.shape[1]) == 0, first, pltpu.roll(v, 1, 0))


def roll_up(v, last):
    return jnp.where(sub_iota(v.shape[1]) == SUB - 1, last, pltpu.roll(v, SUB - 1, 0))


def rows8(step):
    return pl.ds(pl.multiple_of(step * SUB, SUB), SUB)


def strided_load(refs, s, steps):
    return jnp.concatenate([r[pl.ds(s, SUB, stride=steps), :] for r in refs], axis=1)


def strided_store(ref, s, steps, v):
    for n in range(ref.shape[0]):
        ref.at[n][pl.ds(s, SUB, stride=steps), :] = v[:, n * LANES : (n + 1) * LANES]


def forward_kernel(*refs, taps, groups):
    forward_body(refs[:groups], *refs[groups:], taps=taps)


def forward_body(
    branch_refs,
    chan_ref,
    gw_ref,
    states_ref,
    decay_ref,
    rgate_ref,
    igate_ref,
    scale_ref,
    low_ref,
    brow_ref,
    enter_ref,
    ext,
    pre0,
    pre1,
    prod,
    tail,
    carry,
    *,
    taps,
):
    rows, width = states_ref.shape
    steps = rows // SUB
    halo = taps - 1

    @pl.when(pl.program_id(1) == 0)
    def _():
        tail[...] = jnp.zeros_like(tail)
        carry[...] = jnp.zeros_like(carry)

    def load(s, _):
        v = strided_load(branch_refs, s, steps).astype(BF16).astype(F32)
        ext[rows8(s + halo), :] = v
        return 0

    lax.fori_loop(0, steps, load, 0, unroll=8)
    for back in range(1, halo + 1):
        v = ext[rows8(halo + steps - back), :]
        ext[rows8(halo - back), :] = roll_down(v, tail[back - 1 : back, :])
        tail[back - 1 : back, :] = v[SUB - 1 : SUB]
    big = 8
    wide = SUB * big

    def block(i):
        return pl.ds(pl.multiple_of(i * wide, wide), wide)

    def conv(i, _):
        out = chan_ref[taps : taps + 1, :]
        for k in range(taps):
            v = ext[pl.ds(pl.multiple_of((i * big + halo - k) * SUB, SUB), wide), :]
            out = out + chan_ref[k : k + 1, :] * v
            if k == 0:
                brow_ref[block(i), :] = v.astype(BF16)
        low_ref[block(i), :] = out.astype(BF16)
        return 0

    lax.fori_loop(0, steps // big, conv, 0, unroll=2)
    low = low_ref[...]
    pre0[...] = dot_back(low, gw_ref[0, 0])
    pre1[...] = dot_back(low, gw_ref[1, 0])

    def gates(i, _):
        r = jax.nn.sigmoid(pre0[block(i), :] + chan_ref[taps + 1 : taps + 2, :])
        g = jax.nn.sigmoid(pre1[block(i), :] + chan_ref[taps + 2 : taps + 3, :])
        log_decay = r * chan_ref[taps + 3 : taps + 4, :]
        scale = jnp.sqrt(minus_expm1(2.0 * log_decay))
        rgate_ref[block(i), :] = r
        igate_ref[block(i), :] = g
        scale_ref[block(i), :] = scale
        decay_ref[block(i), :] = jnp.exp(log_decay)
        pre0[block(i), :] = scale * g * low_ref[block(i), :].astype(F32)
        return 0

    lax.fori_loop(0, steps // big, gates, 0, unroll=2)

    def scan(s, hp):
        h, p = hp
        a = decay_ref[rows8(s), :]
        h = a * h + pre0[rows8(s), :]
        p = a * p
        states_ref[rows8(s), :] = h
        prod[rows8(s), :] = p
        return h, p

    zero = jnp.zeros((SUB, width), F32)
    h, p = lax.fori_loop(0, steps, scan, (zero, zero + 1.0), unroll=16)
    for shift in (1, 2, 4):
        keep = sub_iota(width) >= shift
        h = h + p * jnp.where(keep, pltpu.roll(h, shift, 0), 0.0)
        p = p * jnp.where(keep, pltpu.roll(p, shift, 0), 1.0)
    first = carry[0:1, :]
    ends = h + p * first
    enter = roll_down(ends, first)
    enter_ref[...] = enter
    carry[0:1, :] = ends[SUB - 1 : SUB]

    def finish(s, _):
        states_ref[rows8(s), :] = states_ref[rows8(s), :] + prod[rows8(s), :] * enter
        return 0

    lax.fori_loop(0, steps, finish, 0, unroll=8)


def near_index(device, n):
    bits = lax.axis_index("wide") ^ device
    return (bits >> 1) + (bits & 1) * (n // 2)


def mix_kernel(*refs, groups, n, size):
    states_ref, mixed_ref, gperm_ref, out, stage, sems = refs[groups:]
    rows, width = states_ref.shape
    steps = rows // SUB
    head, chunk = pl.program_id(0), pl.program_id(1)
    chunks = pl.num_programs(1)
    step = head * chunks + chunk
    last = pl.num_programs(0) * chunks - 1
    slot = step % 2

    def copies(slot):
        made = []
        for k in range(rows // size):
            place = near_index(chunk * (rows // size) + k, n)
            made.append(
                pltpu.make_async_copy(
                    stage.at[slot, pl.ds(k * size, size)],
                    mixed_ref.at[
                        pl.ds(pl.multiple_of(place * size, size), size),
                        pl.ds(pl.multiple_of(head * width, width), width),
                    ],
                    sems.at[slot, k],
                )
            )
        return made

    def body(s, _):
        v = strided_load(refs[:groups], s, steps)
        gperm_ref[rows8(s), :] = v
        strided_store(out, s, steps, gelu_parts(v)[0] * states_ref[rows8(s), :])
        return 0

    lax.fori_loop(0, steps, body, 0, unroll=8)

    @pl.when(step >= 2)
    def _():
        for copy in copies(slot):
            copy.wait()

    for g in range(width // LANES):
        stage[slot, :, g * LANES : (g + 1) * LANES] = out[g].astype(BF16)
    for copy in copies(slot):
        copy.start()

    @pl.when(step == last)
    def _():
        for copy in copies(slot):
            copy.wait()

    @pl.when((step == last) & (step >= 1))
    def _():
        for copy in copies(1 - slot):
            copy.wait()


def mix_forward(gate_branch, states, head, chunk, size):
    total, width = states.shape
    groups = head // LANES
    blk = pl.BlockSpec((chunk, head), lambda j, c: (c, j))
    lane = [
        pl.BlockSpec((chunk, LANES), lambda j, c, n=n: (c, j * groups + n))
        for n in range(groups)
    ]
    return pl.pallas_call(
        functools.partial(
            mix_kernel, groups=groups, n=lax.axis_size("wide"), size=size
        ),
        grid=(width // head, total // chunk),
        in_specs=lane + [blk],
        out_specs=[pl.BlockSpec(memory_space=pl.ANY), blk],
        out_shape=[
            jax.ShapeDtypeStruct((total, width), BF16),
            jax.ShapeDtypeStruct((total, width), F32),
        ],
        scratch_shapes=[
            pltpu.VMEM((groups, chunk, LANES), F32),
            pltpu.VMEM((2, chunk, head), BF16),
            pltpu.SemaphoreType.DMA((2, chunk // size)),
        ],
        compiler_params=pltpu.CompilerParams(
            dimension_semantics=("arbitrary", "arbitrary"), vmem_limit_bytes=60 << 20
        ),
        name="mix_forward",
    )(*[gate_branch] * groups, states)


def recur_forward(projected, chan, gate_w, taps, chunk):
    total, width = projected.shape
    head = gate_w.shape[2]
    heads = width // head
    chunks = total // chunk
    rows = lambda j, c: (c, j)
    blk = pl.BlockSpec((chunk, head), rows)
    f32s = jax.ShapeDtypeStruct((total, width), F32)
    b16s = jax.ShapeDtypeStruct((total, width), BF16)
    work = pltpu.VMEM((chunk, head), F32)
    groups = head // LANES
    lane = [
        pl.BlockSpec((chunk, LANES), lambda j, c, n=n: (c, j * groups + n))
        for n in range(groups)
    ]
    return pl.pallas_call(
        functools.partial(forward_kernel, taps=taps, groups=groups),
        grid=(heads, chunks),
        in_specs=[
            *lane,
            pl.BlockSpec((chan.shape[0], head), lambda j, c: (0, j)),
            pl.BlockSpec((2, 1, head, head), lambda j, c: (0, j, 0, 0)),
        ],
        out_specs=[blk] * 7 + [pl.BlockSpec((SUB, head), rows)],
        out_shape=[f32s, f32s, f32s, f32s, f32s, b16s, b16s]
        + [jax.ShapeDtypeStruct((chunks * SUB, width), F32)],
        scratch_shapes=[
            pltpu.VMEM((chunk + (taps - 1) * SUB, head), F32),
            work,
            work,
            work,
            pltpu.VMEM((SUB, head), F32),
            pltpu.VMEM((SUB, head), F32),
        ],
        compiler_params=pltpu.CompilerParams(
            dimension_semantics=("arbitrary", "arbitrary"), vmem_limit_bytes=60 << 20
        ),
        name="recur_forward",
    )(*[projected] * groups, chan, gate_w)


def gate_back_kernel(
    mgrad_ref, states_ref, gperm_ref, ggrad_ref, sgrad_ref, out, near, sems, *, n, size
):
    rows, width = states_ref.shape
    steps = rows // SUB
    groups = width // LANES
    chunks = pl.num_programs(1)
    step = pl.program_id(0) * chunks + pl.program_id(1)
    last = pl.num_programs(0) * chunks - 1
    slot = step % 2

    def copies(step, slot):
        made = []
        for k in range(rows // size):
            place = near_index(step % chunks * (rows // size) + k, n)
            for g in range(groups):
                lane = step // chunks * width + g * LANES
                made.append(
                    pltpu.make_async_copy(
                        mgrad_ref.at[
                            pl.ds(pl.multiple_of(place * size, size), size),
                            pl.ds(pl.multiple_of(lane, LANES), LANES),
                        ],
                        near.at[slot, g, pl.ds(k * size, size)],
                        sems.at[slot, k, g],
                    )
                )
        return made

    @pl.when(step == 0)
    def _():
        for copy in copies(step, slot):
            copy.start()

    @pl.when(step < last)
    def _():
        for copy in copies(step + 1, 1 - slot):
            copy.start()

    for copy in copies(step, slot):
        copy.wait()

    def body(s, _):
        value, slope = gelu_parts(gperm_ref[rows8(s), :])
        mg = strided_load([near.at[slot, g] for g in range(groups)], s, steps)
        strided_store(out, s, steps, mg * states_ref[rows8(s), :] * slope)
        sgrad_ref[rows8(s), :] = mg * value
        return 0

    lax.fori_loop(0, steps, body, 0, unroll=8)
    for g in range(groups):
        ggrad_ref[:, g * LANES : (g + 1) * LANES] = out[g].astype(BF16)


def gate_backward(mixed_grad, states, gate_rows, head, chunk, size):
    total, width = mixed_grad.shape
    groups = head // LANES
    blk = pl.BlockSpec((chunk, head), lambda j, c: (c, j))
    return pl.pallas_call(
        functools.partial(gate_back_kernel, n=lax.axis_size("wide"), size=size),
        grid=(width // head, total // chunk),
        in_specs=[pl.BlockSpec(memory_space=pl.ANY), blk, blk],
        out_specs=[blk, blk],
        out_shape=[
            jax.ShapeDtypeStruct((total, width), BF16),
            jax.ShapeDtypeStruct((total, width), F32),
        ],
        scratch_shapes=[
            pltpu.VMEM((groups, chunk, LANES), F32),
            pltpu.VMEM((2, groups, chunk, LANES), F32),
            pltpu.SemaphoreType.DMA((2, chunk // size, groups)),
        ],
        compiler_params=pltpu.CompilerParams(
            dimension_semantics=("arbitrary", "arbitrary"), vmem_limit_bytes=60 << 20
        ),
        name="gate_backward",
    )(mixed_grad, states, gate_rows)


def backward_kernel(
    sgrad_ref,
    states_ref,
    decay_ref,
    rgate_ref,
    igate_ref,
    scale_ref,
    low_ref,
    brow_ref,
    enter_ref,
    chan_ref,
    gw_ref,
    pgrad_ref,
    gwg_ref,
    sums_ref,
    car,
    prod,
    cgrad,
    lowf,
    gout,
    pre,
    sums,
    tail,
    carry,
    *,
    taps,
):
    rows, width = states_ref.shape
    steps = rows // SUB
    halo = taps - 1

    @pl.when(pl.program_id(1) == 0)
    def _():
        tail[...] = jnp.zeros_like(tail)
        carry[...] = jnp.zeros_like(carry)
        sums[...] = jnp.zeros_like(sums)
        gwg_ref[...] = jnp.zeros_like(gwg_ref)

    def scan(n, uq):
        u, q = uq
        s = steps - 1 - n
        c = sgrad_ref[rows8(s), :] + u
        car[rows8(s), :] = c
        prod[rows8(s), :] = q
        a = decay_ref[rows8(s), :]
        return a * c, a * q

    zero = jnp.zeros((SUB, width), F32)
    u, q = lax.fori_loop(0, steps, scan, (zero, zero + 1.0), unroll=16)
    for shift in (1, 2, 4):
        keep = sub_iota(width) < SUB - shift
        u = u + q * jnp.where(keep, pltpu.roll(u, SUB - shift, 0), 0.0)
        q = q * jnp.where(keep, pltpu.roll(q, SUB - shift, 0), 1.0)
    last = carry[0:1, :]
    ends = u + q * last
    enter = roll_up(ends, last)
    carry[0:1, :] = ends[0:1]
    neg = chan_ref[taps + 3 : taps + 4, :]
    state_in = enter_ref[...]

    def gates(s, acc):
        sum_r, sum_i, sum_d = acc
        c = car[rows8(s), :] + prod[rows8(s), :] * enter
        before = jnp.where(
            s == 0, state_in, states_ref[rows8(jnp.maximum(s - 1, 0)), :]
        )
        a = decay_ref[rows8(s), :]
        r = rgate_ref[rows8(s), :]
        g = igate_ref[rows8(s), :]
        scale = scale_ref[rows8(s), :]
        low = lowf[rows8(s), :]
        c_low = c * low
        dgrad = c * a * before - c_low * g * (a * a) / scale
        pr = dgrad * neg * r * (1.0 - r)
        pi = c_low * scale * g * (1.0 - g)
        pre[0, rows8(s), :] = pr
        pre[1, rows8(s), :] = pi
        cgrad[rows8(s), :] = c * scale * g
        pr = pr.astype(BF16).astype(F32)
        pi = pi.astype(BF16).astype(F32)
        return sum_r + pr, sum_i + pi, sum_d + dgrad * r

    lowf[...] = low_ref[...].astype(F32)
    sum_r, sum_i, sum_d = lax.fori_loop(0, steps, gates, (zero, zero, zero), unroll=8)
    low = low_ref[...]
    pr = pre[0].astype(BF16)
    pi = pre[1].astype(BF16)
    gwg_ref[0, 0] += dot_over(pr, low)
    gwg_ref[1, 0] += dot_over(pi, low)
    cgrad[pl.ds(0, rows), :] = (
        cgrad[pl.ds(0, rows), :] + dot(pr, gw_ref[0, 0]) + dot(pi, gw_ref[1, 0])
    )
    for ahead in range(halo):
        v = cgrad[rows8(ahead), :]
        cgrad[rows8(steps + ahead), :] = roll_up(v, tail[ahead : ahead + 1, :])
        tail[ahead : ahead + 1, :] = v[0:1]
    car[...] = brow_ref[...].astype(F32)

    def conv(s, acc):
        branch = car[rows8(s), :]
        out = zero
        new = []
        for k in range(taps):
            v = cgrad[rows8(s + k), :]
            out = out + chan_ref[k : k + 1, :] * v
            new.append(acc[k] + v * branch)
            if k == 0:
                new_bias = acc[taps] + v
        strided_store(gout, s, steps, out)
        return (*new, new_bias)

    acc = lax.fori_loop(0, steps, conv, (zero,) * (taps + 1), unroll=8)
    for n in range(width // LANES):
        pgrad_ref[:, n * LANES : (n + 1) * LANES] = gout[n].astype(BF16)
    for n, v in enumerate((*acc, sum_r, sum_i, sum_d)):
        sums[n] += v
        sums_ref[n : n + 1, :] = jnp.sum(sums[n], axis=0, keepdims=True)


def recur_backward(state_grad, saved, chan, gate_w, taps, chunk):
    total, width = state_grad.shape
    head = gate_w.shape[2]
    heads = width // head
    chunks = total // chunk
    rows = lambda j, c: (chunks - 1 - c, j)
    blk = pl.BlockSpec((chunk, head), rows)
    work = pltpu.VMEM((chunk, head), F32)
    gws = pl.BlockSpec((2, 1, head, head), lambda j, c: (0, j, 0, 0))
    groups = head // LANES
    n_sums = -(-(taps + 4) // SUB) * SUB
    return pl.pallas_call(
        functools.partial(backward_kernel, taps=taps),
        grid=(heads, chunks),
        in_specs=[blk] * 8
        + [
            pl.BlockSpec((SUB, head), rows),
            pl.BlockSpec((chan.shape[0], head), lambda j, c: (0, j)),
            gws,
        ],
        out_specs=[
            blk,
            gws,
            pl.BlockSpec((n_sums, head), lambda j, c: (0, j)),
        ],
        out_shape=[
            jax.ShapeDtypeStruct((total, width), BF16),
            jax.ShapeDtypeStruct((2, heads, head, head), F32),
            jax.ShapeDtypeStruct((n_sums, width), F32),
        ],
        scratch_shapes=[
            work,
            work,
            pltpu.VMEM((chunk + (taps - 1) * SUB, head), F32),
            work,
            pltpu.VMEM((groups, chunk, LANES), F32),
            pltpu.VMEM((2, chunk, head), F32),
            pltpu.VMEM((taps + 4, SUB, head), F32),
            pltpu.VMEM((SUB, head), F32),
            pltpu.VMEM((SUB, head), F32),
        ],
        compiler_params=pltpu.CompilerParams(
            dimension_semantics=("arbitrary", "arbitrary"), vmem_limit_bytes=60 << 20
        ),
        name="recur_backward",
    )(state_grad, *saved, chan, gate_w)


def split_kernel(table_ref, src, dst, *, half):
    _, rows, width = dst.shape
    n = pl.num_programs(0)
    first = pl.multiple_of(table_ref[pl.program_id(0)], LANES)
    start = pl.multiple_of(table_ref[n], rows)
    dst[0] = src[pl.ds(start, rows), half, pl.ds(first, width)]


def split_columns(weight, half, firsts, head, span, start, rows):
    total, _, lru = weight.shape
    n = len(firsts)
    table = jnp.stack([jnp.int32(f * head) for f in firsts] + [start])
    return pl.pallas_call(
        functools.partial(split_kernel, half=half),
        grid_spec=pltpu.PrefetchScalarGridSpec(
            num_scalar_prefetch=1,
            grid=(n,),
            in_specs=[pl.BlockSpec((total, 2, lru), lambda w, table: (0, 0, 0))],
            out_specs=pl.BlockSpec((1, rows, span * head), lambda w, table: (w, 0, 0)),
        ),
        out_shape=jax.ShapeDtypeStruct((n, rows, span * head), weight.dtype),
        name="split_columns",
    )(table, weight)


def far_kernel(
    normed_ref,
    cot_ref,
    gate_ref,
    up_ref,
    wout_ref,
    own_gate_ref,
    own_up_ref,
    own_out_ref,
    ggate_ref,
    gup_ref,
    gout_ref,
):
    @pl.when(pl.program_id(0) == 0)
    def _():
        ggate_ref[...] = own_gate_ref[...]
        gup_ref[...] = own_up_ref[...]
        gout_ref[...] = own_out_ref[...]

    normed = normed_ref[...]
    cot = cot_ref[...]
    value, slope = gelu_parts(dot(normed, gate_ref[...]))
    up = dot(normed, up_ref[...])
    grad = dot_back(cot, wout_ref[...])
    gout_ref[...] += dot_over((value * up).astype(BF16), cot)
    ggate_ref[...] += dot_over(normed, (grad * up * slope).astype(BF16))
    gup_ref[...] += dot_over(normed, (grad * value).astype(BF16))


def far_grads(normed, cot, weight_in, weight_out, sums, part, parts):
    total, width = normed.shape
    hidden = weight_out.shape[0] // parts
    rows = min(512, total)
    once = pl.Buffered(1)
    data = pl.BlockSpec((rows, width), lambda i: (i, 0))
    cols = lambda i: (0, part)
    lines = lambda i: (part, 0)
    held = pl.BlockSpec((width, hidden), cols, pipeline_mode=once)
    up = pl.BlockSpec((width, hidden), lambda i: (0, parts + part), pipeline_mode=once)
    held_out = pl.BlockSpec((hidden, width), lines, pipeline_mode=once)
    return pl.pallas_call(
        far_kernel,
        grid=(total // rows,),
        in_specs=[data, data, held, up, held_out, held, held, held_out],
        out_specs=[
            pl.BlockSpec((width, hidden), cols),
            pl.BlockSpec((width, hidden), cols),
            pl.BlockSpec((hidden, width), lines),
        ],
        out_shape=[jax.ShapeDtypeStruct(v.shape, F32) for v in sums],
        input_output_aliases={5: 0, 6: 1, 7: 2},
        cost_estimate=pl.CostEstimate(
            flops=1024, bytes_accessed=1024, transcendentals=0
        ),
        compiler_params=pltpu.CompilerParams(
            dimension_semantics=("arbitrary",), vmem_limit_bytes=60 << 20
        ),
        name="far_grads",
    )(normed, cot, weight_in, weight_in, weight_out, *sums)


def norm_kernel(src, gain, dst):
    rows = src[0].astype(F32)
    inv = lax.rsqrt(jnp.mean(rows * rows, axis=-1, keepdims=True) + 1e-06)
    dst[...] = (rows * inv * gain[...]).astype(BF16)


def norm_packed(packed, gain, size):
    n, _, width = packed.shape
    return pl.pallas_call(
        norm_kernel,
        grid=(n,),
        in_specs=[
            pl.BlockSpec((1, size, width), lambda w: (w, 0, 0)),
            pl.BlockSpec((1, width), lambda w: (0, 0)),
        ],
        out_specs=pl.BlockSpec((size, width), lambda w: (w, 0)),
        out_shape=jax.ShapeDtypeStruct((n * size, width), BF16),
        name="norm_packed",
    )(packed, gain)


def join_kernel(first, second, joined):
    joined[:, 0, :] = first[...].astype(F32)
    joined[:, 1, :] = second[...].astype(F32)


def join_halves(first, second):
    total, width = first.shape
    rows = math.gcd(total, 512)
    block = pl.BlockSpec((rows, width), lambda i: (i, 0))
    return pl.pallas_call(
        join_kernel,
        grid=(total // rows,),
        in_specs=[block, block],
        out_specs=pl.BlockSpec((rows, 2, width), lambda i: (i, 0, 0)),
        out_shape=jax.ShapeDtypeStruct((total, 2, width), F32),
        compiler_params=pltpu.CompilerParams(vmem_limit_bytes=60 << 20),
        name="join_halves",
    )(first, second)


def bit_list(n):
    return [1 << i for i in range(n.bit_length() - 1)]


def swap(block, axis, bit):
    return lax.ppermute(block, axis, [(i, i ^ bit) for i in range(lax.axis_size(axis))])


def gather_steps(block):
    n = lax.axis_size("wide")
    links = bit_list(n)[1:]
    half = block.shape[1] // 2
    sides = [block[:, :half], block[:, half:]]
    orders = [links, links[::-1]]
    for m, bits in enumerate(zip(*orders)):
        got = yield [swap(side, "wide", bit) for side, bit in zip(sides, bits)]
        sides = [jnp.stack([s, g], axis=m) for s, g in zip(sides, got)]
    for i, order in enumerate(orders):
        place = sorted(range(len(order)), key=lambda k: -order[k])
        sides[i] = sides[i].transpose(*place, len(order), len(order) + 1)
    return jnp.concatenate(sides, axis=-1).reshape(-1, block.shape[1])


def other_core(rows):
    return swap(rows, "wide", 1)


def scatter_steps(keep, send):
    n = lax.axis_size("wide")
    links = bit_list(n)[1:]
    rows, width = keep.shape[0] // (n // 2), keep.shape[1]
    half = width // 2
    got = yield [other_core(send)]
    held = keep + got[0].astype(F32)
    held = held.reshape((2,) * len(links) + (rows, width))
    sides = [held[..., :half], held[..., half:]]
    axes = [links[::-1], links[::-1]]
    for bits in zip(links, links[::-1]):
        kept, sent = [], []
        for i, bit in enumerate(bits):
            axis = axes[i].index(bit)
            kept.append(lax.index_in_dim(sides[i], 0, axis, keepdims=False))
            part = lax.index_in_dim(sides[i], 1, axis, keepdims=False)
            sent.append(swap(part.astype(BF16), "wide", bit))
            axes[i] = axes[i][:axis] + axes[i][axis + 1 :]
        got = yield sent
        sides = [k + g.astype(F32) for k, g in zip(kept, got)]
    return jnp.concatenate(sides, axis=-1)


def run_steps(steps, arrived=None):
    try:
        while True:
            arrived = steps.send(arrived)
    except StopIteration as end:
        return end.value


def tie(value, *before):
    return lax.optimization_barrier((value, *before))[0]


def line_step(part, stage):
    n = lax.axis_size("seq")
    if n < 2 or n % 2:
        return lax.psum(part, "seq") if stage == 1 else part
    here = lax.axis_index("seq")

    def step(pairs):
        got = lax.ppermute(part, "seq", pairs)
        return got, (part.astype(F32) + got.astype(F32)).astype(BF16)

    middle = n // 2
    if stage == 0:
        for k in range(middle - 1):
            part = step([(k, k + 1), (n - 1 - k, n - 2 - k)])[1]
    elif stage == 1:
        part = step([(middle - 1, middle), (middle, middle - 1)])[1]
    else:
        for k in range(middle - 2, -1, -1):
            got = step([(k + 1, k), (n - 2 - k, n - 1 - k)])[0]
            part = jnp.where((here == k) | (here == n - 1 - k), got, part)
    return part


def sum_small(values, axis):
    n = lax.axis_size(axis)
    if n & (n - 1):
        return lax.psum(values, axis)
    length = values.shape[0]
    padded = jnp.pad(values, (0, -length % (SUB * LANES))).reshape(-1, LANES)
    for bit in bit_list(n):
        padded = padded + swap(padded, axis, bit)
    return padded.reshape(-1)[:length]


def exchange(blocks):
    return lax.all_to_all(blocks, "wide", split_axis=0, concat_axis=0, tiled=True)


def near_place(r, n):
    return 2 * (r % (n // 2)) + r // (n // 2)


def move_kernel(table_ref, src, dst):
    dst[...] = src[...]


def move_rows(rows, near):
    n = lax.axis_size("wide")
    here = lax.axis_index("wide")
    size = rows.shape[0] // n
    table = jnp.stack([here ^ near_place(r, n) for r in range(n)]).astype(jnp.int32)
    device = lambda r, table: (table[r], 0)
    place = lambda r, table: (r, 0)
    block = (size, rows.shape[1])
    return pl.pallas_call(
        move_kernel,
        grid_spec=pltpu.PrefetchScalarGridSpec(
            num_scalar_prefetch=1,
            grid=(n,),
            in_specs=[pl.BlockSpec(block, device if near else place)],
            out_specs=pl.BlockSpec(block, place if near else device),
        ),
        out_shape=jax.ShapeDtypeStruct(rows.shape, rows.dtype),
        name="move_rows",
    )(table, rows)


def to_near(rows):
    return move_rows(rows, True)


def norm_rows(rows):
    inv = lax.rsqrt(jnp.mean(rows * rows, axis=-1, keepdims=True) + 1e-06)
    return inv, rows * inv


def norm_back(grad, gain, inv, unit):
    scaled = grad * gain
    return inv * (scaled - unit * jnp.mean(scaled * unit, axis=-1, keepdims=True))


def feed_forward_back(gate_up, cot, weight_out):
    hidden_width = weight_out.shape[0]
    gate, up = gate_up[:, :hidden_width], gate_up[:, hidden_width:]
    value, slope = gelu_parts(gate)
    hidden_grad = dot_back(cot, weight_out)
    hidden = (value * up).astype(BF16)
    gate_up_grad = jnp.concatenate(
        [
            (hidden_grad * up * slope).astype(BF16),
            (hidden_grad * value).astype(BF16),
        ],
        axis=1,
    )
    return hidden, gate_up_grad


def feed_forward(normed, cot, weight_in, weight_out):
    return feed_forward_back(dot(normed, weight_in), cot, weight_out)


def shards(
    tokens,
    cotangent,
    norm_gains,
    in_weight,
    conv_weight,
    conv_bias,
    gate_weights,
    gate_biases,
    decay_param,
    out_weight,
    mlp_in_weight,
    mlp_out_weight,
):
    n_wide, n_seq = lax.axis_size("wide"), lax.axis_size("seq")
    here = lax.axis_index("wide")
    tok_low, cot_low = tokens[0], cotangent[0]
    size, width = tok_low.shape
    own = out_weight.shape[0]
    lru = own * n_wide
    heads, head = gate_weights.shape[1:3]
    taps = conv_weight.shape[0]
    gain_own = norm_gains.shape[1]
    hidden_units = mlp_out_weight.shape[0]
    part = head // n_wide

    span = max(
        ((w + 1) * own - 1) // head - w * own // head + 1 for w in range(n_wide)
    )
    firsts = [min(w * own // head, heads - span) for w in range(n_wide)]
    win = span * head
    start = jnp.minimum(here * own // head, heads - span) * head
    offset = here * own - start

    total = size * n_wide
    half = total // 2
    recompute = n_seq * total <= 8192 and n_seq & (n_seq - 1) == 0 and n_seq > 1

    def far_rows(rows):
        return [swap(rows, "seq", d) for d in range(1, n_seq)] if recompute else []

    def far_gather(rows):
        return lax.all_gather(rows, "wide", axis=0, tiled=True)

    small = jnp.concatenate(
        [
            norm_gains.reshape(-1),
            conv_weight.reshape(-1),
            conv_bias,
            gate_biases.reshape(-1),
            decay_param,
        ]
    )
    n_small = small.shape[0]
    small = jnp.pad(small, (0, -n_small % (16 * width))).reshape(-1, width)
    gate_rows = heads * part * head // width
    packed = jnp.concatenate(
        [
            tok_low,
            small,
            gate_weights.transpose(0, 1, 3, 2).reshape(2 * gate_rows, width),
        ]
    )
    got = lax.all_gather(packed, "wide")
    gates_all = got[:, -2 * gate_rows :].reshape(n_wide, 2, gate_rows, width)
    gate_rows = gate_rows // heads
    small = got[:, size : -2 * heads * gate_rows].reshape(n_wide, -1)[:, :n_small]

    own_rows = in_weight.shape[0]
    shared = n_seq % 2 == 0 and own_rows % 32 == 0
    row_part = own_rows // 2 if shared else own_rows
    odd = lax.axis_index("seq") % 2

    def fetch(half):
        begin = (odd * row_part if shared else odd * 0).astype(jnp.int32)
        return split_columns(in_weight, half, firsts, head, span, begin, row_part)

    def share(rows):
        return swap(rows, "seq", 1) if shared else ()

    def whole(rows, other):
        if shared:
            even = jnp.where(odd == 0, rows, other)
            rows = jnp.stack([even, jnp.where(odd == 0, other, rows)], axis=1)
        return rows.reshape(width, win)

    send_branch, send_gate = lax.optimization_barrier((fetch(0), fetch(1)))
    branch_mine = exchange(send_branch)
    gate_mine = exchange(send_gate)
    branch_other, gate_other = share(branch_mine), share(gate_mine)
    in_branch = whole(branch_mine, branch_other)
    gains = (
        small[:, : 2 * gain_own]
        .reshape(n_wide, 2, gain_own)
        .transpose(1, 0, 2)
        .reshape(2, width)
        .astype(F32)
    )
    channels = (
        small[:, 2 * gain_own :]
        .reshape(n_wide, taps + 4, own)
        .transpose(1, 0, 2)
        .reshape(taps + 4, lru)
    )
    channels = lax.dynamic_slice_in_dim(channels, start, win, axis=1).astype(F32)
    chan = jnp.concatenate(
        [channels[: taps + 3], -8.0 * jax.nn.softplus(-channels[taps + 3 :])]
    )
    normed_all = norm_packed(got, gains[:1], size)
    out_own = lax.dynamic_update_slice_in_dim(
        jnp.zeros((win, width), BF16), out_weight, offset, 0
    )
    mlp_in = mlp_in_weight.reshape(width, -1)

    in_branch, normed_all, chan, gains, out_own, mlp_in, gate_mine = (
        lax.optimization_barrier(
            (in_branch, normed_all, chan, gains, out_own, mlp_in, gate_mine)
        )
    )


    below = max(w * own - f * head for w, f in enumerate(firsts))
    above = max(f * head + win - (w + 1) * own for w, f in enumerate(firsts))
    if max(below, above) <= own:
        around = [
            lax.ppermute(
                out_weight[own - below :],
                "wide",
                [(i, i + 1) for i in range(n_wide - 1)],
            ),
            out_weight,
            lax.ppermute(
                out_weight[:above], "wide", [(i + 1, i) for i in range(n_wide - 1)]
            ),
        ]
        first_row = below - offset
    else:
        around = [lax.all_gather(out_weight, "wide", axis=0, tiled=True)]
        first_row = start
    cot_sent = far_rows(cot_low)
    cot_all = lax.all_gather(tie(cot_low, in_branch), "wide", axis=0, tiled=True)
    gate_w = (
        lax.dynamic_slice_in_dim(
            gates_all, start // head * gate_rows, span * gate_rows, axis=2
        )
        .reshape(n_wide, 2, span, part, head)
        .transpose(1, 2, 0, 3, 4)
        .reshape(2, span, head, head)
    )
    chunk = min(total, 512)
    states, *saved, enter = recur_forward(
        dot(normed_all, in_branch), chan, gate_w, taps, chunk
    )
    gate_mine, gate_other, states, around = lax.optimization_barrier(
        (gate_mine, gate_other, states, around)
    )
    in_gate = whole(gate_mine, gate_other)
    mixed_near, gate_rows = mix_forward(
        dot(normed_all, in_gate), states, head, chunk, size
    )
    out_send = dot(mixed_near[half:], out_own).astype(BF16)
    out_send, mixed_near, cot_all = lax.optimization_barrier(
        (out_send, mixed_near, cot_all)
    )
    rows = tok_low.astype(F32)
    steps = scatter_steps(dot(mixed_near[:half], out_own), out_send)
    way, in_branch, in_gate, around = lax.optimization_barrier(
        (steps.send(None), in_branch, in_gate, around)
    )
    way = steps.send(way)
    in_own = jnp.concatenate(
        [
            lax.dynamic_slice_in_dim(weight, offset, own, axis=1)
            for weight in (in_branch, in_gate)
        ],
        axis=1,
    )
    out_win = lax.dynamic_slice_in_dim(jnp.concatenate(around), first_row, win)
    way, in_own, out_win = lax.optimization_barrier((way, in_own, out_win))
    middle = rows + run_steps(steps, way)
    inv_two, unit_two = norm_rows(middle)
    normed_two = (unit_two * gains[1]).astype(BF16)
    middle, normed_two, inv_two, unit_two, cot_all = lax.optimization_barrier(
        (middle, normed_two, inv_two, unit_two, cot_all)
    )

    steps = gather_steps(normed_two)
    way = steps.send(None)
    sent = far_rows(normed_two)
    cot_near = to_near(cot_all)
    way, cot_near, cot_sent = lax.optimization_barrier((way, cot_near, cot_sent))
    cot_sent = jnp.concatenate(cot_sent) if recompute else ()
    way, cot_sent = lax.optimization_barrier((steps.send(way), cot_sent))
    normed_even = run_steps(steps, way)
    normed_even, cot_sent = lax.optimization_barrier((normed_even, cot_sent))
    cot_far = far_gather(cot_sent) if recompute else ()
    normed_odd = other_core(normed_even)
    hidden_even, grad_even = feed_forward(
        normed_even, cot_near[:half], mlp_in, mlp_out_weight
    )
    hidden_odd, grad_odd = feed_forward(
        normed_odd, cot_near[half:], mlp_in, mlp_out_weight
    )
    up_send = dot_back(grad_odd, mlp_in).astype(BF16)
    up_send, hidden_even, hidden_odd, grad_even, grad_odd, normed_odd, first_sent = (
        lax.optimization_barrier(
            (
                up_send,
                hidden_even,
                hidden_odd,
                grad_even,
                grad_odd,
                normed_odd,
                sent[:1],
            )
        )
    )
    sent = first_sent + sent[1:]
    steps = scatter_steps(dot_back(grad_even, mlp_in), up_send)
    way, grad_even, grad_odd, hidden_even, hidden_odd = lax.optimization_barrier(
        (steps.send(None), grad_even, grad_odd, hidden_even, hidden_odd)
    )
    way = steps.send(way)
    gate_sum = dot_over(normed_even, grad_even[:, :hidden_units]) + dot_over(
        normed_odd, grad_odd[:, :hidden_units]
    )
    up_sum = dot_over(normed_even, grad_even[:, hidden_units:]) + dot_over(
        normed_odd, grad_odd[:, hidden_units:]
    )
    way, gate_sum, up_sum, hidden_even, hidden_odd = lax.optimization_barrier(
        (way, gate_sum, up_sum, hidden_even, hidden_odd)
    )
    out_sum = dot_over(hidden_even, cot_near[:half]) + dot_over(
        hidden_odd, cot_near[half:]
    )
    normed_two_grad = run_steps(steps, way)
    middle_grad = cot_low.astype(F32) + norm_back(
        normed_two_grad, gains[1], inv_two, unit_two
    )
    mix_low = middle_grad.astype(BF16)
    gain_two_grad = jnp.sum(normed_two_grad * unit_two, axis=0)
    (
        middle_grad,
        mix_low,
        gain_two_grad,
        out_sum,
        hidden_even,
        hidden_odd,
        sent,
    ) = lax.optimization_barrier(
        (
            middle_grad,
            mix_low,
            gain_two_grad,
            out_sum,
            hidden_even,
            hidden_odd,
            sent,
        )
    )

    steps = gather_steps(mix_low)
    way, sent = lax.optimization_barrier((steps.send(None), sent))
    way = steps.send(way)
    normed_far = far_gather(jnp.concatenate(sent)) if recompute else ()
    feed_send = dot(hidden_odd, mlp_out_weight).astype(BF16)
    feed_keep = dot(hidden_even, mlp_out_weight)
    way, feed_send, feed_keep = lax.optimization_barrier((way, feed_send, feed_keep))
    mix_even = run_steps(steps, way)
    mix_odd = other_core(mix_even)
    even_grad = dot_back(mix_even, out_win)
    mix_odd, even_grad, cot_far = lax.optimization_barrier(
        (mix_odd, even_grad, cot_far)
    )
    mix_near = jnp.concatenate([mix_even, mix_odd])
    mixed_grad = jnp.concatenate([even_grad, dot_back(mix_odd, out_win)])
    out_grad = lax.dynamic_slice_in_dim(
        dot_over(mixed_near, mix_near).astype(BF16), offset, own
    )
    gate_half, state_grad = gate_backward(
        mixed_grad, states, gate_rows, head, chunk, size
    )
    state_grad, out_grad = lax.optimization_barrier((state_grad, out_grad))
    out_grad = line_step(out_grad, 0)

    def in_part(grad):
        return dot_over(normed_all, grad).astype(BF16).reshape(n_wide, -1, own)

    def in_rows(part):
        return jnp.moveaxis(exchange(part), 0, 1).reshape(-1, lru)

    branch_half, gate_grad, sums = recur_backward(
        state_grad, (states, *saved, enter), chan, gate_w, taps, chunk
    )
    branch_half = lax.dynamic_slice_in_dim(branch_half, offset, own, axis=1)
    branch_part = in_part(branch_half)
    branch_half, branch_part, gate_half, gate_grad, sums = lax.optimization_barrier(
        (branch_half, branch_part, gate_half, gate_grad, sums)
    )
    branch_rows_grad = in_rows(branch_part)
    gate_half = lax.dynamic_slice_in_dim(gate_half, offset, own, axis=1)
    gate_part = in_part(gate_half)
    own_near = to_near(jnp.concatenate([branch_half, gate_half], axis=1))
    normed_send = dot_back(own_near[half:], in_own).astype(BF16)
    (
        branch_rows_grad,
        gate_part,
        own_near,
        normed_send,
        out_grad,
        normed_far,
        gate_grad,
        feed_keep,
    ) = lax.optimization_barrier(
        (
            branch_rows_grad,
            gate_part,
            own_near,
            normed_send,
            out_grad,
            normed_far,
            gate_grad,
            feed_keep,
        )
    )
    branch_rows_grad = lax.psum(branch_rows_grad, "seq")
    gate_rows_grad = in_rows(gate_part)
    out_grad = line_step(out_grad, 1)
    normed_steps = scatter_steps(dot_back(own_near[:half], in_own), normed_send)
    way = normed_steps.send(None)

    parts = hidden_units // 256 if hidden_units % 256 == 0 else 1
    held = (gate_sum, up_sum, out_sum)
    feed_steps = scatter_steps(feed_keep, feed_send)

    def far_part(held, done):
        for p in range(done, parts if done == 2 else min(done + 1, parts)):
            if recompute:
                held = far_grads(
                    normed_far, cot_far, mlp_in, mlp_out_weight, held, p, parts
                )
        return held

    held = far_part(held, 0)
    way, held, gate_rows_grad, out_grad, normed_far, gate_grad, feed_keep = (
        lax.optimization_barrier(
            (way, held, gate_rows_grad, out_grad, normed_far, gate_grad, feed_keep)
        )
    )
    gate_grad = exchange(
        gate_grad.astype(BF16)
        .reshape(2, span, n_wide, part, head)
        .transpose(2, 0, 1, 3, 4)
    )
    out_grad = line_step(out_grad, 2)
    way = normed_steps.send(way)
    feed_way = feed_steps.send(None)
    held = far_part(held, 1)
    way, feed_way, held, gate_grad, out_grad, normed_far = lax.optimization_barrier(
        (way, feed_way, held, gate_grad, out_grad, normed_far)
    )
    holders = [
        next(w for w, f in enumerate(firsts) if f <= j < f + span) for j in range(heads)
    ]
    gate_grad = jnp.stack(
        [gate_grad[w, :, j - firsts[w]] for j, w in enumerate(holders)], axis=1
    )
    out_grad = out_grad.astype(F32)
    way = normed_steps.send(way)
    feed_way = feed_steps.send(feed_way)
    branch_rows_grad, gate_rows_grad, gate_grad, out_grad, normed_far = (
        lax.optimization_barrier(
            (branch_rows_grad, gate_rows_grad, gate_grad, out_grad, normed_far)
        )
    )
    gate_rows_grad, gate_grad = lax.psum((gate_rows_grad, gate_grad), "seq")
    held = far_part(held, 2)
    way, feed_way, held = lax.optimization_barrier((way, feed_way, held))
    normed_grad = run_steps(normed_steps, way)
    inv_one, unit_one = norm_rows(rows)
    input_grad = middle_grad + norm_back(normed_grad, gains[0], inv_one, unit_one)
    gain_one_grad = jnp.sum(normed_grad * unit_one, axis=0)
    feed = run_steps(feed_steps, feed_way)
    result = (middle + feed).astype(BF16)
    if recompute:
        mlp_in_grad = join_halves(held[0], held[1])
    else:
        mlp_in_grad = jnp.stack(held[:2], axis=1)
    mlp_out_grad = held[2]
    in_grad = join_halves(branch_rows_grad, gate_rows_grad)
    sums = lax.dynamic_slice_in_dim(sums[: taps + 4], offset, own, axis=1)
    gate_grad = gate_grad.astype(F32).transpose(0, 1, 3, 2)

    gains_grad = sum_small(jnp.concatenate([gain_one_grad, gain_two_grad]), "wide")
    gains_grad = lax.dynamic_slice_in_dim(
        gains_grad.reshape(2, width), here * gain_own, gain_own, axis=1
    )
    small = sum_small(
        jnp.concatenate([gains_grad.reshape(-1), sums.reshape(-1)]), "seq"
    )
    gains_grad = small[: 2 * gain_own].reshape(2, gain_own)
    sums = small[2 * gain_own :].reshape(taps + 4, own)
    decay_grad = sums[taps + 3] * 8.0 * jax.nn.sigmoid(-decay_param.astype(F32))
    if not recompute:
        mlp_out_grad, mlp_in_grad = (
            lax.psum(g.astype(BF16), "seq").astype(F32)
            for g in (mlp_out_grad, mlp_in_grad)
        )
    return (
        result[None],
        input_grad[None],
        gains_grad,
        in_grad,
        sums[:taps],
        sums[taps],
        gate_grad,
        sums[taps + 1 : taps + 3],
        decay_grad,
        out_grad,
        mlp_in_grad,
        mlp_out_grad,
    )


def solution(mesh):
    placed = (
        P("seq", "wide", None),
        P("seq", "wide", None),
        P(None, "wide"),
        P("wide", None, None),
        P(None, "wide"),
        P("wide"),
        P(None, None, None, "wide"),
        P(None, "wide"),
        P("wide"),
        P("wide", None),
        P(None, None, "wide"),
        P("wide", None),
    )
    return jax.shard_map(
        shards,
        mesh=mesh,
        in_specs=placed,
        out_specs=(
            P("seq", "wide", None),
            P("seq", "wide", None),
            P(None, "wide"),
            P("wide", None, None),
            P(None, "wide"),
            P("wide"),
            P(None, None, None, "wide"),
            P(None, "wide"),
            P("wide"),
            P("wide", None),
            P(None, None, "wide"),
            P("wide", None),
        ),
        check_vma=False,
    )
```
